32 devices in a mesh: section: 4 (over x, core), wide: 8 (over z, y).
Axes of the slice: x: 2, y: 2, z: 4, core: 2. Of those that a mesh axis runs over, the one named last changes fastest.
Arguments:
- tokens: bfloat16 [48, 208, 768], P('wide', 'section'), may hold values from -6 to 6
- cotangent: bfloat16 [48, 208, 768], P('wide', 'section'), may hold values from -6 to 6
- shape_id: int32 [48], P('wide'), may hold values from 0 to 2
- rel_index: int32 [3, 43264], replicated, may hold values from 0 to 1271, as said below
- norm1_gain: bfloat16 [2, 768], replicated, may hold values from 0.25 to 1.75
- norm1_bias: bfloat16 [2, 768], replicated, may hold values from -1.75 to 1.75
- qkv_weight: bfloat16 [2, 768, 2304], P(None, 'section'), may hold values from -0.3125 to 0.3125
- q_bias: bfloat16 [2, 768], replicated, may hold values from -3 to 3
- v_bias: bfloat16 [2, 768], replicated, may hold values from -3 to 3
- proj_weight: bfloat16 [2, 768, 768], P(None, 'section'), may hold values from -0.875 to 0.875
- proj_bias: bfloat16 [2, 768], replicated, may hold values from -1.75 to 1.75
- attn_scale: bfloat16 [2, 768], replicated, may hold values from 0.29882812 to 1
- rel_table: bfloat16 [2, 1272, 12], replicated, may hold values from -6 to 6
- norm2_gain: bfloat16 [2, 768], replicated, may hold values from 0.25 to 1.75
- norm2_bias: bfloat16 [2, 768], replicated, may hold values from -1.75 to 1.75
- fc1_weight: bfloat16 [2, 768, 3072], P(None, 'section'), may hold values from -0.21875 to 0.21875
- fc1_bias: bfloat16 [2, 3072], replicated, may hold values from -3 to 3
- fc2_weight: bfloat16 [2, 3072, 768], P(None, 'section'), may hold values from -0.109375 to 0.109375
- fc2_bias: bfloat16 [2, 768], replicated, may hold values from -1.75 to 1.75
- mlp_scale: bfloat16 [2, 768], replicated, may hold values from 0.29882812 to 1
Outputs:
- outputs: bfloat16 [48, 208, 768], P('wide', 'section')
- d_tokens: float32 [48, 208, 768], P('wide', 'section')
- d_norm1_gain: float32 [2, 768], replicated
- d_norm1_bias: float32 [2, 768], replicated
- d_qkv_weight: float32 [2, 768, 2304], P(None, 'wide', 'section')
- d_q_bias: float32 [2, 768], replicated
- d_v_bias: float32 [2, 768], replicated
- d_proj_weight: float32 [2, 768, 768], P(None, 'wide', 'section')
- d_proj_bias: float32 [2, 768], replicated
- d_attn_scale: float32 [2, 768], replicated
- d_rel_table: float32 [2, 1272, 12], replicated
- d_norm2_gain: float32 [2, 768], replicated
- d_norm2_bias: float32 [2, 768], replicated
- d_fc1_weight: float32 [2, 768, 3072], P(None, 'wide', 'section')
- d_fc1_bias: float32 [2, 3072], replicated
- d_fc2_weight: float32 [2, 3072, 768], P(None, 'wide', 'section')
- d_fc2_bias: float32 [2, 768], replicated
- d_mlp_scale: float32 [2, 768], replicated
The draws below stay inside these ranges and needn't reach their ends.
Inputs may be any that keep to these rules, and one draw needn't show every extreme that they name: `rel_index`: for grid shape s, slot 0 is the class token and slots 1 .. GH*GW the patches row by row; pairs of patch slots with equal row and column offsets read the same row, distinct offsets distinct rows below 1269; rows 1269, 1270, 1271 serve class token to patch, patch to class token, class token to itself; pairs with a slot past the grid read row 0.
All inputs are finite; a program needn't handle non-finite values.
Results may differ from the reference program's by a relative error of at most 0.025.
The reference program's roundings to bfloat16 on the way count: a program that leaves them out, or rounds other values in their place, can miss the bound.
Values may be sent and summed in bfloat16 or wider, within the bound.
A program may use at most 256 MiB of HBM per device.

```python
import jax
import jax.numpy as jnp
from jax import lax

D = 768
HEADS = 12
HEAD_DIM = 64
FF = 3072
SLOTS = 208
GRID_A_H = 14
GRID_A_W = 14
GRID_B_H = 10
GRID_B_W = 20
GRID_C_H = 8
GRID_C_W = 24
SPAN_H = 14
SPAN_W = 24
NUM_REL = 1272
LAYERS = 2
IMAGES = 48


def draw_rel_index(key, part):
    key = jax.random.fold_in(key, 7)
    span_cols = 2 * SPAN_W - 1
    geo_count = (2 * SPAN_H - 1) * span_cols
    relabel = jax.random.permutation(key, jnp.arange(geo_count, dtype=jnp.int32))
    slot_ids = jnp.arange(SLOTS, dtype=jnp.int32)
    grids = ((GRID_A_H, GRID_A_W), (GRID_B_H, GRID_B_W), (GRID_C_H, GRID_C_W))
    tables = []
    for grid_rows, grid_cols in grids:
        patch = jnp.maximum(slot_ids - 1, 0)
        row_pos = patch // grid_cols
        col_pos = patch % grid_cols
        geometry = (row_pos[:, None] - row_pos[None, :] + SPAN_H - 1) * span_cols + (col_pos[:, None] - col_pos[None, :] + SPAN_W - 1)
        mapped = relabel[jnp.clip(geometry, 0, geo_count - 1)]
        query_cls = slot_ids[:, None] == 0
        key_cls = slot_ids[None, :] == 0
        entries = jnp.where(query_cls & key_cls, NUM_REL - 1, jnp.where(query_cls, NUM_REL - 3, jnp.where(key_cls, NUM_REL - 2, mapped)))
        inside = slot_ids < grid_rows * grid_cols + 1
        entries = jnp.where(inside[:, None] & inside[None, :], entries, 0)
        tables.append(entries.astype(jnp.int32).reshape(SLOTS * SLOTS))
    return jnp.stack(tables).astype(jnp.int32)


def plant(result, rng, least, top_value):
    dims = result.shape
    index_at = [jax.random.randint(jax.random.fold_in(rng, axis), (), 0, dims[axis]) for axis in range(len(dims))]
    result = result.at[tuple(index_at)].set(least)
    longest = dims.index(max(dims))
    index_at[longest] = (index_at[longest] + 1) % dims[longest]
    return result.at[tuple(index_at)].set(top_value)


def block_scale(stream_key, shape, cuts, smallest, largest):
    level, own = 1.0, jax.random.fold_in(stream_key, 6)
    for axis_at, blocks in cuts:
        draws = jnp.exp(jax.random.uniform(jax.random.fold_in(own, axis_at), (blocks,), jnp.float32, smallest / len(cuts), largest / len(cuts)))
        level = level * jnp.repeat(draws, shape[axis_at] // blocks).reshape([-1 if axis == axis_at else 1 for axis in range(len(shape))])
    return level


def centred(rng, extent, scale, most, split=(), held_as=jnp.bfloat16):
    gain = block_scale(rng, extent, split, -0.22, 0.18) if split else 1.0
    values = jax.random.normal(rng, extent, jnp.float32) * scale * gain
    return jnp.minimum(jnp.maximum(values, -most), most).astype(held_as)


def setup_inputs(seed: int = 0) -> dict:
    streams_of = jax.random.split(jax.random.key(seed), 21)
    tokens = centred(streams_of[0], (IMAGES, SLOTS, D), 1.0, 6.0, ((0, 8), (1, 4)))
    cotangent = centred(streams_of[1], (IMAGES, SLOTS, D), 1.0, 6.0, ((0, 8), (1, 4)))
    shape_id = plant(jax.random.randint(streams_of[2], (IMAGES,), 0, 3), jax.random.fold_in(streams_of[2], 1), 0, 2).astype(jnp.int32)
    rel_index = draw_rel_index(jax.random.fold_in(streams_of[20], 71), 0)
    norm1_gain = jnp.clip(1.0 + 0.15 * jax.random.normal(streams_of[4], (LAYERS, D), jnp.float32), 0.25, 1.75).astype(jnp.bfloat16)
    norm1_bias = centred(streams_of[5], (LAYERS, D), 0.3, 1.75)
    qkv_weight = centred(streams_of[6], (LAYERS, D, 3 * D), (D // 2) ** -0.5, 0.3125, ((1, 4),))
    q_bias = centred(streams_of[7], (LAYERS, D), 0.5, 3.0)
    v_bias = centred(streams_of[8], (LAYERS, D), 0.5, 3.0)
    proj_weight = centred(streams_of[9], (LAYERS, D, D), (D // 16) ** -0.5, 0.875, ((1, 4),))
    proj_bias = centred(streams_of[10], (LAYERS, D), 0.3, 1.75)
    attn_scale = jnp.clip(jax.random.uniform(streams_of[11], (LAYERS, D), jnp.float32, 0.29882812, 1.0), 0.29882812, 1.0).astype(jnp.bfloat16)
    rel_table = centred(streams_of[12], (LAYERS, NUM_REL, HEADS), 1.0, 6.0)
    norm2_gain = jnp.clip(1.0 + 0.15 * jax.random.normal(streams_of[13], (LAYERS, D), jnp.float32), 0.25, 1.75).astype(jnp.bfloat16)
    norm2_bias = centred(streams_of[14], (LAYERS, D), 0.3, 1.75)
    fc1_weight = centred(streams_of[15], (LAYERS, D, FF), D ** -0.5, 0.21875, ((1, 4),))
    fc1_bias = centred(streams_of[16], (LAYERS, FF), 0.5, 3.0)
    fc2_weight = centred(streams_of[17], (LAYERS, FF, D), FF ** -0.5, 0.109375, ((1, 4),))
    fc2_bias = centred(streams_of[18], (LAYERS, D), 0.3, 1.75)
    mlp_scale = jnp.clip(jax.random.uniform(streams_of[19], (LAYERS, D), jnp.float32, 0.29882812, 1.0), 0.29882812, 1.0).astype(jnp.bfloat16)
    return {"tokens": tokens, "cotangent": cotangent, "shape_id": shape_id, "rel_index": rel_index, "norm1_gain": norm1_gain, "norm1_bias": norm1_bias, "qkv_weight": qkv_weight, "q_bias": q_bias, "v_bias": v_bias, "proj_weight": proj_weight, "proj_bias": proj_bias, "attn_scale": attn_scale, "rel_table": rel_table, "norm2_gain": norm2_gain, "norm2_bias": norm2_bias, "fc1_weight": fc1_weight, "fc1_bias": fc1_bias, "fc2_weight": fc2_weight, "fc2_bias": fc2_bias, "mlp_scale": mlp_scale}


exact_mode = lax.Precision.HIGHEST
eps_norm = 1e-06
neg_large = -1e+30
root_half = 0.7071067811865476

@jax.custom_vjp
def low(v):
    return lax.optimization_barrier(v.astype(jnp.bfloat16)).astype(jnp.float32)

@jax.custom_vjp
def low_back(v):
    return v

def low_keep(v):
    return (low(v), None)

def low_pass(kept, grad):
    return (grad,)

def back_keep(v):
    return (v, None)

def back_low(kept, grad):
    return (low(grad),)
low.defvjp(low_keep, low_pass)
low_back.defvjp(back_keep, back_low)

def layer_norm(hidden, gain_vec, offset):
    average = lax.optimization_barrier(jnp.mean(hidden, axis=-1, keepdims=True))
    centered = hidden - average
    spread = lax.optimization_barrier(jnp.mean(centered * centered, axis=-1, keepdims=True))
    return centered * lax.rsqrt(spread + eps_norm) * gain_vec + offset

def gelu_exact(pre_act):
    return 0.5 * pre_act * (1.0 + lax.erf(pre_act * root_half))

def grid_counts(shape_ids):
    count_list = (GRID_A_H * GRID_A_W + 1, GRID_B_H * GRID_B_W + 1, GRID_C_H * GRID_C_W + 1)
    running = jnp.zeros(shape_ids.shape, jnp.int32)
    for number, amount in enumerate(count_list):
        running = running + jnp.where(shape_ids == number, amount, 0).astype(jnp.int32)
    return running

def attention_block(hidden, params, relbias, key_live):
    norm_gain, norm_offset, qkv_w, query_bias, value_bias, proj_w, proj_b, scale_vec = params
    image_count, slot_count, model_width = hidden.shape
    normed = low(layer_norm(hidden, norm_gain, norm_offset))
    bias_row = jnp.concatenate([query_bias, jnp.zeros_like(query_bias), value_bias])
    qkv = low_back(low(jnp.einsum('isd,de->ise', normed, qkv_w, precision=exact_mode) + bias_row))
    split_shape = (image_count, slot_count, HEADS, HEAD_DIM)
    queries = qkv[..., :model_width].reshape(split_shape)
    key_rows = qkv[..., model_width:2 * model_width].reshape(split_shape)
    value_rows = qkv[..., 2 * model_width:].reshape(split_shape)
    scores = jnp.einsum('iqhd,ikhd->ihqk', queries, key_rows, precision=exact_mode) * HEAD_DIM ** (-0.5) + relbias
    scores = low_back(scores)
    scores = jnp.where(key_live[:, None, None, :], scores, neg_large)
    row_top = lax.optimization_barrier(jnp.max(scores, axis=-1, keepdims=True))
    exp_rows = jnp.exp(scores - row_top)
    soft = low(exp_rows / lax.optimization_barrier(jnp.sum(exp_rows, axis=-1, keepdims=True)))
    mixture = jnp.einsum('ihqk,ikhd->iqhd', soft, value_rows, precision=exact_mode)
    mixture = low_back(low(mixture.reshape(image_count, slot_count, model_width)))
    branch = low_back(jnp.einsum('isd,de->ise', mixture, proj_w, precision=exact_mode) + proj_b)
    return hidden + scale_vec * branch

def mlp_block(hidden, params):
    norm_gain, norm_offset, fc1_w, fc1_b, fc2_w, fc2_b, scale_vec = params
    normed = low(layer_norm(hidden, norm_gain, norm_offset))
    pre_act = low_back(jnp.einsum('isd,df->isf', normed, fc1_w, precision=exact_mode) + fc1_b)
    activated = low(gelu_exact(pre_act))
    branch = low_back(jnp.einsum('isf,fd->isd', activated, fc2_w, precision=exact_mode) + fc2_b)
    return hidden + scale_vec * branch

def forward(block_tokens, params, shape_ids, rel_index):
    slot_ids = jnp.arange(SLOTS, dtype=jnp.int32)
    key_live = slot_ids[None, :] < grid_counts(shape_ids)[:, None]
    index_cube = rel_index.reshape(rel_index.shape[0], SLOTS, SLOTS)
    picked = index_cube[shape_ids.astype(jnp.int32)]
    hidden = block_tokens
    for layer_id in range(LAYERS):
        att_params = tuple((item[layer_id] for item in params[:8]))
        table = params[8][layer_id]
        relbias = jnp.transpose(table[picked], (0, 3, 1, 2))
        hidden = low_back(low(attention_block(hidden, att_params, relbias, key_live)))
        mlp_params = tuple((item[layer_id] for item in params[9:]))
        hidden = low_back(low(mlp_block(hidden, mlp_params)))
    return hidden

def reference(tokens, cotangent, shape_id, rel_index, norm1_gain, norm1_bias, qkv_weight, q_bias, v_bias, proj_weight, proj_bias, attn_scale, rel_table, norm2_gain, norm2_bias, fc1_weight, fc1_bias, fc2_weight, fc2_bias, mlp_scale):
    params = tuple((item.astype(jnp.float32) for item in (norm1_gain, norm1_bias, qkv_weight, q_bias, v_bias, proj_weight, proj_bias, attn_scale, rel_table, norm2_gain, norm2_bias, fc1_weight, fc1_bias, fc2_weight, fc2_bias, mlp_scale)))
    slot_ids = jnp.arange(SLOTS, dtype=jnp.int32)
    live = slot_ids[None, :] < grid_counts(shape_id)[:, None]
    masked = jnp.where(live[..., None], cotangent.astype(jnp.float32), 0.0)
    block_count = IMAGES // 16
    model_width = tokens.shape[2]

    def one_block(grad_sums, pieces):
        block_tokens, block_cot, block_shapes = pieces
        block_out, pullback = jax.vjp(lambda xval, pval: forward(xval, pval, block_shapes, rel_index), block_tokens, params)
        block_dx, block_grads = pullback(block_cot)
        return (tuple((left + right for left, right in zip(grad_sums, block_grads))), (block_out, block_dx))
    zero_grads = tuple((jnp.zeros_like(item) for item in params))
    grad_sums, (outs_all, dx_all) = lax.scan(one_block, zero_grads, (tokens.astype(jnp.float32).reshape(block_count, 16, SLOTS, model_width), masked.reshape(block_count, 16, SLOTS, model_width), shape_id.reshape(block_count, 16)))
    outputs = outs_all.reshape(IMAGES, SLOTS, model_width).astype(jnp.bfloat16)
    d_tokens = dx_all.reshape(IMAGES, SLOTS, model_width)
    return (outputs, d_tokens, grad_sums[0], grad_sums[1], grad_sums[2], grad_sums[3], grad_sums[4], grad_sums[5], grad_sums[6], grad_sums[7], grad_sums[8], grad_sums[9], grad_sums[10], grad_sums[11], grad_sums[12], grad_sums[13], grad_sums[14], grad_sums[15])
```

```python
import functools

import numpy as np
import jax
import jax.numpy as jnp
from jax import lax
from jax.experimental import pallas as pl
from jax.experimental.pallas import tpu as pltpu
from jax.sharding import PartitionSpec as P

GRIDS = ((14, 14), (10, 20), (8, 24))
EPS = 1e-06
DEAD = -1e30
ROOT_HALF = 0.7071067811865476
INV_ROOT_2PI = 0.3989422804014327
HEAD = 64
BF = jnp.bfloat16
F32 = jnp.float32


def swap(value, axis, bit):
    count = lax.axis_size(axis)
    return lax.ppermute(value, axis, [(i, i ^ bit) for i in range(count)])


def pick(flag, zero, one):
    return jnp.where(flag == 0, zero, one)


def dot(a, b, ca=1, cb=0, **kw):
    return lax.dot_general(a, b, (((ca,), (cb,)), ((), ())), preferred_element_type=F32, **kw)


LANES = 768

def up8(n): return -(-n//8)*8

def offset_sources(rows, cols, slots):
    pitch, span = 2 * cols - 1, 2 * rows - 1
    source = np.full((1, LANES), -1, np.int32)
    for j in range(span):
        r, rk = (0, j - (rows - 1)) if j >= rows - 1 else (rows - 1, j)
        for t in range(pitch):
            c, ck = (0, t - (cols - 1)) if t >= cols - 1 else (cols - 1, t)
            which = 1 + (1 if r else 0) * 2 + (1 if c else 0)
            source[0, j * pitch + t] = which * slots + 1 + rk * cols + ck
    length = pitch * span
    source[0, length : length + 4] = (0, 1, slots, slots - 1)
    return source

def key_targets(rows, cols, slots):
    pitch, length = 2 * cols - 1, (2 * cols - 1) * (2 * rows - 1)
    out = np.zeros((3, slots), np.int32)
    for k in range(slots):
        if k == 0:
            out[:, k] = length + 2, 0, length
        elif k <= rows * cols:
            rk, ck = divmod(k - 1, cols)
            out[:, k] = (rows - 1 + rk) * pitch + ck, pitch, length + 1
        else:
            out[:, k] = length + 3, 0, length + 3
    return out

def lane_onehot(target, dtype):
    n = target.shape[1]
    number = lax.broadcasted_iota(jnp.int32, (LANES, n), 0)
    return jnp.where(number == target, 1.0, 0.0).astype(dtype)

def block_order(core):
    return (0, 2, 1, 3) if core == 0 else (1, 3, 0, 2)

def bias_kernel(part, core_ref, table_ref, tgt_ref, *refs):
    idx_refs, src_refs = refs[:3], refs[3:6]
    out_ref, wide_ref, nat_ref = refs[6:]
    heads = out_ref.shape[1]
    slots = out_ref.shape[2]
    entries = table_ref.shape[1]
    for s, (rows, cols) in enumerate(GRIDS):
        length = (2 * cols - 1) * (2 * rows - 1)
        step = up8(cols)
        count = rows * cols + 1
        pairs = idx_refs[s].shape[0]
        hot = jnp.where(lax.broadcasted_iota(jnp.int32, (pairs, entries), 1) == idx_refs[s][...], 1.0, 0.0).astype(BF)
        looked = dot(table_ref[...], hot, 1, 1).astype(BF)
        place = lax.broadcasted_iota(jnp.int32, (pairs, LANES), 0)
        hot = jnp.where(place == src_refs[s][...], 1.0, 0.0).astype(BF)
        offsets = dot(looked, hot)
        turned = pltpu.roll(offsets, LANES - (cols - 1), 1)
        tail = lax.broadcasted_iota(jnp.int32, (step, LANES), 1) >= length
        for h in range(heads):
            row = jnp.broadcast_to(offsets[h : h + 1], (step, LANES))
            rolled = jnp.broadcast_to(turned[h : h + 1], (step, LANES))
            rolled = pltpu.roll(rolled, 0, 1, stride=1, stride_axis=0)
            wide_ref[h * step : (h + 1) * step, :] = jnp.where(tail, row, rolled)
        shifted = wide_ref[0 : heads * step, :].astype(BF)
        for r in range(rows):
            target = tgt_ref[s, 0:1, :] - r * tgt_ref[s, 1:2, :]
            patch = dot(shifted, lane_onehot(target, BF))
            for h in range(heads):
                nat_ref[h, 1 + r * cols : 1 + (r + 1) * cols, :] = patch[h * step : h * step + cols]
        first = dot(offsets.astype(BF), lane_onehot(tgt_ref[s, 2:3, :], BF))
        live = jnp.broadcast_to(tgt_ref[s, 2:3, :] < length + 2, (part, slots))
        for h in range(heads):
            nat_ref[h, 0:1, :] = first[h : h + 1]
            nat_ref[h, count:, :] = jnp.broadcast_to(
                offsets[h : h + 1, length + 3 : length + 4], (slots - count, slots)
            )
        for core in range(2):
            @pl.when(core_ref[0] == core)
            def _(core=core):
                for h in range(heads):
                    for j, b in enumerate(block_order(core)):
                        block = nat_ref[h, b * part : (b + 1) * part, :]
                        out_ref[s, h, j * part : (j + 1) * part, :] = jnp.where(live, block, DEAD)

def table_kernel(part, core_ref, db_ref, tgt_ref, *refs):
    idx_refs, src_refs = refs[:3], refs[3:6]
    out_ref, nat_ref, acc_ref, row_ref = refs[6:]
    heads = db_ref.shape[1]
    slots = db_ref.shape[2]
    entries = out_ref.shape[1]
    total = jnp.zeros(out_ref.shape, F32)
    for s, (rows, cols) in enumerate(GRIDS):
        length = (2 * cols - 1) * (2 * rows - 1)
        step = up8(cols)
        count = rows * cols + 1
        pairs = idx_refs[s].shape[0]
        for core in range(2):
            @pl.when(core_ref[0] == core)
            def _(core=core):
                for h in range(heads):
                    for j, b in enumerate(block_order(core)):
                        nat_ref[h, b * part : (b + 1) * part, :] = db_ref[s, h, j * part : (j + 1) * part, :]
        acc_ref[...] = jnp.zeros_like(acc_ref)
        row_ref[...] = jnp.zeros_like(row_ref)
        for r in range(rows):
            for h in range(heads):
                row_ref[h * step : h * step + cols, :] = nat_ref[h, 1 + r * cols : 1 + (r + 1) * cols, :]
            target = tgt_ref[s, 0:1, :] - r * tgt_ref[s, 1:2, :]
            acc_ref[0 : heads * step, :] += dot(row_ref[0 : heads * step, :].astype(BF), lane_onehot(target, BF), 1, 1)
        lane = lax.broadcasted_iota(jnp.int32, (8, LANES), 1)
        offsets = jnp.zeros((8, LANES), F32)
        for c in range(cols):
            part_c = jnp.concatenate([acc_ref[h * step + c : h * step + c + 1, :] for h in range(heads)]
                + [jnp.zeros((8 - heads, LANES), F32)], axis=0)
            back = pltpu.roll(part_c, cols - 1 - c, 1)
            offsets += jnp.where(lane >= length, part_c, back)
        first = jnp.concatenate([nat_ref[h, 0:1, :] for h in range(heads)] + [jnp.zeros((8 - heads, slots), F32)], axis=0)
        offsets += dot(first, lane_onehot(tgt_ref[s, 2:3, :], F32), 1, 1, precision=lax.Precision.HIGHEST)
        rest = jnp.concatenate([jnp.sum(jnp.sum(nat_ref[h, count:, :], axis=0, keepdims=True), axis=1, keepdims=True) for h in range(heads)]
            + [jnp.zeros((8 - heads, 1), F32)], axis=0)
        offsets += jnp.where(lane == length + 3, rest, 0.0)
        place = lax.broadcasted_iota(jnp.int32, (pairs, LANES), 0)
        hot = jnp.where(place == src_refs[s][...], 1.0, 0.0)
        looked = dot(offsets, hot, 1, 1, precision=lax.Precision.HIGHEST)
        hot = jnp.where(lax.broadcasted_iota(jnp.int32, (pairs, entries), 1) == idx_refs[s][...], 1.0, 0.0)
        total += dot(looked, hot, precision=lax.Precision.HIGHEST)
    out_ref[...] = total

VM = pl.BlockSpec(memory_space=pltpu.VMEM)
SM = pl.BlockSpec(memory_space=pltpu.SMEM)

def build_bias(core, table_rows, targets, indices, sources, heads, part):
    slots=4*part
    wide = heads*24
    return pl.pallas_call(functools.partial(bias_kernel, part),
        out_shape=jax.ShapeDtypeStruct((3,heads,slots,slots),F32),
        in_specs=[SM]+[VM]*8, out_specs=VM,
        scratch_shapes=[pltpu.VMEM((wide,LANES),F32), pltpu.VMEM((heads,slots,slots),F32)],
        compiler_params=pltpu.CompilerParams(vmem_limit_bytes=56*2**20),
    )(core, table_rows, targets, *indices, *sources)

def table_grad(core, d_bias, targets, indices, sources, entries, part):
    heads, slots = d_bias.shape[1:3]
    return pl.pallas_call(functools.partial(table_kernel, part),
        out_shape=jax.ShapeDtypeStruct((8,entries),F32),
        in_specs=[SM]+[VM]*8, out_specs=VM,
        scratch_shapes=[pltpu.VMEM((heads,slots,slots),F32), pltpu.VMEM((heads*24,LANES),F32), pltpu.VMEM((heads*24,slots),F32)],
        compiler_params=pltpu.CompilerParams(vmem_limit_bytes=56*2**20),
    )(core, d_bias, targets, *indices, *sources)

def bias_inputs(rel_index, ci, slots, part):
    place = jnp.arange(slots, dtype=jnp.int32)
    core_of = (place // (2 * part)) ^ ci
    within = place % (2 * part)
    slot_of = (within // part) * (2 * part) + core_of * part + within % part
    indices, sources = [], []
    for s,(gr,gc) in enumerate(GRIDS):
        queries = (0, 1, gc, 1 + (gr - 1) * gc, gr * gc)
        indices.append(jnp.concatenate([rel_index[s, a * slots : (a + 1) * slots] for a in queries])[:, None])
        sources.append(jnp.asarray(offset_sources(gr, gc, slots)))
    nat = jnp.asarray(np.stack([key_targets(gr, gc, slots) for gr, gc in GRIDS]))
    blocks = nat.reshape(3, 3, 2, 2, part)
    def order(c):
        return jnp.concatenate([blocks[:, :, :, c].reshape(3,3,2*part), blocks[:, :, :, 1-c].reshape(3,3,2*part)], axis=2)
    targets = jnp.where(ci == 0, order(0), order(1))
    return targets, indices, sources, slot_of


def attn_fwd_kernel(shape_ref, qkv_ref, bias_ref, o_ref):
    width = o_ref.shape[2]
    slots = o_ref.shape[1]
    lane = lax.broadcasted_iota(jnp.int32, (slots, 128), 1)
    for pair in range(width // 128):
        at = pair * 128
        q = qkv_ref[0, :, at : at + 128]
        k = qkv_ref[0, :, width + at : width + at + 128]
        v = qkv_ref[0, :, 2 * width + at : 2 * width + at + 128]
        outs = []
        for e in range(2):
            own = (lane // HEAD) == e
            qm = jnp.where(own, q, jnp.zeros_like(q))
            s = dot(qm, k, 1, 1) * HEAD**-0.5 + bias_ref[0, 2 * pair + e]
            ex = jnp.exp(s - jnp.max(s, axis=1, keepdims=True))
            p = ex / jnp.sum(ex, axis=1, keepdims=True)
            outs.append(dot(p.astype(BF), v))
        o_ref[0, :, at : at + 128] = jnp.where(lane < HEAD, outs[0], outs[1]).astype(BF)


def attn_bwd_kernel(shape_ref, qkv_ref, do_ref, bias_ref, dqkv_ref, db_ref):
    step = pl.program_id(0)
    width = do_ref.shape[2]
    slots = do_ref.shape[1]
    shape = shape_ref[step]

    @pl.when(step == 0)
    def _():
        db_ref[...] = jnp.zeros_like(db_ref)

    lane = lax.broadcasted_iota(jnp.int32, (slots, 128), 1)
    factor = HEAD**-0.5
    for pair in range(width // 128):
        at = pair * 128
        q = qkv_ref[0, :, at : at + 128]
        k = qkv_ref[0, :, width + at : width + at + 128]
        v = qkv_ref[0, :, 2 * width + at : 2 * width + at + 128]
        g = do_ref[0, :, at : at + 128]
        dqs, dks, dvs = [], [], []
        for e in range(2):
            own = (lane // HEAD) == e
            qm = jnp.where(own, q, jnp.zeros_like(q))
            gm = jnp.where(own, g, jnp.zeros_like(g))
            s = dot(qm, k, 1, 1) * factor + bias_ref[0, 2 * pair + e]
            ex = jnp.exp(s - jnp.max(s, axis=1, keepdims=True))
            p = ex / jnp.sum(ex, axis=1, keepdims=True)
            dp = dot(gm, v, 1, 1)
            ds = (p * (dp - jnp.sum(p * dp, axis=1, keepdims=True))).astype(BF)
            db_ref[shape, 2 * pair + e] += ds.astype(F32)
            dvs.append(dot(p.astype(BF), g, 0, 0))
            dqs.append(dot(ds, k))
            dks.append(dot(ds, q, 0, 0))
        low = lane < HEAD
        dqkv_ref[0, :, at : at + 128] = (jnp.where(low, dqs[0], dqs[1]) * factor).astype(BF)
        dqkv_ref[0, :, width + at : width + at + 128] = (
            jnp.where(low, dks[0], dks[1]) * factor
        ).astype(BF)
        dqkv_ref[0, :, 2 * width + at : 2 * width + at + 128] = jnp.where(
            low, dvs[0], dvs[1]
        ).astype(BF)


def attn_fwd(shape_ids, qkv, bias):
    images, slots, wide = qkv.shape
    width = wide // 3
    heads = width // HEAD
    pairs = images * heads
    return pl.pallas_call(
        attn_fwd_kernel,
        grid_spec=pltpu.PrefetchScalarGridSpec(
            num_scalar_prefetch=1,
            grid=(images,),
            in_specs=[
                pl.BlockSpec((1, slots, wide), lambda i, s: (i, 0, 0)),
                pl.BlockSpec((1, heads, slots, slots), lambda i, s: (s[i], 0, 0, 0)),
            ],
            out_specs=pl.BlockSpec((1, slots, width), lambda i, s: (i, 0, 0)),
        ),
        out_shape=jax.ShapeDtypeStruct((images, slots, width), BF),
        compiler_params=pltpu.CompilerParams(vmem_limit_bytes=48 * 2**20),
        cost_estimate=pl.CostEstimate(
            flops=pairs * slots * slots * 128 * 4, bytes_accessed=pairs * slots * slots * 4,
            transcendentals=pairs * slots * slots,
        ),
    )(shape_ids, qkv, bias)


def attn_bwd(shape_ids, qkv, d_out, bias):
    images, slots, wide = qkv.shape
    width = wide // 3
    heads = width // HEAD
    pairs = images * heads
    shapes = bias.shape[0]
    return pl.pallas_call(
        attn_bwd_kernel,
        grid_spec=pltpu.PrefetchScalarGridSpec(
            num_scalar_prefetch=1,
            grid=(images,),
            in_specs=[
                pl.BlockSpec((1, slots, wide), lambda i, s: (i, 0, 0)),
                pl.BlockSpec((1, slots, width), lambda i, s: (i, 0, 0)),
                pl.BlockSpec((1, heads, slots, slots), lambda i, s: (s[i], 0, 0, 0)),
            ],
            out_specs=[
                pl.BlockSpec((1, slots, wide), lambda i, s: (i, 0, 0)),
                pl.BlockSpec((shapes, heads, slots, slots), lambda i, s: (0, 0, 0, 0)),
            ],
        ),
        out_shape=[
            jax.ShapeDtypeStruct((images, slots, wide), BF),
            jax.ShapeDtypeStruct((shapes, heads, slots, slots), F32),
        ],
        compiler_params=pltpu.CompilerParams(vmem_limit_bytes=48 * 2**20),
        cost_estimate=pl.CostEstimate(
            flops=pairs * slots * slots * 128 * 10, bytes_accessed=pairs * slots * slots * 8,
            transcendentals=pairs * slots * slots,
        ),
    )(shape_ids, qkv, d_out, bias)


def norm_parts(hidden):
    hidden = hidden.astype(F32)
    centered = hidden - jnp.mean(hidden, axis=1, keepdims=True)
    inv = lax.rsqrt(jnp.mean(centered * centered, axis=1, keepdims=True) + EPS)
    return centered * inv, inv


def norm_back(hidden, d_normed, gain):
    xhat, inv = norm_parts(hidden)
    d_gain = jnp.sum(d_normed * xhat, axis=0)
    d_offset = jnp.sum(d_normed, axis=0)
    dx = d_normed * gain
    mean_dx = jnp.mean(dx, axis=1, keepdims=True)
    mean_dxx = jnp.mean(dx * xhat, axis=1, keepdims=True)
    return inv * (dx - mean_dx - xhat * mean_dxx), d_gain, d_offset


def shards(
    tokens,
    cotangent,
    shape_id,
    rel_index,
    norm1_gain,
    norm1_bias,
    qkv_weight,
    q_bias,
    v_bias,
    proj_weight,
    proj_bias,
    attn_scale,
    rel_table,
    norm2_gain,
    norm2_bias,
    fc1_weight,
    fc1_bias,
    fc2_weight,
    fc2_bias,
    mlp_scale,
):
    section = lax.axis_index("section")
    wide = lax.axis_index("wide")
    xi, ci, yi = section // 2, section % 2, wide % 2
    wide_count = lax.axis_size("wide")
    layers = qkv_weight.shape[0]
    images, part, width = tokens.shape
    slots = part * 4
    mine = images // 2
    rows = mine * 2 * part
    half = width // 2
    ff = fc1_weight.shape[2]

    def to_images(value):
        cut = value.reshape(2, mine, part, width)
        keep = lax.dynamic_index_in_dim(cut, xi, 0, keepdims=False)
        got = swap(lax.dynamic_index_in_dim(cut, 1 - xi, 0, keepdims=False), "section", 2)
        both = jnp.concatenate([pick(xi, keep, got), pick(xi, got, keep)], axis=1)
        return both.reshape(rows, width)

    def to_slots(value):
        cut = value.reshape(mine, 2, part, width)
        keep = lax.dynamic_index_in_dim(cut, xi, 1, keepdims=False)
        got = swap(lax.dynamic_index_in_dim(cut, 1 - xi, 1, keepdims=False), "section", 2)
        return jnp.concatenate([pick(xi, keep, got), pick(xi, got, keep)], axis=0)

    def gather_rows(own):
        depth = own.shape[0]
        cut = depth // 2
        beside = swap(own, "section", 1)
        first = swap(lax.dynamic_slice_in_dim(own, yi * cut, cut, 0), "section", 2)
        second = swap(first, "wide", 1)
        far = jnp.concatenate([pick(yi, first, second), pick(yi, second, first)], axis=0)
        far_beside = swap(far, "section", 1)
        whole = jnp.zeros((4 * depth, own.shape[1]), own.dtype)
        for r, piece in enumerate((own, beside, far, far_beside)):
            whole = lax.dynamic_update_slice_in_dim(whole, piece, (section ^ r) * depth, 0)
        return whole

    hidden = to_images(tokens)
    weights = []
    for l in range(layers):
        weights.append(
            [gather_rows(w[l]) for w in (qkv_weight, proj_weight, fc1_weight, fc2_weight)]
        )
    whole_cot = to_images(cotangent)
    shapes = lax.dynamic_slice_in_dim(shape_id, xi * mine, mine, 0)

    targets, indices, sources, slot_of = bias_inputs(rel_index, ci, slots, part)
    counts = [r * c + 1 for r, c in GRIDS]
    heads = rel_table.shape[2]
    entries = rel_table.shape[1]
    mine_heads = heads // 2
    core_arg = jnp.reshape(ci, (1,)).astype(jnp.int32)
    table = pick(ci, rel_table[:, :, :mine_heads], rel_table[:, :, mine_heads:])
    table_rows = jnp.transpose(table, (0, 2, 1)).reshape(layers * mine_heads, entries)
    table_rows = jnp.pad(table_rows, ((0, 16 - layers * mine_heads), (0, 0)))
    bias_all = build_bias(
        core_arg, table_rows, targets, indices, sources, layers * mine_heads, part
    )
    bias = [bias_all[:, l * mine_heads : (l + 1) * mine_heads] for l in range(layers)]

    def f32_row(vector, l):
        return vector[l].astype(F32)[None, :]

    def to_heads(value):
        blocks = value.shape[1] // width
        lows = [value[:, b * width : b * width + half] for b in range(blocks)]
        tops = [value[:, b * width + half : (b + 1) * width] for b in range(blocks)]
        keep = jnp.concatenate([pick(ci, a, b) for a, b in zip(lows, tops)], axis=1)
        send = jnp.concatenate([pick(ci, b, a) for a, b in zip(lows, tops)], axis=1)
        got = swap(send, "section", 1)
        shape = (mine, 2 * part, blocks * half)
        return jnp.concatenate([keep.reshape(shape), got.reshape(shape)], axis=1)

    def from_heads(value):
        blocks = value.shape[2] // half
        keep = value[:, : 2 * part].reshape(rows, blocks * half)
        got = swap(value[:, 2 * part :], "section", 1).reshape(rows, blocks * half)
        pieces = []
        for b in range(blocks):
            a, o = keep[:, b * half : (b + 1) * half], got[:, b * half : (b + 1) * half]
            pieces += [pick(ci, a, o), pick(ci, o, a)]
        return jnp.concatenate(pieces, axis=1)

    saved = []
    for l in range(layers):
        qkv_w, proj_w, fc1_w, fc2_w = weights[l]
        kept = {"h": hidden}
        xhat, unused = norm_parts(hidden)
        normed = (xhat * f32_row(norm1_gain, l) + f32_row(norm1_bias, l)).astype(BF)
        qb = f32_row(q_bias, l)
        qkv_b = jnp.concatenate([qb, jnp.zeros_like(qb), f32_row(v_bias, l)], axis=1)
        qkv = (dot(normed, qkv_w) + qkv_b).astype(BF)
        by_head = to_heads(qkv)
        mixed = from_heads(attn_fwd(shapes, by_head, bias[l]))
        branch = dot(mixed, proj_w) + f32_row(proj_bias, l)
        kept.update(n=normed, qkv=by_head, o=mixed, r=branch)
        hidden = (hidden.astype(F32) + f32_row(attn_scale, l) * branch).astype(BF)
        kept["h1"] = hidden
        xhat, unused = norm_parts(hidden)
        normed = (xhat * f32_row(norm2_gain, l) + f32_row(norm2_bias, l)).astype(BF)
        pre = dot(normed, fc1_w) + f32_row(fc1_bias, l)
        cdf = 0.5 * (1.0 + lax.erf(pre * ROOT_HALF))
        act = (pre * cdf).astype(BF)
        slope = cdf + pre * jnp.exp(-0.5 * pre * pre) * INV_ROOT_2PI
        branch = dot(act, fc2_w) + f32_row(fc2_bias, l)
        kept.update(n2=normed, u=act, slope=slope, m=branch)
        hidden = (hidden.astype(F32) + f32_row(mlp_scale, l) * branch).astype(BF)
        saved.append(kept)
    out = to_slots(hidden)

    def columns(value, x, c):
        block = value.shape[1] // 4
        at = (2 * x + c) * block
        return value[:, at : at + block]

    def add(a, b):
        return (a.astype(F32) + b.astype(F32)).astype(BF)

    def core_sum(left, right):
        own = jnp.concatenate(
            [pick(ci, columns(right, x, 0), columns(right, x, 1)) for x in range(2)], axis=1
        )
        other = jnp.concatenate(
            [pick(ci, columns(right, x, 1), columns(right, x, 0)) for x in range(2)], axis=1
        )
        got = swap(dot(left, other, 0, 0).astype(BF), "section", 1)
        return (dot(left, own, 0, 0) + got.astype(F32)).astype(BF)

    def x_step(value):
        block = value.shape[1] // 2
        low, top = value[:, :block], value[:, block:]
        return add(pick(xi, low, top), swap(pick(xi, top, low), "section", 2))

    def wide_steps(value):
        group = value.shape[0] // wide_count
        bit = 1
        value = value[None]
        while bit < wide_count:
            total = value.shape[0] * value.shape[1]
            left = wide_count // bit
            cut = value.reshape(left // 2, 2, total // left, value.shape[2])
            flag = (wide // bit) % 2
            keep = lax.dynamic_index_in_dim(cut, flag, 1, keepdims=False)
            send = lax.dynamic_index_in_dim(cut, 1 - flag, 1, keepdims=False)
            value = add(keep, swap(send, "wide", bit))
            bit *= 2
        return value.reshape(group, value.shape[2])

    def x_first(value):
        return wide_steps(x_step(value)).astype(F32)

    def wide_first(value):
        return x_step(wide_steps(value)).astype(F32)

    def all_sum(value):
        for bit in (1, 2):
            value = value + swap(value, "section", bit)
        bit = 1
        while bit < wide_count:
            value = value + swap(value, "wide", bit)
            bit *= 2
        return value

    counts_of = sum(jnp.where(shapes == s, n, 0) for s, n in enumerate(counts))
    live = slot_of[None, : 2 * part] < counts_of[:, None]
    upstream = jnp.where(live.reshape(rows, 1), whole_cot, jnp.zeros((), BF))

    matrix = {"qkv": [None] * layers, "proj": [None] * layers, "fc1": [None] * layers, "fc2": [None] * layers}
    small = [None] * layers
    for l in reversed(range(layers)):
        kept = saved[l]
        qkv_w, proj_w, fc1_w, fc2_w = weights[l]
        up = upstream.astype(F32)
        d_mlp_scale = jnp.sum(up * kept["m"], axis=0)
        d_branch = (f32_row(mlp_scale, l) * up).astype(BF)
        d_fc2_b = jnp.sum(d_branch.astype(F32), axis=0)
        matrix["fc2"][l] = wide_first(core_sum(kept["u"], d_branch))
        d_pre = (dot(d_branch, fc2_w, 1, 1) * kept["slope"]).astype(BF)
        d_fc1_b = jnp.sum(d_pre.astype(F32), axis=0)
        matrix["fc1"][l] = x_first(core_sum(kept["n2"], d_pre))
        step, d_gain2, d_offset2 = norm_back(
            kept["h1"], dot(d_pre, fc1_w, 1, 1), f32_row(norm2_gain, l)
        )
        upstream = (up + step).astype(BF)
        mlp_small = jnp.concatenate([d_gain2, d_offset2, d_fc1_b, d_fc2_b, d_mlp_scale])
        mlp_small = all_sum(mlp_small.reshape(-1, 128))

        up = upstream.astype(F32)
        d_attn_scale = jnp.sum(up * kept["r"], axis=0)
        d_branch = (f32_row(attn_scale, l) * up).astype(BF)
        d_proj_b = jnp.sum(d_branch.astype(F32), axis=0)
        matrix["proj"][l] = x_first(core_sum(kept["o"], d_branch))
        d_mixed = dot(d_branch, proj_w, 1, 1).astype(BF)
        d_heads, d_bias = attn_bwd(shapes, kept["qkv"], to_heads(d_mixed), bias[l])
        d_qkv = from_heads(d_heads)
        matrix["qkv"][l] = x_first(core_sum(kept["n"], d_qkv))
        d_qkv_b = jnp.sum(d_qkv.astype(F32), axis=0)
        step, d_gain1, d_offset1 = norm_back(
            kept["h"], dot(d_qkv, qkv_w, 1, 1), f32_row(norm1_gain, l)
        )
        entering = up + step
        upstream = entering.astype(BF)
        d_table = table_grad(
            core_arg, d_bias, targets, indices, sources, entries, part
        )[:mine_heads]
        d_table = jnp.concatenate(
            [pick(ci, d_table, jnp.zeros_like(d_table)), pick(ci, jnp.zeros_like(d_table), d_table)]
        )
        att_small = jnp.concatenate(
            [d_gain1, d_offset1, d_qkv_b[:width], d_qkv_b[2 * width :], d_proj_b, d_attn_scale]
        )
        att_small = all_sum(att_small.reshape(-1, 128))
        d_table = all_sum(d_table)
        small[l] = (mlp_small.reshape(-1), att_small.reshape(-1), d_table)
    d_tokens = to_slots(upstream).astype(F32)

    def piece(which, at, size):
        return jnp.stack([small[l][which][at : at + size] for l in range(layers)])

    def matrices(name):
        return jnp.stack(matrix[name])

    w = width
    return (
        out,
        d_tokens,
        piece(1, 0, w),
        piece(1, w, w),
        matrices("qkv"),
        piece(1, 2 * w, w),
        piece(1, 3 * w, w),
        matrices("proj"),
        piece(1, 4 * w, w),
        piece(1, 5 * w, w),
        jnp.stack([jnp.transpose(small[l][2]) for l in range(layers)]),
        piece(0, 0, w),
        piece(0, w, w),
        matrices("fc1"),
        piece(0, 2 * w, ff),
        matrices("fc2"),
        piece(0, 2 * w + ff, w),
        piece(0, 3 * w + ff, w),
    )


def solution(mesh):
    return jax.shard_map(
        shards,
        mesh=mesh,
        in_specs=(
            P("wide", "section", None),
            P("wide", "section", None),
            P("wide"),
            P(),
            P(),
            P(),
            P(None, "section", None),
            P(),
            P(),
            P(None, "section", None),
            P(),
            P(),
            P(),
            P(),
            P(),
            P(None, "section", None),
            P(),
            P(None, "section", None),
            P(),
            P(),
        ),
        out_specs=(
            P("wide", "section", None),
            P("wide", "section", None),
            P(),
            P(),
            P(None, "wide", "section"),
            P(),
            P(),
            P(None, "wide", "section"),
            P(),
            P(),
            P(),
            P(),
            P(),
            P(None, "wide", "section"),
            P(),
            P(None, "wide", "section"),
            P(),
            P(),
        ),
        check_vma=False,
    )
```

```python
import functools

import numpy as np
import jax
import jax.numpy as jnp
from jax import lax
from jax.experimental import pallas as pl
from jax.experimental.pallas import tpu as pltpu
from jax.sharding import PartitionSpec as P

GRIDS = ((14, 14), (10, 20), (8, 24))
EPS = 1e-06
DEAD = -1e30
ROOT_HALF = 0.7071067811865476
INV_ROOT_2PI = 0.3989422804014327
HEAD = 64
BF = jnp.bfloat16
F32 = jnp.float32


def swap(value, axis, bit):
    count = lax.axis_size(axis)
    return lax.ppermute(value, axis, [(i, i ^ bit) for i in range(count)])


def pick(flag, zero, one):
    return jnp.where(flag == 0, zero, one)


def dot(a, b, ca=1, cb=0, **kw):
    return lax.dot_general(a, b, (((ca,), (cb,)), ((), ())), preferred_element_type=F32, **kw)


LANES = 768

def up8(n): return -(-n//8)*8

def offset_sources(rows, cols, slots):
    pitch, span = 2 * cols - 1, 2 * rows - 1
    source = np.full((1, LANES), -1, np.int32)
    for j in range(span):
        r, rk = (0, j - (rows - 1)) if j >= rows - 1 else (rows - 1, j)
        for t in range(pitch):
            c, ck = (0, t - (cols - 1)) if t >= cols - 1 else (cols - 1, t)
            which = 1 + (1 if r else 0) * 2 + (1 if c else 0)
            source[0, j * pitch + t] = which * slots + 1 + rk * cols + ck
    length = pitch * span
    source[0, length : length + 4] = (0, 1, slots, slots - 1)
    return source

def key_targets(rows, cols, slots):
    pitch, length = 2 * cols - 1, (2 * cols - 1) * (2 * rows - 1)
    out = np.zeros((3, slots), np.int32)
    for k in range(slots):
        if k == 0:
            out[:, k] = length + 2, 0, length
        elif k <= rows * cols:
            rk, ck = divmod(k - 1, cols)
            out[:, k] = (rows - 1 + rk) * pitch + ck, pitch, length + 1
        else:
            out[:, k] = length + 3, 0, length + 3
    return out

def lane_onehot(target, dtype):
    n = target.shape[1]
    number = lax.broadcasted_iota(jnp.int32, (LANES, n), 0)
    return jnp.where(number == target, 1.0, 0.0).astype(dtype)

def block_order(core):
    return (0, 2, 1, 3) if core == 0 else (1, 3, 0, 2)

def bias_kernel(part, core_ref, table_ref, tgt_ref, *refs):
    idx_refs, src_refs = refs[:3], refs[3:6]
    out_ref, wide_ref, nat_ref = refs[6:]
    heads = out_ref.shape[1]
    slots = out_ref.shape[2]
    entries = table_ref.shape[1]
    for s, (rows, cols) in enumerate(GRIDS):
        length = (2 * cols - 1) * (2 * rows - 1)
        step = up8(cols)
        count = rows * cols + 1
        pairs = idx_refs[s].shape[0]
        hot = jnp.where(lax.broadcasted_iota(jnp.int32, (pairs, entries), 1) == idx_refs[s][...], 1.0, 0.0).astype(BF)
        looked = dot(table_ref[...], hot, 1, 1).astype(BF)
        place = lax.broadcasted_iota(jnp.int32, (pairs, LANES), 0)
        hot = jnp.where(place == src_refs[s][...], 1.0, 0.0).astype(BF)
        offsets = dot(looked, hot)
        turned = pltpu.roll(offsets, LANES - (cols - 1), 1)
        tail = lax.broadcasted_iota(jnp.int32, (step, LANES), 1) >= length
        for h in range(heads):
            row = jnp.broadcast_to(offsets[h : h + 1], (step, LANES))
            rolled = jnp.broadcast_to(turned[h : h + 1], (step, LANES))
            rolled = pltpu.roll(rolled, 0, 1, stride=1, stride_axis=0)
            wide_ref[h * step : (h + 1) * step, :] = jnp.where(tail, row, rolled)
        shifted = wide_ref[0 : heads * step, :].astype(BF)
        for r in range(rows):
            target = tgt_ref[s, 0:1, :] - r * tgt_ref[s, 1:2, :]
            patch = dot(shifted, lane_onehot(target, BF))
            for h in range(heads):
                nat_ref[h, 1 + r * cols : 1 + (r + 1) * cols, :] = patch[h * step : h * step + cols]
        first = dot(offsets.astype(BF), lane_onehot(tgt_ref[s, 2:3, :], BF))
        live = jnp.broadcast_to(tgt_ref[s, 2:3, :] < length + 2, (part, slots))
        for h in range(heads):
            nat_ref[h, 0:1, :] = first[h : h + 1]
            nat_ref[h, count:, :] = jnp.broadcast_to(
                offsets[h : h + 1, length + 3 : length + 4], (slots - count, slots)
            )
        for core in range(2):
            @pl.when(core_ref[0] == core)
            def _(core=core):
                for h in range(heads):
                    for j, b in enumerate(block_order(core)):
                        block = nat_ref[h, b * part : (b + 1) * part, :]
                        out_ref[s, h, j * part : (j + 1) * part, :] = jnp.where(live, block, DEAD)

def table_kernel(part, core_ref, db_ref, tgt_ref, *refs):
    idx_refs, src_refs = refs[:3], refs[3:6]
    out_ref, nat_ref, acc_ref, row_ref = refs[6:]
    heads = db_ref.shape[1]
    slots = db_ref.shape[2]
    entries = out_ref.shape[1]
    total = jnp.zeros(out_ref.shape, F32)
    for s, (rows, cols) in enumerate(GRIDS):
        length = (2 * cols - 1) * (2 * rows - 1)
        step = up8(cols)
        count = rows * cols + 1
        pairs = idx_refs[s].shape[0]
        for core in range(2):
            @pl.when(core_ref[0] == core)
            def _(core=core):
                for h in range(heads):
                    for j, b in enumerate(block_order(core)):
                        nat_ref[h, b * part : (b + 1) * part, :] = db_ref[s, h, j * part : (j + 1) * part, :]
        acc_ref[...] = jnp.zeros_like(acc_ref)
        row_ref[...] = jnp.zeros_like(row_ref)
        for r in range(rows):
            for h in range(heads):
                row_ref[h * step : h * step + cols, :] = nat_ref[h, 1 + r * cols : 1 + (r + 1) * cols, :]
            target = tgt_ref[s, 0:1, :] - r * tgt_ref[s, 1:2, :]
            acc_ref[0 : heads * step, :] += dot(row_ref[0 : heads * step, :].astype(BF), lane_onehot(target, BF), 1, 1)
        lane = lax.broadcasted_iota(jnp.int32, (8, LANES), 1)
        offsets = jnp.zeros((8, LANES), F32)
        for c in range(cols):
            part_c = jnp.concatenate([acc_ref[h * step + c : h * step + c + 1, :] for h in range(heads)]
                + [jnp.zeros((8 - heads, LANES), F32)], axis=0)
            back = pltpu.roll(part_c, cols - 1 - c, 1)
            offsets += jnp.where(lane >= length, part_c, back)
        first = jnp.concatenate([nat_ref[h, 0:1, :] for h in range(heads)] + [jnp.zeros((8 - heads, slots), F32)], axis=0)
        offsets += dot(first, lane_onehot(tgt_ref[s, 2:3, :], F32), 1, 1, precision=lax.Precision.HIGHEST)
        rest = jnp.concatenate([jnp.sum(jnp.sum(nat_ref[h, count:, :], axis=0, keepdims=True), axis=1, keepdims=True) for h in range(heads)]
            + [jnp.zeros((8 - heads, 1), F32)], axis=0)
        offsets += jnp.where(lane == length + 3, rest, 0.0)
        place = lax.broadcasted_iota(jnp.int32, (pairs, LANES), 0)
        hot = jnp.where(place == src_refs[s][...], 1.0, 0.0)
        looked = dot(offsets, hot, 1, 1, precision=lax.Precision.HIGHEST)
        hot = jnp.where(lax.broadcasted_iota(jnp.int32, (pairs, entries), 1) == idx_refs[s][...], 1.0, 0.0)
        total += dot(looked, hot, precision=lax.Precision.HIGHEST)
    out_ref[...] = total

VM = pl.BlockSpec(memory_space=pltpu.VMEM)
SM = pl.BlockSpec(memory_space=pltpu.SMEM)

def build_bias(core, table_rows, targets, indices, sources, heads, part):
    slots=4*part
    wide = heads*24
    return pl.pallas_call(functools.partial(bias_kernel, part),
        out_shape=jax.ShapeDtypeStruct((3,heads,slots,slots),F32),
        in_specs=[SM]+[VM]*8, out_specs=VM,
        scratch_shapes=[pltpu.VMEM((wide,LANES),F32), pltpu.VMEM((heads,slots,slots),F32)],
        compiler_params=pltpu.CompilerParams(vmem_limit_bytes=56*2**20),
    )(core, table_rows, targets, *indices, *sources)

def table_grad(core, d_bias, targets, indices, sources, entries, part):
    heads, slots = d_bias.shape[1:3]
    return pl.pallas_call(functools.partial(table_kernel, part),
        out_shape=jax.ShapeDtypeStruct((8,entries),F32),
        in_specs=[SM]+[VM]*8, out_specs=VM,
        scratch_shapes=[pltpu.VMEM((heads,slots,slots),F32), pltpu.VMEM((heads*24,LANES),F32), pltpu.VMEM((heads*24,slots),F32)],
        compiler_params=pltpu.CompilerParams(vmem_limit_bytes=56*2**20),
    )(core, d_bias, targets, *indices, *sources)

def bias_inputs(rel_index, ci, slots, part):
    place = jnp.arange(slots, dtype=jnp.int32)
    core_of = (place // (2 * part)) ^ ci
    within = place % (2 * part)
    slot_of = (within // part) * (2 * part) + core_of * part + within % part
    indices, sources = [], []
    for s,(gr,gc) in enumerate(GRIDS):
        queries = (0, 1, gc, 1 + (gr - 1) * gc, gr * gc)
        indices.append(jnp.concatenate([rel_index[s, a * slots : (a + 1) * slots] for a in queries])[:, None])
        sources.append(jnp.asarray(offset_sources(gr, gc, slots)))
    nat = jnp.asarray(np.stack([key_targets(gr, gc, slots) for gr, gc in GRIDS]))
    blocks = nat.reshape(3, 3, 2, 2, part)
    def order(c):
        return jnp.concatenate([blocks[:, :, :, c].reshape(3,3,2*part), blocks[:, :, :, 1-c].reshape(3,3,2*part)], axis=2)
    targets = jnp.where(ci == 0, order(0), order(1))
    return targets, indices, sources, slot_of


def attn_fwd_kernel(shape_ref, qkv_ref, bias_ref, o_ref):
    width = o_ref.shape[2]
    slots = o_ref.shape[1]
    lane = lax.broadcasted_iota(jnp.int32, (slots, 128), 1)
    for pair in range(width // 128):
        at = pair * 128
        q = qkv_ref[0, :, at : at + 128]
        k = qkv_ref[0, :, width + at : width + at + 128]
        v = qkv_ref[0, :, 2 * width + at : 2 * width + at + 128]
        outs = []
        for e in range(2):
            own = (lane // HEAD) == e
            qm = jnp.where(own, q, jnp.zeros_like(q))
            s = dot(qm, k, 1, 1) * HEAD**-0.5 + bias_ref[0, 2 * pair + e]
            ex = jnp.exp(s - jnp.max(s, axis=1, keepdims=True))
            p = ex / jnp.sum(ex, axis=1, keepdims=True)
            outs.append(dot(p.astype(BF), v))
        o_ref[0, :, at : at + 128] = jnp.where(lane < HEAD, outs[0], outs[1]).astype(BF)


def attn_bwd_kernel(shape_ref, qkv_ref, do_ref, bias_ref, dqkv_ref, db_ref):
    step = pl.program_id(0)
    width = do_ref.shape[2]
    slots = do_ref.shape[1]
    shape = shape_ref[step]

    @pl.when(step == 0)
    def _():
        db_ref[...] = jnp.zeros_like(db_ref)

    lane = lax.broadcasted_iota(jnp.int32, (slots, 128), 1)
    factor = HEAD**-0.5
    for pair in range(width // 128):
        at = pair * 128
        q = qkv_ref[0, :, at : at + 128]
        k = qkv_ref[0, :, width + at : width + at + 128]
        v = qkv_ref[0, :, 2 * width + at : 2 * width + at + 128]
        g = do_ref[0, :, at : at + 128]
        dqs, dks, dvs = [], [], []
        for e in range(2):
            own = (lane // HEAD) == e
            qm = jnp.where(own, q, jnp.zeros_like(q))
            gm = jnp.where(own, g, jnp.zeros_like(g))
            s = dot(qm, k, 1, 1) * factor + bias_ref[0, 2 * pair + e]
            ex = jnp.exp(s - jnp.max(s, axis=1, keepdims=True))
            p = ex / jnp.sum(ex, axis=1, keepdims=True)
            dp = dot(gm, v, 1, 1)
            ds = (p * (dp - jnp.sum(p * dp, axis=1, keepdims=True))).astype(BF)
            db_ref[shape, 2 * pair + e] += ds.astype(F32)
            dvs.append(dot(p.astype(BF), g, 0, 0))
            dqs.append(dot(ds, k))
            dks.append(dot(ds, q, 0, 0))
        low = lane < HEAD
        dqkv_ref[0, :, at : at + 128] = (jnp.where(low, dqs[0], dqs[1]) * factor).astype(BF)
        dqkv_ref[0, :, width + at : width + at + 128] = (
            jnp.where(low, dks[0], dks[1]) * factor
        ).astype(BF)
        dqkv_ref[0, :, 2 * width + at : 2 * width + at + 128] = jnp.where(
            low, dvs[0], dvs[1]
        ).astype(BF)


def attn_fwd(shape_ids, qkv, bias):
    images, slots, wide = qkv.shape
    width = wide // 3
    heads = width // HEAD
    pairs = images * heads
    return pl.pallas_call(
        attn_fwd_kernel,
        grid_spec=pltpu.PrefetchScalarGridSpec(
            num_scalar_prefetch=1,
            grid=(images,),
            in_specs=[
                pl.BlockSpec((1, slots, wide), lambda i, s: (i, 0, 0)),
                pl.BlockSpec((1, heads, slots, slots), lambda i, s: (s[i], 0, 0, 0)),
            ],
            out_specs=pl.BlockSpec((1, slots, width), lambda i, s: (i, 0, 0)),
        ),
        out_shape=jax.ShapeDtypeStruct((images, slots, width), BF),
        compiler_params=pltpu.CompilerParams(vmem_limit_bytes=48 * 2**20),
        cost_estimate=pl.CostEstimate(
            flops=pairs * slots * slots * 128 * 4, bytes_accessed=pairs * slots * slots * 4,
            transcendentals=pairs * slots * slots,
        ),
    )(shape_ids, qkv, bias)


def attn_bwd(shape_ids, qkv, d_out, bias):
    images, slots, wide = qkv.shape
    width = wide // 3
    heads = width // HEAD
    pairs = images * heads
    shapes = bias.shape[0]
    return pl.pallas_call(
        attn_bwd_kernel,
        grid_spec=pltpu.PrefetchScalarGridSpec(
            num_scalar_prefetch=1,
            grid=(images,),
            in_specs=[
                pl.BlockSpec((1, slots, wide), lambda i, s: (i, 0, 0)),
                pl.BlockSpec((1, slots, width), lambda i, s: (i, 0, 0)),
                pl.BlockSpec((1, heads, slots, slots), lambda i, s: (s[i], 0, 0, 0)),
            ],
            out_specs=[
                pl.BlockSpec((1, slots, wide), lambda i, s: (i, 0, 0)),
                pl.BlockSpec((shapes, heads, slots, slots), lambda i, s: (0, 0, 0, 0)),
            ],
        ),
        out_shape=[
            jax.ShapeDtypeStruct((images, slots, wide), BF),
            jax.ShapeDtypeStruct((shapes, heads, slots, slots), F32),
        ],
        compiler_params=pltpu.CompilerParams(vmem_limit_bytes=48 * 2**20),
        cost_estimate=pl.CostEstimate(
            flops=pairs * slots * slots * 128 * 10, bytes_accessed=pairs * slots * slots * 8,
            transcendentals=pairs * slots * slots,
        ),
    )(shape_ids, qkv, d_out, bias)


MESH = pl.DeviceIdType.MESH


def ids():
    section, wide = lax.axis_index("section"), lax.axis_index("wide")
    ci, yi = lax.rem(section, 2), lax.rem(wide, 2)
    core = {"section": section + 1 - 2 * ci}
    across = {"section": lax.rem(section + 2, 4)}
    beside = {"wide": wide + 1 - 2 * yi}
    return section, ci, yi, core, across, beside


def greet(partners):
    barrier = pltpu.get_barrier_semaphore()
    for device in partners:
        pl.semaphore_signal(barrier, inc=1, device_id=device, device_id_type=MESH)
    pl.semaphore_wait(barrier, len(partners))


class Remote:
    def __init__(self, send, recv):
        self.send, self.recv, self.used, self.open = send, recv, 0, []

    def start(self, src, dst, device):
        copy = pltpu.make_async_remote_copy(
            src_ref=src, dst_ref=dst, send_sem=self.send.at[self.used],
            recv_sem=self.recv.at[self.used], device_id=device, device_id_type=MESH,
        )
        self.used += 1
        copy.start()
        self.open.append(copy)
        return copy

    def sent(self, copy):
        if any(copy is other for other in self.open):
            copy.wait_send()
            self.open = [other for other in self.open if other is not copy]

    def finish(self):
        for copy in self.open:
            copy.wait_send()
        self.open = []


class Local:
    def __init__(self, sems):
        self.sems, self.used, self.open = sems, 0, {}

    def start(self, src, dst, name=None):
        copy = pltpu.make_async_copy(src, dst, self.sems.at[self.used])
        self.open[name if name is not None else self.used] = copy
        self.used += 1
        copy.start()

    def wait(self, name):
        if name in self.open:
            self.open.pop(name).wait()

    def finish(self):
        for name in list(self.open):
            self.wait(name)


CHUNKS = (("q", 0, 1152), ("q", 1152, 1152), ("p", 0, 768), ("1", 0, 1536), ("1", 1536, 1536), ("2", 0, 384), ("2", 384, 384))
AHEAD = 2


class Gather:
    def __init__(self, where, own, whole, remote, local, layers):
        section, self.ci, self.yi, self.core, self.across, self.beside = where
        self.own, self.whole, self.remote, self.local = own, whole, remote, local
        self.section = section
        self.far = lax.rem(section + 2, 4)
        self.chunks = [(l,) + chunk for l in range(layers) for chunk in CHUNKS]
        self.state = [dict() for unused in self.chunks]
        self.a_next, self.b_next, self.ready = 0, 0, 0
        for k in range(AHEAD):
            self.begin(k)

    def rows(self, name, shard, half=None):
        depth = self.own[name].shape[1]
        if half is None:
            return pl.ds(pl.multiple_of(shard * depth, depth), depth)
        cut = depth // 2
        return pl.ds(pl.multiple_of(shard * depth + half * cut, cut), cut)

    def begin(self, k):
        if k >= len(self.chunks):
            return
        l, name, at, size = self.chunks[k]
        own, whole = self.own[name], self.whole[name]
        depth = own.shape[1]
        cols = pl.ds(at, size)
        state = self.state[k]
        half = pl.ds(pl.multiple_of(self.yi * (depth // 2), depth // 2), depth // 2)
        state["x"] = self.remote.start(
            own.at[l, half, cols], whole.at[l, self.rows(name, self.section, self.yi), cols], self.across
        )
        place = whole.at[l, self.rows(name, self.section), cols]
        state["c"] = self.remote.start(own.at[l, :, cols], place, self.core)
        self.local.start(own.at[l, :, cols], place, ("own", k))

    def pass_on(self, k, half, device):
        l, name, at, size = self.chunks[k]
        block = self.whole[name].at[l, self.rows(name, self.far, half), pl.ds(at, size)]
        return self.remote.start(block, block, device)

    def step_a(self):
        k = self.a_next
        if k >= len(self.chunks):
            return
        state = self.state[k]
        state["x"].wait_recv()
        state["y"] = self.pass_on(k, self.yi, self.beside)
        state["cx"] = self.pass_on(k, self.yi, self.core)
        self.begin(k + AHEAD)
        self.a_next += 1

    def step_b(self):
        k = self.b_next
        state = self.state[k]
        state["y"].wait_recv()
        state["cy"] = self.pass_on(k, 1 - self.yi, self.core)
        self.b_next += 1

    def need(self, count):
        while self.ready < count:
            k = self.ready
            while self.a_next < k + 2 and self.a_next < len(self.chunks):
                self.step_a()
            while self.b_next < k + 1:
                self.step_b()
            state = self.state[k]
            self.local.wait(("own", k))
            for key in ("c", "cx", "cy"):
                state[key].wait_recv()
            self.ready += 1


def rows_norm(value):
    centered = value - jnp.mean(value, axis=1, keepdims=True)
    return centered * lax.rsqrt(jnp.mean(centered * centered, axis=1, keepdims=True) + EPS)


def two_sides(left, right):
    return jnp.concatenate([left.astype(F32), right.astype(F32)], axis=0).astype(BF)


def forward_kernel(
    h_ref, q_own, p_own, f1_own, f2_own, bias_ref,
    g1_ref, b1_ref, qb_ref, pb_ref, as_ref, g2_ref, b2_ref, fb_ref, mb_ref, ms_ref,
    out_ref, n_out, heads_out, o_out, r_out, h1_out, n2_out, u_out, slope_out, m_out,
    q_out, p_out, f1_out, f2_out,
    wq, wp, w1, w2, h_s, n_s, o_s, r_s, h1_s, n2_s, u_s, slope_s, m_s,
    own_s, send_s, recv_s, om_s, os_s, or_s, bias_s,
    send_sems, recv_sems, local_sems, bias_sems,
):
    layers = q_own.shape[0]
    images, half_slots = own_s.shape[0], own_s.shape[1]
    rows, width = h_ref.shape
    half = width // 2
    heads = half // HEAD
    ff = u_s.shape[1]
    where = ids()
    section, ci, yi, core, across, beside = where
    greet((core, across, beside))
    remote, local = Remote(send_sems, recv_sems), Local(local_sems)
    whole = {"q": wq, "p": wp, "1": w1, "2": w2}
    gather = Gather(
        where, {"q": q_own, "p": p_own, "1": f1_own, "2": f2_own}, whole, remote, local, layers
    )

    def load_bias(l, i, slot):
        return pltpu.make_async_copy(
            bias_ref.at[i, pl.ds(l * heads, heads)], bias_s.at[slot], bias_sems.at[slot]
        )

    load_bias(0, 0, 0).start()
    h_s[...] = h_ref[...]
    lane = lax.broadcasted_iota(jnp.int32, (2 * half_slots, 128), 1)
    for l in range(layers):
        first = l * len(CHUNKS)
        hidden = h_s[...].astype(F32)
        local.wait("n")
        n_s[...] = (rows_norm(hidden) * g1_ref[l : l + 1, :] + b1_ref[l : l + 1, :]).astype(BF)
        local.start(n_s, n_out.at[l], "n")
        gather.need(first + 2)
        local.start(wq.at[l], q_out.at[l], ("w", "q", l))
        if l:
            remote.sent(pending)
            local.wait("own")
        for side, buffer in ((1, send_s), (0, own_s)):
            for which in range(3):
                at = pl.multiple_of(which * width + lax.rem(ci + side, 2) * half, half)
                tile = dot(n_s[...], wq[l, :, pl.ds(at, half)]) + qb_ref[l : l + 1, pl.ds(at, half)]
                buffer[:, :, which * half : (which + 1) * half] = tile.reshape(
                    images, half_slots, half
                ).astype(BF)
            if side:
                pending = remote.start(send_s, recv_s.at[l], core)
        local.start(own_s, heads_out.at[l, 0], "own")
        pending.wait_recv()
        local.start(recv_s.at[l], heads_out.at[l, 1])
        if l:
            remote.sent(o_pending)

        def one_image(i, carry):
            slot = lax.rem(l * images + i, 2)
            if l + 1 < layers:
                load_bias(jnp.where(i + 1 < images, l, l + 1), lax.rem(i + 1, images), 1 - slot).start()
            else:

                @pl.when(i + 1 < images)
                def _():
                    load_bias(l, i + 1, 1 - slot).start()

            load_bias(l, i, slot).wait()
            for pair in range(half // 128):
                q, k, v = (
                    two_sides(
                        own_s[i, :, w * half + pair * 128 : w * half + pair * 128 + 128],
                        recv_s[l, i, :, w * half + pair * 128 : w * half + pair * 128 + 128],
                    )
                    for w in range(3)
                )
                outs = []
                for e in range(2):
                    qm = jnp.where((lane // HEAD) == e, q, jnp.zeros_like(q))
                    s = dot(qm, k, 1, 1) * HEAD**-0.5 + bias_s[slot, 2 * pair + e]
                    ex = jnp.exp(s - jnp.max(s, axis=1, keepdims=True))
                    p = ex / jnp.sum(ex, axis=1, keepdims=True)
                    outs.append(dot(p.astype(BF), v))
                mixed = jnp.where(lane < HEAD, outs[0], outs[1])
                om_s[i, :, pair * 128 : pair * 128 + 128] = mixed[:half_slots].astype(BF)
                os_s[i, :, pair * 128 : pair * 128 + 128] = mixed[half_slots:].astype(BF)
            return carry

        lax.fori_loop(0, images, one_image, 0)
        o_pending = remote.start(os_s, or_s.at[l], core)
        local.wait("o")
        mine = pl.ds(pl.multiple_of(ci * half, half), half)
        other = pl.ds(pl.multiple_of((1 - ci) * half, half), half)
        o_s[:, mine] = om_s[...].astype(F32).reshape(rows, half).astype(BF)
        gather.need(first + 3)
        local.start(wp.at[l], p_out.at[l], ("w", "p", l))
        o_pending.wait_recv()
        o_s[:, other] = or_s[l].astype(F32).reshape(rows, half).astype(BF)
        local.start(o_s, o_out.at[l], "o")
        branch = dot(o_s[...], wp[l]) + pb_ref[l : l + 1, :]
        local.wait("r")
        r_s[...] = branch
        local.start(r_s, r_out.at[l], "r")
        local.wait("h1")
        h1_s[...] = (hidden + as_ref[l : l + 1, :] * branch).astype(BF)
        local.start(h1_s, h1_out.at[l], "h1")
        local.wait("n2")
        n2_s[...] = (
            rows_norm(h1_s[...].astype(F32)) * g2_ref[l : l + 1, :] + b2_ref[l : l + 1, :]
        ).astype(BF)
        local.start(n2_s, n2_out.at[l], "n2")
        local.wait("u")
        local.wait("slope")
        tile = 384
        for part in range(2):
            gather.need(first + 4 + part)

            def one_tile(t, carry):
                at = pl.ds(pl.multiple_of(t * tile, tile), tile)
                pre = dot(n2_s[...], w1[l, :, at]) + fb_ref[l : l + 1, at]
                cdf = 0.5 * (1.0 + lax.erf(pre * ROOT_HALF))
                u_s[:, at] = (pre * cdf).astype(BF)
                slope_s[:, at] = cdf + pre * jnp.exp(-0.5 * pre * pre) * INV_ROOT_2PI
                return carry

            count = ff // tile // 2
            lax.fori_loop(part * count, (part + 1) * count, one_tile, 0)
        local.start(w1.at[l], f1_out.at[l], ("w", "1", l))
        local.start(u_s, u_out.at[l], "u")
        local.start(slope_s, slope_out.at[l], "slope")
        local.wait("m")
        for part in range(2):
            gather.need(first + 6 + part)
            at = slice(part * half, (part + 1) * half)
            branch = dot(u_s[...], w2[l, :, at]) + mb_ref[l : l + 1, at]
            m_s[:, at] = branch
            h_s[:, at] = (h1_s[:, at].astype(F32) + ms_ref[l : l + 1, at] * branch).astype(BF)
        local.start(w2.at[l], f2_out.at[l], ("w", "2", l))
        local.start(m_s, m_out.at[l], "m")
    out_ref[...] = h_s[...]
    remote.finish()
    local.finish()


def forward(hidden, owns, bias, vectors, images):
    rows, width = hidden.shape
    layers = owns[0].shape[0]
    half = width // 2
    half_slots = rows // images
    ff = owns[2].shape[2]
    hbm, vm = pl.BlockSpec(memory_space=pl.ANY), pl.BlockSpec(memory_space=pltpu.VMEM)
    shape = jax.ShapeDtypeStruct
    outs = [
        shape((rows, width), BF),
        shape((layers, rows, width), BF),
        shape((layers, 2, images, half_slots, 3 * half), BF),
        shape((layers, rows, width), BF),
        shape((layers, rows, width), F32),
        shape((layers, rows, width), BF),
        shape((layers, rows, width), BF),
        shape((layers, rows, ff), BF),
        shape((layers, rows, ff), F32),
        shape((layers, rows, width), F32),
        shape((layers, width, 3 * width), BF),
        shape((layers, width, width), BF),
        shape((layers, width, ff), BF),
        shape((layers, ff, width), BF),
    ]
    chunks = layers * len(CHUNKS)
    remote_count = chunks * 5 + 2 * layers
    heads = half // HEAD
    scratch = [
        pltpu.VMEM((layers, width, 3 * width), BF),
        pltpu.VMEM((layers, width, width), BF),
        pltpu.VMEM((layers, width, ff), BF),
        pltpu.VMEM((layers, ff, width), BF),
        pltpu.VMEM((rows, width), BF),
        pltpu.VMEM((rows, width), BF),
        pltpu.VMEM((rows, width), BF),
        pltpu.VMEM((rows, width), F32),
        pltpu.VMEM((rows, width), BF),
        pltpu.VMEM((rows, width), BF),
        pltpu.VMEM((rows, ff), BF),
        pltpu.VMEM((rows, ff), F32),
        pltpu.VMEM((rows, width), F32),
        pltpu.VMEM((images, half_slots, 3 * half), BF),
        pltpu.VMEM((images, half_slots, 3 * half), BF),
        pltpu.VMEM((layers, images, half_slots, 3 * half), BF),
        pltpu.VMEM((images, half_slots, half), BF),
        pltpu.VMEM((images, half_slots, half), BF),
        pltpu.VMEM((layers, images, half_slots, half), BF),
        pltpu.VMEM((2, heads, 2 * half_slots, 2 * half_slots), F32),
        pltpu.SemaphoreType.DMA((remote_count,)),
        pltpu.SemaphoreType.DMA((remote_count,)),
        pltpu.SemaphoreType.DMA((chunks + 14 * layers,)),
        pltpu.SemaphoreType.DMA((2,)),
    ]
    return pl.pallas_call(
        forward_kernel,
        out_shape=outs,
        in_specs=[vm] + [hbm] * 5 + [vm] * 10,
        out_specs=[vm] + [hbm] * 13,
        scratch_shapes=scratch,
        compiler_params=pltpu.CompilerParams(
            collective_id=0, has_side_effects=True, vmem_limit_bytes=60 * 2**20
        ),
    )(hidden, *owns, bias, *vectors)


def norm_parts(hidden):
    hidden = hidden.astype(F32)
    centered = hidden - jnp.mean(hidden, axis=1, keepdims=True)
    inv = lax.rsqrt(jnp.mean(centered * centered, axis=1, keepdims=True) + EPS)
    return centered * inv, inv


def norm_back(hidden, d_normed, gain):
    xhat, inv = norm_parts(hidden)
    d_gain = jnp.sum(d_normed * xhat, axis=0)
    d_offset = jnp.sum(d_normed, axis=0)
    dx = d_normed * gain
    mean_dx = jnp.mean(dx, axis=1, keepdims=True)
    mean_dxx = jnp.mean(dx * xhat, axis=1, keepdims=True)
    return inv * (dx - mean_dx - xhat * mean_dxx), d_gain, d_offset


def shards(
    tokens,
    cotangent,
    shape_id,
    rel_index,
    norm1_gain,
    norm1_bias,
    qkv_weight,
    q_bias,
    v_bias,
    proj_weight,
    proj_bias,
    attn_scale,
    rel_table,
    norm2_gain,
    norm2_bias,
    fc1_weight,
    fc1_bias,
    fc2_weight,
    fc2_bias,
    mlp_scale,
):
    section = lax.axis_index("section")
    wide = lax.axis_index("wide")
    xi, ci, yi = section // 2, section % 2, wide % 2
    wide_count = lax.axis_size("wide")
    layers = qkv_weight.shape[0]
    images, part, width = tokens.shape
    slots = part * 4
    mine = images // 2
    rows = mine * 2 * part
    half = width // 2
    ff = fc1_weight.shape[2]

    def to_images(value):
        cut = value.reshape(2, mine, part, width)
        keep = lax.dynamic_index_in_dim(cut, xi, 0, keepdims=False)
        got = swap(lax.dynamic_index_in_dim(cut, 1 - xi, 0, keepdims=False), "section", 2)
        both = jnp.concatenate([pick(xi, keep, got), pick(xi, got, keep)], axis=1)
        return both.reshape(rows, width)

    def to_slots(value):
        cut = value.reshape(mine, 2, part, width)
        keep = lax.dynamic_index_in_dim(cut, xi, 1, keepdims=False)
        got = swap(lax.dynamic_index_in_dim(cut, 1 - xi, 1, keepdims=False), "section", 2)
        return jnp.concatenate([pick(xi, keep, got), pick(xi, got, keep)], axis=0)

    hidden = to_images(tokens)
    whole_cot = to_images(cotangent)
    shapes = lax.dynamic_slice_in_dim(shape_id, xi * mine, mine, 0)

    targets, indices, sources, slot_of = bias_inputs(rel_index, ci, slots, part)
    counts = [r * c + 1 for r, c in GRIDS]
    heads = rel_table.shape[2]
    entries = rel_table.shape[1]
    mine_heads = heads // 2
    core_arg = jnp.reshape(ci, (1,)).astype(jnp.int32)
    table = pick(ci, rel_table[:, :, :mine_heads], rel_table[:, :, mine_heads:])
    table_rows = jnp.transpose(table, (0, 2, 1)).reshape(layers * mine_heads, entries)
    table_rows = jnp.pad(table_rows, ((0, 16 - layers * mine_heads), (0, 0)))
    bias_all = build_bias(
        core_arg, table_rows, targets, indices, sources, layers * mine_heads, part
    )
    bias = [bias_all[:, l * mine_heads : (l + 1) * mine_heads] for l in range(layers)]
    bias_images = jnp.stack(
        [lax.dynamic_index_in_dim(bias_all, shapes[i], 0, keepdims=False) for i in range(mine)]
    )

    def f32_row(vector, l):
        return vector[l].astype(F32)[None, :]

    def to_heads(value):
        blocks = value.shape[1] // width
        lows = [value[:, b * width : b * width + half] for b in range(blocks)]
        tops = [value[:, b * width + half : (b + 1) * width] for b in range(blocks)]
        keep = jnp.concatenate([pick(ci, a, b) for a, b in zip(lows, tops)], axis=1)
        send = jnp.concatenate([pick(ci, b, a) for a, b in zip(lows, tops)], axis=1)
        got = swap(send, "section", 1)
        shape = (mine, 2 * part, blocks * half)
        return jnp.concatenate([keep.reshape(shape), got.reshape(shape)], axis=1)

    def from_heads(value):
        blocks = value.shape[2] // half
        keep = value[:, : 2 * part].reshape(rows, blocks * half)
        got = swap(value[:, 2 * part :], "section", 1).reshape(rows, blocks * half)
        pieces = []
        for b in range(blocks):
            a, o = keep[:, b * half : (b + 1) * half], got[:, b * half : (b + 1) * half]
            pieces += [pick(ci, a, o), pick(ci, o, a)]
        return jnp.concatenate(pieces, axis=1)

    zero_k = jnp.zeros_like(q_bias)
    vectors = (
        norm1_gain, norm1_bias, jnp.concatenate([q_bias, zero_k, v_bias], axis=1), proj_bias,
        attn_scale, norm2_gain, norm2_bias, fc1_bias, fc2_bias, mlp_scale,
    )
    vectors = [v.astype(F32) for v in vectors]
    entering = hidden
    owns = (qkv_weight, proj_weight, fc1_weight, fc2_weight)
    hidden, *kept_all = forward(hidden, owns, bias_images, vectors, mine)
    n_all, heads_all, o_all, r_all, h1_all, n2_all, u_all, slope_all, m_all = kept_all[:9]
    weights = [[w[l] for w in kept_all[9:]] for l in range(layers)]
    saved = []
    for l in range(layers):
        before = entering if l == 0 else (
            h1_all[l - 1].astype(F32) + f32_row(mlp_scale, l - 1) * m_all[l - 1]
        ).astype(BF)
        saved.append(dict(
            h=before, n=n_all[l], qkv=jnp.concatenate([heads_all[l, 0], heads_all[l, 1]], axis=1),
            o=o_all[l], r=r_all[l], h1=h1_all[l], n2=n2_all[l], u=u_all[l],
            slope=slope_all[l], m=m_all[l],
        ))
    out = to_slots(hidden)

    def columns(value, x, c):
        block = value.shape[1] // 4
        at = (2 * x + c) * block
        return value[:, at : at + block]

    def add(a, b):
        return (a.astype(F32) + b.astype(F32)).astype(BF)

    def core_sum(left, right):
        own = jnp.concatenate(
            [pick(ci, columns(right, x, 0), columns(right, x, 1)) for x in range(2)], axis=1
        )
        other = jnp.concatenate(
            [pick(ci, columns(right, x, 1), columns(right, x, 0)) for x in range(2)], axis=1
        )
        got = swap(dot(left, other, 0, 0).astype(BF), "section", 1)
        return (dot(left, own, 0, 0) + got.astype(F32)).astype(BF)

    def x_step(value):
        block = value.shape[1] // 2
        low, top = value[:, :block], value[:, block:]
        return add(pick(xi, low, top), swap(pick(xi, top, low), "section", 2))

    def wide_steps(value):
        group = value.shape[0] // wide_count
        bit = 1
        value = value[None]
        while bit < wide_count:
            total = value.shape[0] * value.shape[1]
            left = wide_count // bit
            cut = value.reshape(left // 2, 2, total // left, value.shape[2])
            flag = (wide // bit) % 2
            keep = lax.dynamic_index_in_dim(cut, flag, 1, keepdims=False)
            send = lax.dynamic_index_in_dim(cut, 1 - flag, 1, keepdims=False)
            value = add(keep, swap(send, "wide", bit))
            bit *= 2
        return value.reshape(group, value.shape[2])

    def x_first(value):
        return wide_steps(x_step(value)).astype(F32)

    def wide_first(value):
        return x_step(wide_steps(value)).astype(F32)

    def all_sum(value):
        for bit in (1, 2):
            value = value + swap(value, "section", bit)
        bit = 1
        while bit < wide_count:
            value = value + swap(value, "wide", bit)
            bit *= 2
        return value

    counts_of = sum(jnp.where(shapes == s, n, 0) for s, n in enumerate(counts))
    live = slot_of[None, : 2 * part] < counts_of[:, None]
    upstream = jnp.where(live.reshape(rows, 1), whole_cot, jnp.zeros((), BF))

    matrix = {"qkv": [None] * layers, "proj": [None] * layers, "fc1": [None] * layers, "fc2": [None] * layers}
    small = [None] * layers
    for l in reversed(range(layers)):
        kept = saved[l]
        qkv_w, proj_w, fc1_w, fc2_w = weights[l]
        up = upstream.astype(F32)
        d_mlp_scale = jnp.sum(up * kept["m"], axis=0)
        d_branch = (f32_row(mlp_scale, l) * up).astype(BF)
        d_fc2_b = jnp.sum(d_branch.astype(F32), axis=0)
        matrix["fc2"][l] = wide_first(core_sum(kept["u"], d_branch))
        d_pre = (dot(d_branch, fc2_w, 1, 1) * kept["slope"]).astype(BF)
        d_fc1_b = jnp.sum(d_pre.astype(F32), axis=0)
        matrix["fc1"][l] = x_first(core_sum(kept["n2"], d_pre))
        step, d_gain2, d_offset2 = norm_back(
            kept["h1"], dot(d_pre, fc1_w, 1, 1), f32_row(norm2_gain, l)
        )
        upstream = (up + step).astype(BF)
        mlp_small = jnp.concatenate([d_gain2, d_offset2, d_fc1_b, d_fc2_b, d_mlp_scale])
        mlp_small = all_sum(mlp_small.reshape(-1, 128))

        up = upstream.astype(F32)
        d_attn_scale = jnp.sum(up * kept["r"], axis=0)
        d_branch = (f32_row(attn_scale, l) * up).astype(BF)
        d_proj_b = jnp.sum(d_branch.astype(F32), axis=0)
        matrix["proj"][l] = x_first(core_sum(kept["o"], d_branch))
        d_mixed = dot(d_branch, proj_w, 1, 1).astype(BF)
        d_heads, d_bias = attn_bwd(shapes, kept["qkv"], to_heads(d_mixed), bias[l])
        d_qkv = from_heads(d_heads)
        matrix["qkv"][l] = x_first(core_sum(kept["n"], d_qkv))
        d_qkv_b = jnp.sum(d_qkv.astype(F32), axis=0)
        step, d_gain1, d_offset1 = norm_back(
            kept["h"], dot(d_qkv, qkv_w, 1, 1), f32_row(norm1_gain, l)
        )
        entering = up + step
        upstream = entering.astype(BF)
        d_table = table_grad(
            core_arg, d_bias, targets, indices, sources, entries, part
        )[:mine_heads]
        d_table = jnp.concatenate(
            [pick(ci, d_table, jnp.zeros_like(d_table)), pick(ci, jnp.zeros_like(d_table), d_table)]
        )
        att_small = jnp.concatenate(
            [d_gain1, d_offset1, d_qkv_b[:width], d_qkv_b[2 * width :], d_proj_b, d_attn_scale]
        )
        att_small = all_sum(att_small.reshape(-1, 128))
        d_table = all_sum(d_table)
        small[l] = (mlp_small.reshape(-1), att_small.reshape(-1), d_table)
    d_tokens = to_slots(upstream).astype(F32)

    def piece(which, at, size):
        return jnp.stack([small[l][which][at : at + size] for l in range(layers)])

    def matrices(name):
        return jnp.stack(matrix[name])

    w = width
    return (
        out,
        d_tokens,
        piece(1, 0, w),
        piece(1, w, w),
        matrices("qkv"),
        piece(1, 2 * w, w),
        piece(1, 3 * w, w),
        matrices("proj"),
        piece(1, 4 * w, w),
        piece(1, 5 * w, w),
        jnp.stack([jnp.transpose(small[l][2]) for l in range(layers)]),
        piece(0, 0, w),
        piece(0, w, w),
        matrices("fc1"),
        piece(0, 2 * w, ff),
        matrices("fc2"),
        piece(0, 2 * w + ff, w),
        piece(0, 3 * w + ff, w),
    )


def solution(mesh):
    return jax.shard_map(
        shards,
        mesh=mesh,
        in_specs=(
            P("wide", "section", None),
            P("wide", "section", None),
            P("wide"),
            P(),
            P(),
            P(),
            P(None, "section", None),
            P(),
            P(),
            P(None, "section", None),
            P(),
            P(),
            P(),
            P(),
            P(),
            P(None, "section", None),
            P(),
            P(None, "section", None),
            P(),
            P(),
        ),
        out_specs=(
            P("wide", "section", None),
            P("wide", "section", None),
            P(),
            P(),
            P(None, "wide", "section"),
            P(),
            P(),
            P(None, "wide", "section"),
            P(),
            P(),
            P(),
            P(),
            P(),
            P(None, "wide", "section"),
            P(),
            P(None, "wide", "section"),
            P(),
            P(),
        ),
        check_vma=False,
    )
```

```python
import functools

import numpy as np
import jax
import jax.numpy as jnp
from jax import lax
from jax.experimental import pallas as pl
from jax.experimental.pallas import tpu as pltpu
from jax.sharding import PartitionSpec as P

GRIDS = ((14, 14), (10, 20), (8, 24))
EPS = 1e-06
DEAD = -1e30
ROOT_HALF = 0.7071067811865476
INV_ROOT_2PI = 0.3989422804014327
HEAD = 64
BF = jnp.bfloat16
F32 = jnp.float32


def swap(value, axis, bit):
    count = lax.axis_size(axis)
    return lax.ppermute(value, axis, [(i, i ^ bit) for i in range(count)])


def pick(flag, zero, one):
    return jnp.where(flag == 0, zero, one)


def dot(a, b, ca=1, cb=0, **kw):
    return lax.dot_general(a, b, (((ca,), (cb,)), ((), ())), preferred_element_type=F32, **kw)


LANES = 768

def up8(n): return -(-n//8)*8

def offset_sources(rows, cols, slots):
    pitch, span = 2 * cols - 1, 2 * rows - 1
    source = np.full((1, LANES), -1, np.int32)
    for j in range(span):
        r, rk = (0, j - (rows - 1)) if j >= rows - 1 else (rows - 1, j)
        for t in range(pitch):
            c, ck = (0, t - (cols - 1)) if t >= cols - 1 else (cols - 1, t)
            which = 1 + (1 if r else 0) * 2 + (1 if c else 0)
            source[0, j * pitch + t] = which * slots + 1 + rk * cols + ck
    length = pitch * span
    source[0, length : length + 4] = (0, 1, slots, slots - 1)
    return source

def key_targets(rows, cols, slots):
    pitch, length = 2 * cols - 1, (2 * cols - 1) * (2 * rows - 1)
    out = np.zeros((3, slots), np.int32)
    for k in range(slots):
        if k == 0:
            out[:, k] = length + 2, 0, length
        elif k <= rows * cols:
            rk, ck = divmod(k - 1, cols)
            out[:, k] = (rows - 1 + rk) * pitch + ck, pitch, length + 1
        else:
            out[:, k] = length + 3, 0, length + 3
    return out

def lane_onehot(target, dtype):
    n = target.shape[1]
    number = lax.broadcasted_iota(jnp.int32, (LANES, n), 0)
    return jnp.where(number == target, 1.0, 0.0).astype(dtype)

def block_order(core):
    return (0, 2, 1, 3) if core == 0 else (1, 3, 0, 2)

def bias_kernel(part, core_ref, table_ref, tgt_ref, *refs):
    idx_refs, src_refs = refs[:3], refs[3:6]
    out_ref, wide_ref, nat_ref = refs[6:]
    heads = out_ref.shape[1]
    slots = out_ref.shape[2]
    entries = table_ref.shape[1]
    for s, (rows, cols) in enumerate(GRIDS):
        length = (2 * cols - 1) * (2 * rows - 1)
        step = up8(cols)
        count = rows * cols + 1
        pairs = idx_refs[s].shape[0]
        hot = jnp.where(lax.broadcasted_iota(jnp.int32, (pairs, entries), 1) == idx_refs[s][...], 1.0, 0.0).astype(BF)
        looked = dot(table_ref[...], hot, 1, 1).astype(BF)
        place = lax.broadcasted_iota(jnp.int32, (pairs, LANES), 0)
        hot = jnp.where(place == src_refs[s][...], 1.0, 0.0).astype(BF)
        offsets = dot(looked, hot)
        turned = pltpu.roll(offsets, LANES - (cols - 1), 1)
        tail = lax.broadcasted_iota(jnp.int32, (step, LANES), 1) >= length
        for h in range(heads):
            row = jnp.broadcast_to(offsets[h : h + 1], (step, LANES))
            rolled = jnp.broadcast_to(turned[h : h + 1], (step, LANES))
            rolled = pltpu.roll(rolled, 0, 1, stride=1, stride_axis=0)
            wide_ref[h * step : (h + 1) * step, :] = jnp.where(tail, row, rolled)
        shifted = wide_ref[0 : heads * step, :].astype(BF)
        for r in range(rows):
            target = tgt_ref[s, 0:1, :] - r * tgt_ref[s, 1:2, :]
            patch = dot(shifted, lane_onehot(target, BF))
            for h in range(heads):
                nat_ref[h, 1 + r * cols : 1 + (r + 1) * cols, :] = patch[h * step : h * step + cols]
        first = dot(offsets.astype(BF), lane_onehot(tgt_ref[s, 2:3, :], BF))
        live = jnp.broadcast_to(tgt_ref[s, 2:3, :] < length + 2, (part, slots))
        for h in range(heads):
            nat_ref[h, 0:1, :] = first[h : h + 1]
            nat_ref[h, count:, :] = jnp.broadcast_to(
                offsets[h : h + 1, length + 3 : length + 4], (slots - count, slots)
            )
        for core in range(2):
            @pl.when(core_ref[0] == core)
            def _(core=core):
                for h in range(heads):
                    for j, b in enumerate(block_order(core)):
                        block = nat_ref[h, b * part : (b + 1) * part, :]
                        out_ref[s, h, j * part : (j + 1) * part, :] = jnp.where(live, block, DEAD)

def exact_dot(value, hot, ca, cb):
    high = value.astype(BF)
    rest = value - high.astype(F32)
    middle = rest.astype(BF)
    low = (rest - middle.astype(F32)).astype(BF)
    n = value.shape[0]
    out = dot(jnp.concatenate([high, middle, low], axis=0), hot, ca, cb)
    return out[:n] + (out[n : 2 * n] + out[2 * n :])


def table_kernel(part, core_ref, shape_ref, ds_ref, tgt_ref, *refs):
    idx_refs, src_refs = refs[:3], refs[3:6]
    out_ref, nat_ref, acc_ref, row_ref = refs[6:]
    layers, images, per_layer, slots = ds_ref.shape[:4]
    heads = layers * per_layer
    top = out_ref.shape[0]
    entries = out_ref.shape[1]
    total = jnp.zeros(out_ref.shape, F32)

    def stack(pieces):
        return jnp.concatenate(pieces + [jnp.zeros((top - heads,) + pieces[0].shape[1:], F32)], axis=0)

    for s, (rows, cols) in enumerate(GRIDS):
        length = (2 * cols - 1) * (2 * rows - 1)
        step = up8(cols)
        count = rows * cols + 1
        pairs = idx_refs[s].shape[0]
        here = [jnp.where(shape_ref[i] == s, 1.0, 0.0).astype(F32) for i in range(images)]
        for core in range(2):

            @pl.when(core_ref[0] == core)
            def _(core=core):
                for h in range(heads):
                    value = sum(
                        ds_ref[h // per_layer, i, h % per_layer].astype(F32) * here[i] for i in range(images)
                    )
                    for j, b in enumerate(block_order(core)):
                        nat_ref[h, b * part : (b + 1) * part, :] = value[j * part : (j + 1) * part]

        acc_ref[...] = jnp.zeros_like(acc_ref)
        row_ref[...] = jnp.zeros_like(row_ref)
        for r in range(rows):
            for h in range(heads):
                row_ref[h * step : h * step + cols, :] = nat_ref[h, 1 + r * cols : 1 + (r + 1) * cols, :]
            target = tgt_ref[s, 0:1, :] - r * tgt_ref[s, 1:2, :]
            acc_ref[0 : heads * step, :] += dot(
                row_ref[0 : heads * step, :].astype(BF), lane_onehot(target, BF), 1, 1
            )
        lane = lax.broadcasted_iota(jnp.int32, (top, LANES), 1)
        offsets = jnp.zeros((top, LANES), F32)
        for c in range(cols):
            part_c = stack([acc_ref[h * step + c : h * step + c + 1, :] for h in range(heads)])
            back = pltpu.roll(part_c, cols - 1 - c, 1)
            offsets += jnp.where(lane >= length, part_c, back)
        first = stack([nat_ref[h, 0:1, :] for h in range(heads)])
        offsets += exact_dot(first, lane_onehot(tgt_ref[s, 2:3, :], BF), 1, 1)
        rest = stack(
            [
                jnp.sum(jnp.sum(nat_ref[h, count:, :], axis=0, keepdims=True), axis=1, keepdims=True)
                for h in range(heads)
            ]
        )
        offsets += jnp.where(lane == length + 3, rest, 0.0)
        place = lax.broadcasted_iota(jnp.int32, (pairs, LANES), 0)
        hot = jnp.where(place == src_refs[s][...], 1.0, 0.0).astype(BF)
        looked = exact_dot(offsets, hot, 1, 1)
        number = lax.broadcasted_iota(jnp.int32, (pairs, entries), 1)
        hot = jnp.where(number == idx_refs[s][...], 1.0, 0.0).astype(BF)
        total += exact_dot(looked, hot, 1, 0)
    out_ref[...] = total


VM = pl.BlockSpec(memory_space=pltpu.VMEM)
SM = pl.BlockSpec(memory_space=pltpu.SMEM)

def build_bias(core, table_rows, targets, indices, sources, heads, part):
    slots=4*part
    wide = heads*24
    return pl.pallas_call(functools.partial(bias_kernel, part),
        out_shape=jax.ShapeDtypeStruct((3,heads,slots,slots),F32),
        in_specs=[SM]+[VM]*8, out_specs=VM,
        scratch_shapes=[pltpu.VMEM((wide,LANES),F32), pltpu.VMEM((heads,slots,slots),F32)],
        compiler_params=pltpu.CompilerParams(vmem_limit_bytes=56*2**20),
    )(core, table_rows, targets, *indices, *sources)

def table_grad(core, shapes, d_scores, targets, indices, sources, entries, part):
    layers, unused, per_layer, slots = d_scores.shape[:4]
    heads = layers * per_layer
    return pl.pallas_call(
        functools.partial(table_kernel, part),
        out_shape=jax.ShapeDtypeStruct((up8(heads), entries), F32),
        in_specs=[SM] * 2 + [VM] * 8,
        out_specs=VM,
        scratch_shapes=[
            pltpu.VMEM((heads, slots, slots), F32),
            pltpu.VMEM((heads * 24, LANES), F32),
            pltpu.VMEM((heads * 24, slots), F32),
        ],
        compiler_params=pltpu.CompilerParams(vmem_limit_bytes=56 * 2**20),
    )(core, shapes, d_scores, targets, *indices, *sources)


def bias_inputs(rel_index, ci, slots, part):
    place = jnp.arange(slots, dtype=jnp.int32)
    core_of = (place // (2 * part)) ^ ci
    within = place % (2 * part)
    slot_of = (within // part) * (2 * part) + core_of * part + within % part
    indices, sources = [], []
    for s,(gr,gc) in enumerate(GRIDS):
        queries = (0, 1, gc, 1 + (gr - 1) * gc, gr * gc)
        indices.append(jnp.concatenate([rel_index[s, a * slots : (a + 1) * slots] for a in queries])[:, None])
        sources.append(jnp.asarray(offset_sources(gr, gc, slots)))
    nat = jnp.asarray(np.stack([key_targets(gr, gc, slots) for gr, gc in GRIDS]))
    blocks = nat.reshape(3, 3, 2, 2, part)
    def order(c):
        return jnp.concatenate([blocks[:, :, :, c].reshape(3,3,2*part), blocks[:, :, :, 1-c].reshape(3,3,2*part)], axis=2)
    targets = jnp.where(ci == 0, order(0), order(1))
    return targets, indices, sources, slot_of


MESH = pl.DeviceIdType.MESH


def ids():
    section, wide = lax.axis_index("section"), lax.axis_index("wide")
    ci, yi = lax.rem(section, 2), lax.rem(wide, 2)
    core = {"section": section + 1 - 2 * ci}
    across = {"section": lax.rem(section + 2, 4)}
    beside = {"wide": wide + 1 - 2 * yi}
    return section, ci, yi, core, across, beside


def greet(partners):
    barrier = pltpu.get_barrier_semaphore()
    for device in partners:
        pl.semaphore_signal(barrier, inc=1, device_id=device, device_id_type=MESH)
    pl.semaphore_wait(barrier, len(partners))


class Remote:
    def __init__(self, send, recv):
        self.send, self.recv, self.used, self.open = send, recv, 0, []

    def start(self, src, dst, device):
        copy = pltpu.make_async_remote_copy(
            src_ref=src, dst_ref=dst, send_sem=self.send.at[self.used],
            recv_sem=self.recv.at[self.used], device_id=device, device_id_type=MESH,
        )
        self.used += 1
        copy.start()
        self.open.append(copy)
        return copy

    def sent(self, copy):
        if any(copy is other for other in self.open):
            copy.wait_send()
            self.open = [other for other in self.open if other is not copy]

    def finish(self):
        for copy in self.open:
            copy.wait_send()
        self.open = []


class Local:
    def __init__(self, sems):
        self.sems, self.used, self.open = sems, 0, {}

    def start(self, src, dst, name=None):
        copy = pltpu.make_async_copy(src, dst, self.sems.at[self.used])
        self.open[name if name is not None else self.used] = copy
        self.used += 1
        copy.start()

    def wait(self, name):
        if name in self.open:
            self.open.pop(name).wait()

    def finish(self):
        for name in list(self.open):
            self.wait(name)


CHUNKS = (("q", 0, 1152), ("q", 1152, 1152), ("p", 0, 768), ("1", 0, 1536), ("1", 1536, 1536), ("2", 0, 384), ("2", 384, 384))
AHEAD = 2


class Gather:
    def __init__(self, where, own, whole, remote, local, layers):
        section, self.ci, self.yi, self.core, self.across, self.beside = where
        self.own, self.whole, self.remote, self.local = own, whole, remote, local
        self.section = section
        self.far = lax.rem(section + 2, 4)
        self.chunks = [(l,) + chunk for l in range(layers) for chunk in CHUNKS]
        self.state = [dict() for unused in self.chunks]
        self.a_next, self.b_next, self.ready = 0, 0, 0
        for k in range(AHEAD):
            self.begin(k)

    def rows(self, name, shard, half=None):
        depth = self.own[name].shape[1]
        if half is None:
            return pl.ds(pl.multiple_of(shard * depth, depth), depth)
        cut = depth // 2
        return pl.ds(pl.multiple_of(shard * depth + half * cut, cut), cut)

    def begin(self, k):
        if k >= len(self.chunks):
            return
        l, name, at, size = self.chunks[k]
        own, whole = self.own[name], self.whole[name]
        depth = own.shape[1]
        cols = pl.ds(at, size)
        state = self.state[k]
        half = pl.ds(pl.multiple_of(self.yi * (depth // 2), depth // 2), depth // 2)
        state["x"] = self.remote.start(
            own.at[l, half, cols], whole.at[l, self.rows(name, self.section, self.yi), cols], self.across
        )
        place = whole.at[l, self.rows(name, self.section), cols]
        state["c"] = self.remote.start(own.at[l, :, cols], place, self.core)
        self.local.start(own.at[l, :, cols], place, ("own", k))

    def pass_on(self, k, half, device):
        l, name, at, size = self.chunks[k]
        block = self.whole[name].at[l, self.rows(name, self.far, half), pl.ds(at, size)]
        return self.remote.start(block, block, device)

    def step_a(self):
        k = self.a_next
        if k >= len(self.chunks):
            return
        state = self.state[k]
        state["x"].wait_recv()
        state["y"] = self.pass_on(k, self.yi, self.beside)
        state["cx"] = self.pass_on(k, self.yi, self.core)
        self.begin(k + AHEAD)
        self.a_next += 1

    def step_b(self):
        k = self.b_next
        state = self.state[k]
        state["y"].wait_recv()
        state["cy"] = self.pass_on(k, 1 - self.yi, self.core)
        self.b_next += 1

    def need(self, count):
        while self.ready < count:
            k = self.ready
            while self.a_next < k + 2 and self.a_next < len(self.chunks):
                self.step_a()
            while self.b_next < k + 1:
                self.step_b()
            state = self.state[k]
            self.local.wait(("own", k))
            for key in ("c", "cx", "cy"):
                state[key].wait_recv()
            self.ready += 1


def rows_norm(value):
    centered = value - jnp.mean(value, axis=1, keepdims=True)
    return centered * lax.rsqrt(jnp.mean(centered * centered, axis=1, keepdims=True) + EPS)


def two_sides(left, right):
    return jnp.concatenate([left.astype(F32), right.astype(F32)], axis=0).astype(BF)


def forward_kernel(
    h_ref, q_own, p_own, f1_own, f2_own, bias_ref,
    g1_ref, b1_ref, qb_ref, pb_ref, as_ref, g2_ref, b2_ref, fb_ref, mb_ref, ms_ref,
    out_ref, h_out, n_out, heads_out, o_out, r_out, h1_out, n2_out, u_out, slope_out, m_out,
    q_out, p_out, f1_out, f2_out,
    wq, wp, w1, w2, h_s, n_s, o_s, r_s, h1_s, n2_s, u_s, slope_s, m_s,
    own_s, send_s, recv_s, om_s, os_s, or_s, bias_s,
    send_sems, recv_sems, local_sems, bias_sems,
):
    layers = q_own.shape[0]
    images, half_slots = own_s.shape[0], own_s.shape[1]
    rows, width = h_ref.shape
    half = width // 2
    heads = half // HEAD
    ff = u_s.shape[1]
    where = ids()
    section, ci, yi, core, across, beside = where
    greet((core, across, beside))
    remote, local = Remote(send_sems, recv_sems), Local(local_sems)
    whole = {"q": wq, "p": wp, "1": w1, "2": w2}
    gather = Gather(
        where, {"q": q_own, "p": p_own, "1": f1_own, "2": f2_own}, whole, remote, local, layers
    )

    def load_bias(l, i, slot):
        return pltpu.make_async_copy(
            bias_ref.at[i, pl.ds(l * heads, heads)], bias_s.at[slot], bias_sems.at[slot]
        )

    load_bias(0, 0, 0).start()
    h_s[...] = h_ref[...]
    lane = lax.broadcasted_iota(jnp.int32, (2 * half_slots, 128), 1)
    for l in range(layers):
        first = l * len(CHUNKS)
        hidden = h_s[...].astype(F32)
        local.start(h_s, h_out.at[l], "h")
        local.wait("n")
        n_s[...] = (rows_norm(hidden) * g1_ref[l : l + 1, :] + b1_ref[l : l + 1, :]).astype(BF)
        local.start(n_s, n_out.at[l], "n")
        gather.need(first + 2)
        local.start(wq.at[l], q_out.at[l], ("w", "q", l))
        if l:
            remote.sent(pending)
            local.wait("own")
        for side, buffer in ((1, send_s), (0, own_s)):
            for which in range(3):
                at = pl.multiple_of(which * width + lax.rem(ci + side, 2) * half, half)
                tile = dot(n_s[...], wq[l, :, pl.ds(at, half)]) + qb_ref[l : l + 1, pl.ds(at, half)]
                buffer[:, :, which * half : (which + 1) * half] = tile.reshape(
                    images, half_slots, half
                ).astype(BF)
            if side:
                pending = remote.start(send_s, recv_s.at[l], core)
        local.start(own_s, heads_out.at[l, 0], "own")
        pending.wait_recv()
        local.start(recv_s.at[l], heads_out.at[l, 1])
        if l:
            remote.sent(o_pending)

        def one_image(i, carry):
            slot = lax.rem(l * images + i, 2)
            if l + 1 < layers:
                load_bias(jnp.where(i + 1 < images, l, l + 1), lax.rem(i + 1, images), 1 - slot).start()
            else:

                @pl.when(i + 1 < images)
                def _():
                    load_bias(l, i + 1, 1 - slot).start()

            load_bias(l, i, slot).wait()
            for pair in range(half // 128):
                q, k, v = (
                    two_sides(
                        own_s[i, :, w * half + pair * 128 : w * half + pair * 128 + 128],
                        recv_s[l, i, :, w * half + pair * 128 : w * half + pair * 128 + 128],
                    )
                    for w in range(3)
                )
                outs = []
                for e in range(2):
                    qm = jnp.where((lane // HEAD) == e, q, jnp.zeros_like(q))
                    s = dot(qm, k, 1, 1) * HEAD**-0.5 + bias_s[slot, 2 * pair + e]
                    ex = jnp.exp(s - jnp.max(s, axis=1, keepdims=True))
                    p = ex / jnp.sum(ex, axis=1, keepdims=True)
                    outs.append(dot(p.astype(BF), v))
                mixed = jnp.where(lane < HEAD, outs[0], outs[1])
                om_s[i, :, pair * 128 : pair * 128 + 128] = mixed[:half_slots].astype(BF)
                os_s[i, :, pair * 128 : pair * 128 + 128] = mixed[half_slots:].astype(BF)
            return carry

        lax.fori_loop(0, images, one_image, 0)
        o_pending = remote.start(os_s, or_s.at[l], core)
        local.wait("o")
        mine = pl.ds(pl.multiple_of(ci * half, half), half)
        other = pl.ds(pl.multiple_of((1 - ci) * half, half), half)
        o_s[:, mine] = om_s[...].astype(F32).reshape(rows, half).astype(BF)
        gather.need(first + 3)
        local.start(wp.at[l], p_out.at[l], ("w", "p", l))
        o_pending.wait_recv()
        o_s[:, other] = or_s[l].astype(F32).reshape(rows, half).astype(BF)
        local.start(o_s, o_out.at[l], "o")
        branch = dot(o_s[...], wp[l]) + pb_ref[l : l + 1, :]
        local.wait("r")
        r_s[...] = branch
        local.start(r_s, r_out.at[l], "r")
        local.wait("h1")
        h1_s[...] = (hidden + as_ref[l : l + 1, :] * branch).astype(BF)
        local.start(h1_s, h1_out.at[l], "h1")
        local.wait("n2")
        n2_s[...] = (
            rows_norm(h1_s[...].astype(F32)) * g2_ref[l : l + 1, :] + b2_ref[l : l + 1, :]
        ).astype(BF)
        local.start(n2_s, n2_out.at[l], "n2")
        local.wait("u")
        local.wait("slope")
        tile = 384
        for part in range(2):
            gather.need(first + 4 + part)

            def one_tile(t, carry):
                at = pl.ds(pl.multiple_of(t * tile, tile), tile)
                pre = dot(n2_s[...], w1[l, :, at]) + fb_ref[l : l + 1, at]
                cdf = 0.5 * (1.0 + lax.erf(pre * ROOT_HALF))
                u_s[:, at] = (pre * cdf).astype(BF)
                slope_s[:, at] = cdf + pre * jnp.exp(-0.5 * pre * pre) * INV_ROOT_2PI
                return carry

            count = ff // tile // 2
            lax.fori_loop(part * count, (part + 1) * count, one_tile, 0)
        local.start(w1.at[l], f1_out.at[l], ("w", "1", l))
        local.start(u_s, u_out.at[l], "u")
        local.start(slope_s, slope_out.at[l], "slope")
        local.wait("m")
        local.wait("h")
        for part in range(2):
            gather.need(first + 6 + part)
            at = slice(part * half, (part + 1) * half)
            branch = dot(u_s[...], w2[l, :, at]) + mb_ref[l : l + 1, at]
            m_s[:, at] = branch
            h_s[:, at] = (h1_s[:, at].astype(F32) + ms_ref[l : l + 1, at] * branch).astype(BF)
        local.start(w2.at[l], f2_out.at[l], ("w", "2", l))
        local.start(m_s, m_out.at[l], "m")
    out_ref[...] = h_s[...]
    remote.finish()
    local.finish()


def forward(hidden, owns, bias, vectors, images):
    rows, width = hidden.shape
    layers = owns[0].shape[0]
    half = width // 2
    half_slots = rows // images
    ff = owns[2].shape[2]
    hbm, vm = pl.BlockSpec(memory_space=pl.ANY), pl.BlockSpec(memory_space=pltpu.VMEM)
    shape = jax.ShapeDtypeStruct
    outs = [
        shape((rows, width), BF),
        shape((layers, rows, width), BF),
        shape((layers, rows, width), BF),
        shape((layers, 2, images, half_slots, 3 * half), BF),
        shape((layers, rows, width), BF),
        shape((layers, rows, width), F32),
        shape((layers, rows, width), BF),
        shape((layers, rows, width), BF),
        shape((layers, rows, ff), BF),
        shape((layers, rows, ff), F32),
        shape((layers, rows, width), F32),
        shape((layers, width, 3 * width), BF),
        shape((layers, width, width), BF),
        shape((layers, width, ff), BF),
        shape((layers, ff, width), BF),
    ]
    chunks = layers * len(CHUNKS)
    remote_count = chunks * 5 + 2 * layers
    heads = half // HEAD
    scratch = [
        pltpu.VMEM((layers, width, 3 * width), BF),
        pltpu.VMEM((layers, width, width), BF),
        pltpu.VMEM((layers, width, ff), BF),
        pltpu.VMEM((layers, ff, width), BF),
        pltpu.VMEM((rows, width), BF),
        pltpu.VMEM((rows, width), BF),
        pltpu.VMEM((rows, width), BF),
        pltpu.VMEM((rows, width), F32),
        pltpu.VMEM((rows, width), BF),
        pltpu.VMEM((rows, width), BF),
        pltpu.VMEM((rows, ff), BF),
        pltpu.VMEM((rows, ff), F32),
        pltpu.VMEM((rows, width), F32),
        pltpu.VMEM((images, half_slots, 3 * half), BF),
        pltpu.VMEM((images, half_slots, 3 * half), BF),
        pltpu.VMEM((layers, images, half_slots, 3 * half), BF),
        pltpu.VMEM((images, half_slots, half), BF),
        pltpu.VMEM((images, half_slots, half), BF),
        pltpu.VMEM((layers, images, half_slots, half), BF),
        pltpu.VMEM((2, heads, 2 * half_slots, 2 * half_slots), F32),
        pltpu.SemaphoreType.DMA((remote_count,)),
        pltpu.SemaphoreType.DMA((remote_count,)),
        pltpu.SemaphoreType.DMA((chunks + 15 * layers,)),
        pltpu.SemaphoreType.DMA((2,)),
    ]
    return pl.pallas_call(
        forward_kernel,
        out_shape=outs,
        in_specs=[vm] + [hbm] * 5 + [vm] * 10,
        out_specs=[vm] + [hbm] * 14,
        scratch_shapes=scratch,
        compiler_params=pltpu.CompilerParams(
            collective_id=0, has_side_effects=True, vmem_limit_bytes=(48 if rows <= 320 else 60) * 2**20
        ),
    )(hidden, *owns, bias, *vectors)


BEFORE = {
    (0, "im0"): ((0, 0, 1), (0, 1, 1)),
    (0, "im2"): ((0, 0, 2), (0, 1, 2), (0, 2, 1), (0, 3, 1)),
    (0, "sent4"): ((0, 0, 3), (0, 1, 3), (0, 2, 2), (0, 3, 2)),
    (1, "give0"): ((0, 0, 4), (0, 1, 4)),
    (1, "sent0"): ((0, 2, 3), (0, 3, 3), (0, 4, 1), (0, 5, 1)),
    (1, "give2"): ((0, 2, 4), (0, 3, 4)),
    (1, "sent2"): ((0, 4, 2), (0, 5, 2), (1, 0, 1), (1, 1, 1)),
    (1, "im0"): ((0, 4, 3), (0, 5, 3)),
    (1, "im2"): ((1, 0, 2), (1, 1, 2), (1, 2, 1), (1, 3, 1)),
    (1, "give4"): ((0, 4, 4), (0, 5, 4)),
    (1, "sent4"): (
        (1, 0, 3), (1, 1, 3), (1, 2, 2), (1, 3, 2), (1, 0, 4), (1, 1, 4), (1, 4, 1), (1, 5, 1), (1, 2, 3), (1, 3, 3),
        (1, 4, 2), (1, 5, 2), (1, 2, 4), (1, 3, 4), (1, 4, 3), (1, 5, 3), (1, 4, 4), (1, 5, 4),
    ),
}


def backward_kernel(
    e_ref, h_in, n_in, heads_in, o_in, r_in, h1_in, n2_in, u_in, slope_in, m_in, q_in, p_in, f1_in, f2_in, bias_ref,
    g1_ref, as_ref, g2_ref, ms_ref,
    dx_ref, small_ref, matrix_ref, ds_out,
    e_s, h_s, n_s, heads_s, o_s, r_s, h1_s, n2_s, u_s, slope_s, m_s, wq, wp, w1, w2, bias_s,
    dm_s, cols_s, dz_s, dq_s, do_own, do_send, do_recv, dq_own, dq_send, dq_recv, ds_s,
    theirs, total, in1, in2, in3, in4,
    send_sems, recv_sems, load_sems, bias_sems, ds_sems, slope_sems, credit,
):
    layers = q_in.shape[0]
    images, half_slots = do_own.shape[0], do_own.shape[1]
    rows, width = e_ref.shape
    half = width // 2
    heads = half // HEAD
    block = width // 4
    cut = block // 2
    tile = half
    ff = u_s.shape[1]
    section, ci, yi, core, across, beside = ids()
    wide = lax.axis_index("wide")
    xi = section // 2
    z1, z2 = lax.rem(wide // 2, 2), lax.rem(wide // 4, 2)
    not_xi, not_yi, not_z1, not_z2, not_ci = 1 - xi, 1 - yi, 1 - z1, 1 - z2, 1 - ci
    near = {"wide": wide + 2 - 4 * z1}
    far = {"wide": wide + 4 - 8 * z2}
    greet((core, across, beside, near, far))

    def partner(c, stage):
        swap_xy = (core, across, beside, near, far) if c % 2 == 0 else (core, beside, across, near, far)
        return swap_xy[stage]

    def parts(c, stage):
        if stage == 0:
            return theirs.at[c % 2], total.at[c], total.at[c]
        if c % 2 == 0:
            if stage == 1:
                return total.at[c, not_xi], total.at[c, xi], in1.at[c]
            if stage == 2:
                return total.at[c, xi, :, :, not_yi], total.at[c, xi, :, :, yi], in2.at[c]
        else:
            if stage == 1:
                return total.at[c, :, :, :, not_yi], total.at[c, :, :, :, yi], in1.at[c]
            if stage == 2:
                return total.at[c, not_xi, :, :, yi], total.at[c, xi, :, :, yi], in2.at[c]
        if stage == 3:
            return total.at[c, xi, :, not_z1, yi], total.at[c, xi, :, z1, yi], in3.at[c]
        return total.at[c, xi, not_z2, z1, yi], total.at[c, xi, z2, z1, yi], in4.at[c]

    def link(turn, c, stage):
        at = (turn * 6 + c) * 5 + stage
        src, unused, dst = parts(c, stage)
        return pltpu.make_async_remote_copy(
            src_ref=src, dst_ref=dst, send_sem=send_sems.at[at], recv_sem=recv_sems.at[at],
            device_id=partner(c, stage), device_id_type=MESH,
        )

    def launch(turn, c, stage):
        if turn:
            pl.semaphore_wait(credit.at[c, stage], 1)
        link(turn, c, stage).start()

    def advance(turn, c, stage):
        link(turn, c, stage).wait_recv()
        unused, keep, came = parts(c, stage)
        summed = keep[...].astype(F32) + came[...].astype(F32)
        if stage < 4:
            keep[...] = summed.astype(BF)
            launch(turn, c, stage + 1)
            return
        matrix_ref[layers - 1 - turn, c] = summed
        for earlier in range(1, 5):
            link(turn, c, earlier).wait_send()
        if turn + 1 < layers:
            for earlier in range(5):
                pl.semaphore_signal(
                    credit.at[c, earlier], inc=1, device_id=partner(c, earlier), device_id_type=MESH
                )

    def hook(turn, name):
        for item in BEFORE.get((turn, name), ()):
            advance(*item)

    extra = layers * 30

    def exchange(index, src, dst):
        return pltpu.make_async_remote_copy(
            src_ref=src, dst_ref=dst, send_sem=send_sems.at[extra + index], recv_sem=recv_sems.at[extra + index],
            device_id=core, device_id_type=MESH,
        )

    def loads(names, l):
        table = {
            "m": (m_in, m_s), "u": (u_in, u_s), "w2": (f2_in, w2), "n2": (n2_in, n2_s),
            "w1": (f1_in, w1), "h1": (h1_in, h1_s), "r": (r_in, r_s), "wp": (p_in, wp), "heads": (heads_in, heads_s),
            "o": (o_in, o_s), "n": (n_in, n_s), "wq": (q_in, wq), "h": (h_in, h_s),
        }
        order = list(table)
        return [
            pltpu.make_async_copy(table[name][0].at[l], table[name][1], load_sems.at[order.index(name)])
            for name in names
        ]

    def begin(names, l):
        for copy in loads(names, l):
            copy.start()

    def have(name, l):
        loads((name,), l)[0].wait()

    feed = ("m", "u", "w2", "n2", "w1", "h1")
    attend = ("r", "wp", "heads", "o", "n", "wq", "h")

    def load_bias(l, i, slot):
        return pltpu.make_async_copy(
            bias_ref.at[i, pl.ds(l * heads, heads)], bias_s.at[slot], bias_sems.at[slot]
        )

    def load_slope(l, t, slot):
        at = pl.ds(pl.multiple_of(t * tile, tile), tile)
        return pltpu.make_async_copy(slope_in.at[l, :, at], slope_s.at[slot], slope_sems.at[slot])

    def store_ds(l, i, slot):
        return pltpu.make_async_copy(ds_s.at[slot], ds_out.at[l, i], ds_sems.at[slot])

    last = layers - 1
    begin(feed, last)
    begin(attend, last)
    load_bias(last, 0, 0).start()
    e_s[...] = e_ref[...].astype(F32)
    small_ref[...] = jnp.zeros_like(small_ref)

    def note(l, row, value):
        small_ref[l, row : row + 1, :] = jnp.sum(value, axis=0, keepdims=True)

    def mine_first(low, top):
        return jnp.where(ci == 0, low, top)

    def norm_step(l, hidden, d_normed, gain_ref, row):
        hidden = hidden.astype(F32)
        centered = hidden - jnp.mean(hidden, axis=1, keepdims=True)
        inv = lax.rsqrt(jnp.mean(centered * centered, axis=1, keepdims=True) + EPS)
        xhat = centered * inv
        note(l, row, d_normed * xhat)
        note(l, row + 1, d_normed)
        dx = d_normed * gain_ref[l : l + 1, :]
        mean_dx = jnp.mean(dx, axis=1, keepdims=True)
        mean_dxx = jnp.mean(dx * xhat, axis=1, keepdims=True)
        return e_s[...] + inv * (dx - mean_dx - xhat * mean_dxx)

    def give(turn, c):
        hook(turn, "give%d" % c)
        launch(turn, c, 0)
        launch(turn, c + 1, 0)

    def arrive(turn, c):
        link(turn, c, 0).wait_recv()
        link(turn, c + 1, 0).wait_recv()

    def go(turn, c):
        launch(turn, c, 1)
        launch(turn, c + 1, 1)
        link(turn, c, 0).wait_send()
        link(turn, c + 1, 0).wait_send()
        hook(turn, "sent%d" % c)

    def rounds(turn, c, product, side):
        for h in range(2):

            def one_x(x, carry):
                value = product(x, h).reshape(2, 2, 2, width // 8, half)
                if side:
                    theirs[h, x] = value.astype(BF)
                else:
                    total[c + h, x] = (value + total[c + h, x].astype(F32)).astype(BF)
                return carry

            lax.fori_loop(0, 2, one_x, 0)

    for turn in range(layers):
        l = last - turn
        have("m", l)
        up = e_s[...]
        note(l, 9, up * m_s[...])
        d_branch = (ms_ref[l : l + 1, :] * up).astype(BF)
        dm_s[...] = d_branch
        d_branch = d_branch.astype(F32)
        note(l, 8, d_branch)
        sides = [
            jnp.concatenate(
                [
                    d_branch[:, (2 * x + c) * block + h * cut : (2 * x + c) * block + (h + 1) * cut]
                    for h in range(2)
                    for x in range(2)
                ],
                axis=1,
            )
            for c in range(2)
        ]
        cols_s[0] = mine_first(sides[0], sides[1]).astype(BF)
        cols_s[1] = mine_first(sides[1], sides[0]).astype(BF)
        have("u", l)

        def by_rows(side, first):
            def one(w, carry):
                at = pl.ds(pl.multiple_of(w * tile, tile), tile)
                value = dot(cols_s[side], u_s[:, at], 0, 0)
                w2_, w1_, w0_ = w // 4, lax.rem(w // 2, 2), lax.rem(w, 2)
                for h in range(2):
                    for x in range(2):
                        piece = value[(2 * h + x) * cut : (2 * h + x + 1) * cut]
                        if side:
                            theirs[h, x, w2_, w1_, w0_] = piece.astype(BF)
                        else:
                            total[h, x, w2_, w1_, w0_] = (
                                piece + total[h, x, w2_, w1_, w0_].astype(F32)
                            ).astype(BF)
                return carry

            lax.fori_loop(0, ff // tile, one, 0)

        load_slope(l, 0, 0).start()
        by_rows(1, 0)
        give(turn, 0)
        have("w2", l)

        def one_tile(t, carry):
            at = pl.ds(pl.multiple_of(t * tile, tile), tile)
            slot = lax.rem(t, 2)

            @pl.when(t + 1 < ff // tile)
            def _():
                load_slope(l, t + 1, 1 - slot).start()

            load_slope(l, t, slot).wait()
            d_pre = (dot(dm_s[...], w2[at, :], 1, 1) * slope_s[slot]).astype(BF)
            dz_s[:, at] = d_pre
            sums = jnp.sum(d_pre.astype(F32), axis=0, keepdims=True)
            small_ref[l, pl.ds(10 + t // 2, 1), pl.ds(pl.multiple_of(lax.rem(t, 2) * tile, tile), tile)] = sums
            return carry

        lax.fori_loop(0, ff // tile, one_tile, 0)
        arrive(turn, 0)
        by_rows(0, 0)
        go(turn, 0)
        have("n2", l)

        def of_first(side):
            def product(x, h):
                c = not_ci if side else ci
                at = pl.multiple_of((2 * x + c) * width + h * half, half)
                return dot(n2_s[...], dz_s[:, pl.ds(at, half)], 0, 0)

            return product

        rounds(turn, 2, of_first(1), 1)
        give(turn, 2)
        have("w1", l)
        have("h1", l)
        d_normed = jnp.concatenate(
            [dot(dz_s[...], w1[i * half : (i + 1) * half, :], 1, 1) for i in range(2)], axis=1
        )
        e_s[...] = norm_step(l, h1_s[...], d_normed, g2_ref, 6).astype(BF).astype(F32)
        have("r", l)
        up = e_s[...]
        note(l, 5, up * r_s[...])
        d_branch = (as_ref[l : l + 1, :] * up).astype(BF)
        dm_s[...] = d_branch
        note(l, 4, d_branch.astype(F32))
        have("wp", l)
        if turn:
            exchange(2 * (turn - 1), do_send, do_recv.at[turn - 1]).wait_send()
            exchange(2 * (turn - 1) + 1, dq_send, dq_recv.at[turn - 1]).wait_send()
        for buffer, c in ((do_send, not_ci), (do_own, ci)):
            at = pl.ds(pl.multiple_of(c * half, half), half)
            value = dot(dm_s[...], wp[at, :], 1, 1)
            buffer[...] = value.reshape(images, half_slots, half).astype(BF)
            if buffer is do_send:
                exchange(2 * turn, do_send, do_recv.at[turn]).start()
        arrive(turn, 2)
        rounds(turn, 2, of_first(0), 0)
        go(turn, 2)
        if turn + 1 < layers:
            begin(feed, l - 1)
        have("heads", l)
        exchange(2 * turn, do_send, do_recv.at[turn]).wait_recv()
        lane = lax.broadcasted_iota(jnp.int32, (2 * half_slots, 128), 1)
        factor = HEAD**-0.5

        def one_image(i, carry):
            step = turn * images + i
            slot = lax.rem(step, 2)
            following = lax.rem(i + 1, images)
            if turn + 1 < layers:
                load_bias(jnp.where(i + 1 < images, l, l - 1), following, 1 - slot).start()
            else:

                @pl.when(i + 1 < images)
                def _():
                    load_bias(l, i + 1, 1 - slot).start()

            if turn:
                store_ds(l, i, slot).wait()
            else:

                @pl.when(i >= 2)
                def _():
                    store_ds(l, i, slot).wait()

            load_bias(l, i, slot).wait()
            for pair in range(half // 128):
                at = pair * 128
                q, k, v = (
                    two_sides(
                        heads_s[0, i, :, w * half + at : w * half + at + 128],
                        heads_s[1, i, :, w * half + at : w * half + at + 128],
                    )
                    for w in range(3)
                )
                g = two_sides(do_own[i, :, at : at + 128], do_recv[turn, i, :, at : at + 128])
                dqs, dks, dvs = [], [], []
                for e in range(2):
                    own = (lane // HEAD) == e
                    qm = jnp.where(own, q, jnp.zeros_like(q))
                    gm = jnp.where(own, g, jnp.zeros_like(g))
                    s = dot(qm, k, 1, 1) * factor + bias_s[slot, 2 * pair + e]
                    ex = jnp.exp(s - jnp.max(s, axis=1, keepdims=True))
                    p = ex / jnp.sum(ex, axis=1, keepdims=True)
                    dp = dot(gm, v, 1, 1)
                    ds = (p * (dp - jnp.sum(p * dp, axis=1, keepdims=True))).astype(BF)
                    ds_s[slot, 2 * pair + e] = ds
                    dvs.append(dot(p.astype(BF), g, 0, 0))
                    dqs.append(dot(ds, k))
                    dks.append(dot(ds, q, 0, 0))
                low = lane < HEAD
                for w, (zero, one, scale) in enumerate(
                    ((dqs[0], dqs[1], factor), (dks[0], dks[1], factor), (dvs[0], dvs[1], 1.0))
                ):
                    value = jnp.where(low, zero, one) * scale
                    dq_own[i, :, w * half + at : w * half + at + 128] = value[:half_slots].astype(BF)
                    dq_send[i, :, w * half + at : w * half + at + 128] = value[half_slots:].astype(BF)
            store_ds(l, i, slot).start()

            @pl.when(i == 0)
            def _():
                hook(turn, "im0")

            @pl.when(i == images - 1)
            def _():
                hook(turn, "im2")

            return carry

        lax.fori_loop(0, images, one_image, 0)
        exchange(2 * turn + 1, dq_send, dq_recv.at[turn]).start()
        d_branch = dm_s[...].astype(F32)
        for w in range(3):
            at = pl.ds(pl.multiple_of(w * width + ci * half, half), half)
            dq_s[:, at] = dq_own[:, :, w * half : (w + 1) * half].astype(F32).reshape(rows, half).astype(BF)
        exchange(2 * turn + 1, dq_send, dq_recv.at[turn]).wait_recv()
        for w in range(3):
            at = pl.ds(pl.multiple_of(w * width + not_ci * half, half), half)
            dq_s[:, at] = (
                dq_recv[turn, :, :, w * half : (w + 1) * half].astype(F32).reshape(rows, half).astype(BF)
            )
        note(l, 2, dq_s[:, 0:width].astype(F32))
        note(l, 3, dq_s[:, 2 * width : 3 * width].astype(F32))
        three = 3 * block
        for x in range(2):
            sides = []
            for c in range(2):
                s = 2 * x + c
                low, top = s * three // 128 * 128, -(-(s + 1) * three // 128) * 128
                d_part = dq_s[:, low:top].astype(F32)[:, s * three - low : (s + 1) * three - low]
                sides.append(jnp.concatenate([d_part, d_branch[:, s * block : (s + 1) * block]], axis=1))
            dz_s[:, x * width : (x + 1) * width] = mine_first(sides[0], sides[1]).astype(BF)
            dz_s[:, (2 + x) * width : (3 + x) * width] = mine_first(sides[1], sides[0]).astype(BF)
        have("n", l)
        have("o", l)

        def of_attention(side):
            def product(x, h):
                at = pl.multiple_of((2 * side + x) * width + h * half, half)
                right = dz_s[:, pl.ds(at, half)]
                if h == 0:
                    return dot(n_s[...], right, 0, 0)
                column = lax.broadcasted_iota(jnp.int32, (width, half), 1)
                return jnp.where(column < block, dot(n_s[...], right, 0, 0), dot(o_s[...], right, 0, 0))

            return product

        rounds(turn, 4, of_attention(1), 1)
        give(turn, 4)
        have("wq", l)
        have("h", l)
        d_normed = jnp.concatenate(
            [dot(dq_s[...], wq[i * half : (i + 1) * half, :], 1, 1) for i in range(2)], axis=1
        )
        entering = norm_step(l, h_s[...], d_normed, g1_ref, 0)
        if l:
            e_s[...] = entering.astype(BF).astype(F32)
        else:
            dx_ref[...] = entering
        arrive(turn, 4)
        rounds(turn, 4, of_attention(0), 0)
        if turn + 1 < layers:
            begin(attend, l - 1)
        go(turn, 4)
    exchange(2 * layers - 2, do_send, do_recv.at[layers - 1]).wait_send()
    exchange(2 * layers - 1, dq_send, dq_recv.at[layers - 1]).wait_send()
    for back in range(min(2, images * layers)):
        step = layers * images - 1 - back
        store_ds(last - step // images, step % images, step % 2).wait()


def backward(upstream, saved, bias, vectors, images):
    rows, width = upstream.shape
    h_all, n_all, heads_all, o_all, r_all, h1_all, n2_all, u_all, slope_all, m_all = saved[:10]
    layers, half, half_slots = n_all.shape[0], width // 2, rows // images
    ff = u_all.shape[2]
    heads, slots, group = half // HEAD, 2 * half_slots, width // 8
    hbm, vm = pl.BlockSpec(memory_space=pl.ANY), pl.BlockSpec(memory_space=pltpu.VMEM)
    shape, v = jax.ShapeDtypeStruct, pltpu.VMEM
    scratch = [
        v((rows, width), F32), v((rows, width), BF), v((rows, width), BF), v((2, images, half_slots, 3 * half), BF),
        v((rows, width), BF), v((rows, width), F32), v((rows, width), BF), v((rows, width), BF), v((rows, ff), BF),
        v((2, rows, half), F32), v((rows, width), F32), v((width, 3 * width), BF), v((width, width), BF),
        v((width, ff), BF), v((ff, width), BF), v((2, heads, slots, slots), F32),
        v((rows, width), BF), v((2, rows, half), BF), v((rows, ff), BF), v((rows, 3 * width), BF),
        v((images, half_slots, half), BF), v((images, half_slots, half), BF),
        v((layers, images, half_slots, half), BF), v((images, half_slots, 3 * half), BF),
        v((images, half_slots, 3 * half), BF), v((layers, images, half_slots, 3 * half), BF),
        v((2, heads, slots, slots), BF),
        v((2, 2, 2, 2, 2, group, half), BF), v((6, 2, 2, 2, 2, group, half), BF), v((6, 2, 2, 2, group, half), BF),
        v((6, 2, 2, group, half), BF), v((6, 2, group, half), BF), v((6, group, half), BF),
        pltpu.SemaphoreType.DMA((layers * 32,)), pltpu.SemaphoreType.DMA((layers * 32,)),
        pltpu.SemaphoreType.DMA((14,)), pltpu.SemaphoreType.DMA((2,)), pltpu.SemaphoreType.DMA((2,)),
        pltpu.SemaphoreType.DMA((2,)),
        pltpu.SemaphoreType.REGULAR((6, 5)),
    ]
    return pl.pallas_call(
        backward_kernel,
        out_shape=[
            shape((rows, width), F32),
            shape((layers, 16, width), F32),
            shape((layers, 6, group, half), F32),
            shape((layers, images, heads, slots, slots), BF),
        ],
        in_specs=[vm] + [hbm] * 15 + [vm] * 4,
        out_specs=[vm, vm, vm, hbm],
        scratch_shapes=scratch,
        compiler_params=pltpu.CompilerParams(
            collective_id=1, has_side_effects=True, vmem_limit_bytes=60 * 2**20
        ),
    )(upstream, *saved, bias, *vectors)


def attn_bwd_kernel(qkv_ref, do_ref, bias_ref, dqkv_ref, ds_ref):
    width = do_ref.shape[2]
    slots = do_ref.shape[1]
    lane = lax.broadcasted_iota(jnp.int32, (slots, 128), 1)
    factor = HEAD**-0.5
    for pair in range(width // 128):
        at = pair * 128
        q, k, v = (qkv_ref[0, :, w * width + at : w * width + at + 128] for w in range(3))
        g = do_ref[0, :, at : at + 128]
        dqs, dks, dvs = [], [], []
        for e in range(2):
            own = (lane // HEAD) == e
            qm = jnp.where(own, q, jnp.zeros_like(q))
            gm = jnp.where(own, g, jnp.zeros_like(g))
            s = dot(qm, k, 1, 1) * factor + bias_ref[0, 2 * pair + e]
            ex = jnp.exp(s - jnp.max(s, axis=1, keepdims=True))
            p = ex / jnp.sum(ex, axis=1, keepdims=True)
            dp = dot(gm, v, 1, 1)
            ds = (p * (dp - jnp.sum(p * dp, axis=1, keepdims=True))).astype(BF)
            ds_ref[0, 2 * pair + e] = ds
            dvs.append(dot(p.astype(BF), g, 0, 0))
            dqs.append(dot(ds, k))
            dks.append(dot(ds, q, 0, 0))
        low = lane < HEAD
        for w, (zero, one, scale) in enumerate(
            ((dqs[0], dqs[1], factor), (dks[0], dks[1], factor), (dvs[0], dvs[1], 1.0))
        ):
            dqkv_ref[0, :, w * width + at : w * width + at + 128] = (
                jnp.where(low, zero, one) * scale
            ).astype(BF)


def attn_bwd(qkv, d_out, bias):
    images, slots, wide = qkv.shape
    width = wide // 3
    heads = width // HEAD
    one = lambda i: (i, 0, 0)
    return pl.pallas_call(
        attn_bwd_kernel,
        grid=(images,),
        in_specs=[
            pl.BlockSpec((1, slots, wide), one),
            pl.BlockSpec((1, slots, width), one),
            pl.BlockSpec((1, heads, slots, slots), lambda i: (i, 0, 0, 0)),
        ],
        out_specs=[
            pl.BlockSpec((1, slots, wide), one),
            pl.BlockSpec((1, heads, slots, slots), lambda i: (i, 0, 0, 0)),
        ],
        out_shape=[
            jax.ShapeDtypeStruct((images, slots, wide), BF),
            jax.ShapeDtypeStruct((images, heads, slots, slots), BF),
        ],
        compiler_params=pltpu.CompilerParams(vmem_limit_bytes=48 * 2**20),
    )(qkv, d_out, bias)


def norm_back(hidden, d_normed, gain):
    hidden = hidden.astype(F32)
    centered = hidden - jnp.mean(hidden, axis=1, keepdims=True)
    inv = lax.rsqrt(jnp.mean(centered * centered, axis=1, keepdims=True) + EPS)
    xhat = centered * inv
    dx = d_normed * gain
    mean_dx = jnp.mean(dx, axis=1, keepdims=True)
    mean_dxx = jnp.mean(dx * xhat, axis=1, keepdims=True)
    step = inv * (dx - mean_dx - xhat * mean_dxx)
    return step, jnp.sum(d_normed * xhat, axis=0), jnp.sum(d_normed, axis=0)


def backward_general(upstream, saved, bias, vectors, images):
    h_all, n_all, heads_all, o_all, r_all, h1_all, n2_all, u_all, slope_all, m_all = saved[:10]
    wq, wp, w1, w2 = saved[10:]
    gain1, scale_a, gain2, scale_m = vectors
    section, wide = lax.axis_index("section"), lax.axis_index("wide")
    xi, ci = section // 2, section % 2
    wide_count = lax.axis_size("wide")
    layers = n_all.shape[0]
    rows, width = upstream.shape
    half, half_slots = width // 2, rows // images
    heads = half // HEAD

    def to_heads(value):
        keep = pick(ci, value[:, :half], value[:, half:])
        got = swap(pick(ci, value[:, half:], value[:, :half]), "section", 1)
        shape = (images, half_slots, half)
        return jnp.concatenate([keep.reshape(shape), got.reshape(shape)], axis=1)

    def from_heads(value):
        keep = value[:, :half_slots].reshape(rows, 3 * half)
        got = swap(value[:, half_slots:], "section", 1).reshape(rows, 3 * half)
        pieces = []
        for b in range(3):
            a, o = keep[:, b * half : (b + 1) * half], got[:, b * half : (b + 1) * half]
            pieces += [pick(ci, a, o), pick(ci, o, a)]
        return jnp.concatenate(pieces, axis=1)

    def columns(value, x, c):
        size = value.shape[1] // 4
        return value[:, (2 * x + c) * size : (2 * x + c + 1) * size]

    def add(a, b):
        return (a.astype(F32) + b.astype(F32)).astype(BF)

    def core_sum(left, right):
        own = [pick(ci, columns(right, x, 0), columns(right, x, 1)) for x in range(2)]
        other = [pick(ci, columns(right, x, 1), columns(right, x, 0)) for x in range(2)]
        got = swap(dot(left, jnp.concatenate(other, axis=1), 0, 0).astype(BF), "section", 1)
        return (dot(left, jnp.concatenate(own, axis=1), 0, 0) + got.astype(F32)).astype(BF)

    def x_step(value):
        size = value.shape[1] // 2
        low, top = value[:, :size], value[:, size:]
        return add(pick(xi, low, top), swap(pick(xi, top, low), "section", 2))

    def wide_steps(value):
        group = value.shape[0] // wide_count
        bit = 1
        while bit < wide_count:
            left = wide_count // bit
            cut = value.reshape(left // 2, 2, group, value.shape[-1])
            flag = (wide // bit) % 2
            keep = lax.dynamic_index_in_dim(cut, flag, 1, keepdims=False)
            send = lax.dynamic_index_in_dim(cut, 1 - flag, 1, keepdims=False)
            value = add(keep, swap(send, "wide", bit))
            bit *= 2
        return value.reshape(group, value.shape[-1])

    def x_first(left, right):
        return wide_steps(x_step(core_sum(left, right))).astype(F32)

    def wide_first(left, right):
        return x_step(wide_steps(core_sum(left, right))).astype(F32)

    small, matrices, d_scores = [None] * layers, [None] * layers, [None] * layers
    for l in reversed(range(layers)):
        up = upstream.astype(F32)
        d_mlp_scale = jnp.sum(up * m_all[l], axis=0)
        d_branch = (scale_m[l : l + 1] * up).astype(BF)
        d_fc2_b = jnp.sum(d_branch.astype(F32), axis=0)
        d_fc2 = wide_first(u_all[l], d_branch)
        d_pre = (dot(d_branch, w2[l], 1, 1) * slope_all[l]).astype(BF)
        d_fc1_b = jnp.sum(d_pre.astype(F32), axis=0).reshape(-1, width)
        d_fc1 = x_first(n2_all[l], d_pre)
        step, d_gain2, d_offset2 = norm_back(h1_all[l], dot(d_pre, w1[l], 1, 1), gain2[l : l + 1])
        up = (up + step).astype(BF).astype(F32)
        d_attn_scale = jnp.sum(up * r_all[l], axis=0)
        d_branch = (scale_a[l : l + 1] * up).astype(BF)
        d_proj_b = jnp.sum(d_branch.astype(F32), axis=0)
        d_proj = x_first(o_all[l], d_branch)
        d_mixed = to_heads(dot(d_branch, wp[l], 1, 1).astype(BF))
        qkv = jnp.concatenate([heads_all[l, 0], heads_all[l, 1]], axis=1)
        d_heads, d_scores[l] = attn_bwd(qkv, d_mixed, bias[:, l * heads : (l + 1) * heads])
        d_qkv = from_heads(d_heads)
        d_qkv_w = x_first(n_all[l], d_qkv)
        d_qkv_b = jnp.sum(d_qkv.astype(F32), axis=0)
        step, d_gain1, d_offset1 = norm_back(h_all[l], dot(d_qkv, wq[l], 1, 1), gain1[l : l + 1])
        entering = up + step
        upstream = entering.astype(BF)
        one = [d_gain1, d_offset1, d_qkv_b[:width], d_qkv_b[2 * width :], d_proj_b, d_attn_scale]
        one += [d_gain2, d_offset2, d_fc2_b, d_mlp_scale]
        one = jnp.concatenate([jnp.stack(one), d_fc1_b])
        small[l] = jnp.pad(one, ((0, 16 - one.shape[0]), (0, 0)))
        matrices[l] = (d_qkv_w, d_proj, d_fc1, d_fc2)
    matrices = [jnp.stack(group) for group in zip(*matrices)]
    return entering, jnp.stack(small), matrices, jnp.stack(d_scores)


def matrix_blocks(d_matrix):
    layers, unused, group, half = d_matrix.shape
    width, block = 2 * half, half // 2
    second = d_matrix[:, 0:2].reshape(layers, block, half).transpose(0, 2, 1)
    first = d_matrix[:, 2:4].transpose(0, 2, 1, 3).reshape(layers, group, width)
    attend = d_matrix[:, 4:6].transpose(0, 2, 1, 3).reshape(layers, group, width)
    return attend[:, :, : 3 * block], attend[:, :, 3 * block :], first, second


def shards(
    tokens,
    cotangent,
    shape_id,
    rel_index,
    norm1_gain,
    norm1_bias,
    qkv_weight,
    q_bias,
    v_bias,
    proj_weight,
    proj_bias,
    attn_scale,
    rel_table,
    norm2_gain,
    norm2_bias,
    fc1_weight,
    fc1_bias,
    fc2_weight,
    fc2_bias,
    mlp_scale,
):
    section = lax.axis_index("section")
    wide = lax.axis_index("wide")
    xi, ci, yi = section // 2, section % 2, wide % 2
    wide_count = lax.axis_size("wide")
    layers = qkv_weight.shape[0]
    images, part, width = tokens.shape
    slots = part * 4
    mine = images // 2
    rows = mine * 2 * part
    half = width // 2
    ff = fc1_weight.shape[2]

    def to_images(value):
        cut = value.reshape(2, mine, part, width)
        keep = lax.dynamic_index_in_dim(cut, xi, 0, keepdims=False)
        got = swap(lax.dynamic_index_in_dim(cut, 1 - xi, 0, keepdims=False), "section", 2)
        both = jnp.concatenate([pick(xi, keep, got), pick(xi, got, keep)], axis=1)
        return both.reshape(rows, width)

    def to_slots(value):
        cut = value.reshape(mine, 2, part, width)
        keep = lax.dynamic_index_in_dim(cut, xi, 1, keepdims=False)
        got = swap(lax.dynamic_index_in_dim(cut, 1 - xi, 1, keepdims=False), "section", 2)
        return jnp.concatenate([pick(xi, keep, got), pick(xi, got, keep)], axis=0)

    hidden = to_images(tokens)
    whole_cot = to_images(cotangent)
    shapes = lax.dynamic_slice_in_dim(shape_id, xi * mine, mine, 0)

    targets, indices, sources, slot_of = bias_inputs(rel_index, ci, slots, part)
    counts = [r * c + 1 for r, c in GRIDS]
    heads = rel_table.shape[2]
    entries = rel_table.shape[1]
    mine_heads = heads // 2
    core_arg = jnp.reshape(ci, (1,)).astype(jnp.int32)
    table = pick(ci, rel_table[:, :, :mine_heads], rel_table[:, :, mine_heads:])
    table_rows = jnp.transpose(table, (0, 2, 1)).reshape(layers * mine_heads, entries)
    table_rows = jnp.pad(table_rows, ((0, 16 - layers * mine_heads), (0, 0)))
    bias_all = build_bias(
        core_arg, table_rows, targets, indices, sources, layers * mine_heads, part
    )
    bias_images = jnp.stack(
        [lax.dynamic_index_in_dim(bias_all, shapes[i], 0, keepdims=False) for i in range(mine)]
    )

    def f32_row(vector, l):
        return vector[l].astype(F32)[None, :]

    zero_k = jnp.zeros_like(q_bias)
    vectors = (
        norm1_gain, norm1_bias, jnp.concatenate([q_bias, zero_k, v_bias], axis=1), proj_bias,
        attn_scale, norm2_gain, norm2_bias, fc1_bias, fc2_bias, mlp_scale,
    )
    vectors = [v.astype(F32) for v in vectors]
    owns = (qkv_weight, proj_weight, fc1_weight, fc2_weight)
    hidden, *saved = forward(hidden, owns, bias_images, vectors, mine)
    out = to_slots(hidden)

    def all_sum(value):
        for bit in (1, 2):
            value = value + swap(value, "section", bit)
        bit = 1
        while bit < wide_count:
            value = value + swap(value, "wide", bit)
            bit *= 2
        return value

    counts_of = sum(jnp.where(shapes == s, n, 0) for s, n in enumerate(counts))
    live = slot_of[None, : 2 * part] < counts_of[:, None]
    upstream = jnp.where(live.reshape(rows, 1), whole_cot, jnp.zeros((), BF))

    scales = (vectors[0], vectors[4], vectors[5], vectors[9])
    if layers == 2 and wide_count == 8 and rows <= 320:
        d_entering, d_small, d_matrix, d_scores = backward(upstream, saved, bias_images, scales, mine)
        d_matrix = matrix_blocks(d_matrix)
    else:
        d_entering, d_small, d_matrix, d_scores = backward_general(
            upstream, saved, bias_images, scales, mine
        )
    d_tokens = to_slots(d_entering.astype(BF)).astype(F32)
    d_small = all_sum(d_small.reshape(layers * 16, width))
    d_small = d_small.reshape(layers, 16, width)
    d_table = table_grad(core_arg, shapes, d_scores, targets, indices, sources, entries, part)
    d_table = d_table[: layers * mine_heads].reshape(layers, mine_heads, entries)
    empty = jnp.zeros_like(d_table)
    d_table = jnp.concatenate([pick(ci, d_table, empty), pick(ci, empty, d_table)], axis=1)
    d_table = all_sum(d_table.reshape(layers * heads, entries)).reshape(layers, heads, entries)

    def row(at):
        return d_small[:, at]

    return (
        out,
        d_tokens,
        row(0),
        row(1),
        d_matrix[0],
        row(2),
        row(3),
        d_matrix[1],
        row(4),
        row(5),
        d_table.transpose(0, 2, 1),
        row(6),
        row(7),
        d_matrix[2],
        d_small[:, 10:14].reshape(layers, ff),
        d_matrix[3],
        row(8),
        row(9),
    )


def solution(mesh):
    return jax.shard_map(
        shards,
        mesh=mesh,
        in_specs=(
            P("wide", "section", None),
            P("wide", "section", None),
            P("wide"),
            P(),
            P(),
            P(),
            P(None, "section", None),
            P(),
            P(),
            P(None, "section", None),
            P(),
            P(),
            P(),
            P(),
            P(),
            P(None, "section", None),
            P(),
            P(None, "section", None),
            P(),
            P(),
        ),
        out_specs=(
            P("wide", "section", None),
            P("wide", "section", None),
            P(),
            P(),
            P(None, "wide", "section"),
            P(),
            P(),
            P(None, "wide", "section"),
            P(),
            P(),
            P(),
            P(),
            P(),
            P(None, "wide", "section"),
            P(),
            P(None, "wide", "section"),
            P(),
            P(),
        ),
        check_vma=False,
    )
```

```python
import functools

import numpy as np
import jax
import jax.numpy as jnp
from jax import lax
from jax.experimental import pallas as pl
from jax.experimental.pallas import tpu as pltpu
from jax.sharding import PartitionSpec as P

GRIDS = ((14, 14), (10, 20), (8, 24))
EPS = 1e-06
DEAD = -1e30
ROOT_HALF = 0.7071067811865476
INV_ROOT_2PI = 0.3989422804014327
HEAD = 64
BF = jnp.bfloat16
F32 = jnp.float32


def swap(value, axis, bit):
    count = lax.axis_size(axis)
    return lax.ppermute(value, axis, [(i, i ^ bit) for i in range(count)])


def pick(flag, zero, one):
    return jnp.where(flag == 0, zero, one)


def dot(a, b, ca=1, cb=0, **kw):
    return lax.dot_general(a, b, (((ca,), (cb,)), ((), ())), preferred_element_type=F32, **kw)


LANES = 768

def up8(n): return -(-n//8)*8

def offset_sources(rows, cols, slots):
    pitch, span = 2 * cols - 1, 2 * rows - 1
    source = np.full((1, LANES), -1, np.int32)
    for j in range(span):
        r, rk = (0, j - (rows - 1)) if j >= rows - 1 else (rows - 1, j)
        for t in range(pitch):
            c, ck = (0, t - (cols - 1)) if t >= cols - 1 else (cols - 1, t)
            which = 1 + (1 if r else 0) * 2 + (1 if c else 0)
            source[0, j * pitch + t] = which * slots + 1 + rk * cols + ck
    length = pitch * span
    source[0, length : length + 4] = (0, 1, slots, slots - 1)
    return source

def key_targets(rows, cols, slots):
    pitch, length = 2 * cols - 1, (2 * cols - 1) * (2 * rows - 1)
    out = np.zeros((3, slots), np.int32)
    for k in range(slots):
        if k == 0:
            out[:, k] = length + 2, 0, length
        elif k <= rows * cols:
            rk, ck = divmod(k - 1, cols)
            out[:, k] = (rows - 1 + rk) * pitch + ck, pitch, length + 1
        else:
            out[:, k] = length + 3, 0, length + 3
    return out

def lane_onehot(target, dtype):
    n = target.shape[1]
    number = lax.broadcasted_iota(jnp.int32, (LANES, n), 0)
    return jnp.where(number == target, 1.0, 0.0).astype(dtype)

def block_order(core):
    return (0, 2, 1, 3) if core == 0 else (1, 3, 0, 2)

def bias_constants(slots, part):
    sources = np.concatenate([offset_sources(r, c, slots) for r, c in GRIDS])
    natural = np.stack([key_targets(r, c, slots) for r, c in GRIDS]).reshape(3, 3, 4, part)
    targets = np.stack([natural[:, :, list(block_order(c))].reshape(3, 3, slots) for c in range(2)])
    return jnp.asarray(sources), jnp.asarray(targets)


def make_bias(part, ci, table_ref, idx_ref, src_ref, tgt_ref, out_ref, nat_ref, wide_ref):
    layers, entries, all_heads = table_ref.shape
    own = all_heads // 2
    heads, slots = out_ref.shape[1:3]
    for s, (rows, cols) in enumerate(GRIDS):
        length = (2 * cols - 1) * (2 * rows - 1)
        step = up8(cols)
        count = rows * cols + 1
        pairs = idx_ref.shape[1]
        target = jnp.where(ci == 0, tgt_ref[0, s], tgt_ref[1, s])
        number = lax.broadcasted_iota(jnp.int32, (entries, pairs), 0)
        hot = jnp.where(number == idx_ref[s : s + 1, :], 1.0, 0.0).astype(BF)
        looked = []
        for l in range(layers):
            both = dot(table_ref[l], hot, 0, 0)
            looked.append(jnp.where(ci == 0, both[:own], both[own:]))
        looked = jnp.concatenate(looked + [jnp.zeros((16 - heads, pairs), F32)], axis=0).astype(BF)
        place = lax.broadcasted_iota(jnp.int32, (pairs, LANES), 0)
        hot = jnp.where(place == src_ref[s : s + 1, :], 1.0, 0.0).astype(BF)
        offsets = dot(looked, hot)
        turned = pltpu.roll(offsets, LANES - (cols - 1), 1)
        tail = lax.broadcasted_iota(jnp.int32, (step, LANES), 1) >= length
        for h in range(heads):
            row = jnp.broadcast_to(offsets[h : h + 1], (step, LANES))
            rolled = jnp.broadcast_to(turned[h : h + 1], (step, LANES))
            rolled = pltpu.roll(rolled, 0, 1, stride=1, stride_axis=0)
            wide_ref[h * step : (h + 1) * step, :] = jnp.where(tail, row, rolled)
        shifted = wide_ref[0 : heads * step, :].astype(BF)
        for r in range(rows):
            patch = dot(shifted, lane_onehot(target[0:1] - r * target[1:2], BF))
            for h in range(heads):
                nat_ref[h, 1 + r * cols : 1 + (r + 1) * cols, :] = patch[h * step : h * step + cols]
        first = dot(offsets.astype(BF), lane_onehot(target[2:3], BF))
        live = jnp.broadcast_to(target[2:3] < length + 2, (part, slots))
        for h in range(heads):
            nat_ref[h, 0:1, :] = first[h : h + 1]
            nat_ref[h, count:, :] = jnp.broadcast_to(
                offsets[h : h + 1, length + 3 : length + 4], (slots - count, slots)
            )
        for core in range(2):

            @pl.when(ci == core)
            def _(core=core):
                for h in range(heads):
                    for j, b in enumerate(block_order(core)):
                        block = nat_ref[h, b * part : (b + 1) * part, :]
                        out_ref[s, h, j * part : (j + 1) * part, :] = jnp.where(live, block, DEAD)


def exact_dot(value, hot, ca, cb):
    high = value.astype(BF)
    rest = value - high.astype(F32)
    middle = rest.astype(BF)
    low = (rest - middle.astype(F32)).astype(BF)
    n = value.shape[0]
    out = dot(jnp.concatenate([high, middle, low], axis=0), hot, ca, cb)
    return out[:n] + (out[n : 2 * n] + out[2 * n :])


def fold_scores(s, part, ci, read, tgt_ref, heads, nat_ref, acc_ref, row_ref):
    rows, cols = GRIDS[s]
    slots = 4 * part
    length = (2 * cols - 1) * (2 * rows - 1)
    step = up8(cols)
    count = rows * cols + 1
    target = jnp.where(ci == 0, tgt_ref[0, s], tgt_ref[1, s])

    def stack(pieces):
        return jnp.concatenate(pieces + [jnp.zeros((16 - heads,) + pieces[0].shape[1:], F32)], axis=0)

    for core in range(2):

        @pl.when(ci == core)
        def _(core=core):
            for h in range(heads):
                value = read(h)
                for j, b in enumerate(block_order(core)):
                    nat_ref[h, b * part : (b + 1) * part, :] = value[j * part : (j + 1) * part]

    acc_ref[0 : heads * step, :] = jnp.zeros((heads * step, LANES), F32)
    row_ref[0 : heads * step, 0:slots] = jnp.zeros((heads * step, slots), F32)
    for r in range(rows):
        for h in range(heads):
            row_ref[h * step : h * step + cols, 0:slots] = nat_ref[h, 1 + r * cols : 1 + (r + 1) * cols, :]
        hot = lane_onehot(target[0:1] - r * target[1:2], BF)
        acc_ref[0 : heads * step, :] += dot(row_ref[0 : heads * step, 0:slots].astype(BF), hot, 1, 1)
    lane = lax.broadcasted_iota(jnp.int32, (16, LANES), 1)
    offsets = jnp.zeros((16, LANES), F32)
    for c in range(cols):
        part_c = stack([acc_ref[h * step + c : h * step + c + 1, :] for h in range(heads)])
        back = pltpu.roll(part_c, cols - 1 - c, 1)
        offsets += jnp.where(lane >= length, part_c, back)
    first = stack([nat_ref[h, 0:1, :] for h in range(heads)])
    offsets += exact_dot(first, lane_onehot(target[2:3], BF), 1, 1)
    rest = stack(
        [
            jnp.sum(jnp.sum(nat_ref[h, count:, :], axis=0, keepdims=True), axis=1, keepdims=True)
            for h in range(heads)
        ]
    )
    return offsets + jnp.where(lane == length + 3, rest, 0.0)


def table_rows(offsets, idx_ref, src_ref, entries):
    total = None
    pairs = idx_ref.shape[1]
    for s in range(len(GRIDS)):
        place = lax.broadcasted_iota(jnp.int32, (pairs, LANES), 0)
        hot = jnp.where(place == src_ref[s : s + 1, :], 1.0, 0.0).astype(BF)
        looked = exact_dot(offsets[s], hot, 1, 1)
        number = lax.broadcasted_iota(jnp.int32, (entries, pairs), 0)
        hot = jnp.where(number == idx_ref[s : s + 1, :], 1.0, 0.0).astype(BF)
        value = exact_dot(looked, hot, 1, 1)
        total = value if total is None else total + value
    return total


VM = pl.BlockSpec(memory_space=pltpu.VMEM)
SM = pl.BlockSpec(memory_space=pltpu.SMEM)


MESH = pl.DeviceIdType.MESH


def ids():
    section, wide = lax.axis_index("section"), lax.axis_index("wide")
    ci, yi = lax.rem(section, 2), lax.rem(wide, 2)
    core = {"section": section + 1 - 2 * ci}
    across = {"section": lax.rem(section + 2, 4)}
    beside = {"wide": wide + 1 - 2 * yi}
    return section, ci, yi, core, across, beside


def greet(partners):
    barrier = pltpu.get_barrier_semaphore()
    for device in partners:
        pl.semaphore_signal(barrier, inc=1, device_id=device, device_id_type=MESH)
    pl.semaphore_wait(barrier, len(partners))


class Remote:
    def __init__(self, send, recv):
        self.send, self.recv, self.used, self.open = send, recv, 0, []

    def start(self, src, dst, device):
        copy = pltpu.make_async_remote_copy(
            src_ref=src, dst_ref=dst, send_sem=self.send.at[self.used],
            recv_sem=self.recv.at[self.used], device_id=device, device_id_type=MESH,
        )
        self.used += 1
        copy.start()
        self.open.append(copy)
        return copy

    def sent(self, copy):
        if any(copy is other for other in self.open):
            copy.wait_send()
            self.open = [other for other in self.open if other is not copy]

    def finish(self):
        for copy in self.open:
            copy.wait_send()
        self.open = []


class Local:
    def __init__(self, sems):
        self.sems, self.used, self.open = sems, 0, {}

    def start(self, src, dst, name=None):
        copy = pltpu.make_async_copy(src, dst, self.sems.at[self.used])
        self.open[name if name is not None else self.used] = copy
        self.used += 1
        copy.start()

    def wait(self, name):
        if name in self.open:
            self.open.pop(name).wait()

    def finish(self):
        for name in list(self.open):
            self.wait(name)


CHUNKS = (("q", 0, 1152), ("q", 1152, 1152), ("p", 0, 768), ("1", 0, 1536), ("1", 1536, 1536), ("2", 0, 384), ("2", 384, 384))
AHEAD = 2


class Gather:
    def __init__(self, where, own, whole, remote, local, layers):
        section, self.ci, self.yi, self.core, self.across, self.beside = where
        self.own, self.whole, self.remote, self.local = own, whole, remote, local
        self.section = section
        self.far = lax.rem(section + 2, 4)
        self.chunks = [(l,) + chunk for l in range(layers) for chunk in CHUNKS]
        self.state = [dict() for unused in self.chunks]
        self.a_next, self.b_next, self.ready = 0, 0, 0
        for k in range(AHEAD):
            self.begin(k)

    def rows(self, name, shard, half=None):
        depth = self.own[name].shape[1]
        if half is None:
            return pl.ds(pl.multiple_of(shard * depth, depth), depth)
        cut = depth // 2
        return pl.ds(pl.multiple_of(shard * depth + half * cut, cut), cut)

    def begin(self, k):
        if k >= len(self.chunks):
            return
        l, name, at, size = self.chunks[k]
        own, whole = self.own[name], self.whole[name]
        depth = own.shape[1]
        cols = pl.ds(at, size)
        state = self.state[k]
        half = pl.ds(pl.multiple_of(self.yi * (depth // 2), depth // 2), depth // 2)
        state["x"] = self.remote.start(
            own.at[l, half, cols], whole.at[l, self.rows(name, self.section, self.yi), cols], self.across
        )
        place = whole.at[l, self.rows(name, self.section), cols]
        state["c"] = self.remote.start(own.at[l, :, cols], place, self.core)
        self.local.start(own.at[l, :, cols], place, ("own", k))

    def pass_on(self, k, half, device):
        l, name, at, size = self.chunks[k]
        block = self.whole[name].at[l, self.rows(name, self.far, half), pl.ds(at, size)]
        return self.remote.start(block, block, device)

    def step_a(self):
        k = self.a_next
        if k >= len(self.chunks):
            return
        state = self.state[k]
        state["x"].wait_recv()
        state["y"] = self.pass_on(k, self.yi, self.beside)
        state["cx"] = self.pass_on(k, self.yi, self.core)
        self.begin(k + AHEAD)
        self.a_next += 1

    def step_b(self):
        k = self.b_next
        state = self.state[k]
        state["y"].wait_recv()
        state["cy"] = self.pass_on(k, 1 - self.yi, self.core)
        self.b_next += 1

    def need(self, count):
        while self.ready < count:
            k = self.ready
            while self.a_next < k + 2 and self.a_next < len(self.chunks):
                self.step_a()
            while self.b_next < k + 1:
                self.step_b()
            state = self.state[k]
            self.local.wait(("own", k))
            for key in ("c", "cx", "cy"):
                state[key].wait_recv()
            self.ready += 1


def rows_norm(value):
    centered = value - jnp.mean(value, axis=1, keepdims=True)
    return centered * lax.rsqrt(jnp.mean(centered * centered, axis=1, keepdims=True) + EPS)


def two_sides(left, right):
    return jnp.concatenate([left.astype(F32), right.astype(F32)], axis=0).astype(BF)


def forward_kernel(
    shape_ref, tokens_ref, cot_ref, q_own, p_own, f1_own, f2_own, table_ref, idx_ref, src_ref, tgt_ref,
    g1_ref, b1_ref, qb_ref, vb_ref, pb_ref, as_ref, g2_ref, b2_ref, fb_ref, mb_ref, ms_ref,
    out_ref, e_ref, bias_out, h_out, n_out, heads_out, o_out, r_out, h1_out, n2_out, u_out, slope_out, m_out,
    q_out, p_out, f1_out, f2_out,
    wq, wp, w1, w2, h_s, n_s, o_s, r_s, h1_s, n2_s, u_s, slope_s, m_s,
    own_s, send_s, recv_s, om_s, os_s, or_s, bias_s, nat_s, tok_s, cot_s,
    send_sems, recv_sems, local_sems, slope_sems,
):
    layers = q_own.shape[0]
    images, half_slots = own_s.shape[0], own_s.shape[1]
    rows, width = h_s.shape
    half = width // 2
    heads = half // HEAD
    ff = u_s.shape[1]
    part = half_slots // 2
    tile = half
    where = ids()
    section, ci, yi, core, across, beside = where
    greet((core, across, beside))
    remote, local = Remote(send_sems, recv_sems), Local(local_sems)
    xi = section // 2
    ours, others = pl.ds(xi * images, images), pl.ds((1 - xi) * images, images)
    tokens_sent = remote.start(tokens_ref.at[others], tok_s.at[xi], across)
    local.start(tokens_ref.at[ours], tok_s.at[xi], "tokens")
    local.start(cot_ref.at[ours], cot_s.at[xi], "cot")
    whole = {"q": wq, "p": wp, "1": w1, "2": w2}
    gather = Gather(
        where, {"q": q_own, "p": p_own, "1": f1_own, "2": f2_own}, whole, remote, local, layers
    )

    def vec(ref, l, at=slice(None)):
        return ref[:, at].astype(F32)[l : l + 1]

    def join(blocks):
        return jnp.concatenate([blocks[x, i].astype(F32) for i in range(images) for x in range(2)], axis=0)

    make_bias(part, ci, table_ref, idx_ref, src_ref, tgt_ref, bias_s, nat_s, r_s)
    local.start(bias_s, bias_out)
    local.wait("tokens")
    tokens_sent.wait_recv()
    h_s[...] = join(tok_s).astype(BF)
    lane = lax.broadcasted_iota(jnp.int32, (2 * half_slots, 128), 1)
    for l in range(layers):
        first = l * len(CHUNKS)
        hidden = h_s[...].astype(F32)
        local.start(h_s, h_out.at[l], "h")
        local.wait("n")
        n_s[...] = (rows_norm(hidden) * vec(g1_ref, l) + vec(b1_ref, l)).astype(BF)
        local.start(n_s, n_out.at[l], "n")
        gather.need(first + 2)
        local.start(wq.at[l], q_out.at[l], ("w", "q", l))
        if l:
            remote.sent(pending)
            local.wait("own")
        for side, buffer in ((1, send_s), (0, own_s)):
            for which in range(3):
                at = pl.multiple_of(which * width + lax.rem(ci + side, 2) * half, half)
                value = dot(n_s[...], wq[l, :, pl.ds(at, half)])
                if which != 1:
                    at = pl.multiple_of(lax.rem(ci + side, 2) * half, half)
                    value = value + vec(qb_ref if which == 0 else vb_ref, l, pl.ds(at, half))
                buffer[:, :, which * half : (which + 1) * half] = value.reshape(
                    images, half_slots, half
                ).astype(BF)
            if side:
                pending = remote.start(send_s, recv_s.at[l], core)
        local.start(own_s, heads_out.at[l, 0], "own")
        pending.wait_recv()
        local.start(recv_s.at[l], heads_out.at[l, 1])
        if l:
            remote.sent(o_pending)

        def one_image(i, carry):
            shape = shape_ref[xi * images + i]
            for pair in range(half // 128):
                q, k, v = (
                    two_sides(
                        own_s[i, :, w * half + pair * 128 : w * half + pair * 128 + 128],
                        recv_s[l, i, :, w * half + pair * 128 : w * half + pair * 128 + 128],
                    )
                    for w in range(3)
                )
                outs = []
                for e in range(2):
                    qm = jnp.where((lane // HEAD) == e, q, jnp.zeros_like(q))
                    s = dot(qm, k, 1, 1) * HEAD**-0.5 + bias_s[shape, l * heads + 2 * pair + e]
                    ex = jnp.exp(s - jnp.max(s, axis=1, keepdims=True))
                    p = ex / jnp.sum(ex, axis=1, keepdims=True)
                    outs.append(dot(p.astype(BF), v))
                mixed = jnp.where(lane < HEAD, outs[0], outs[1])
                om_s[i, :, pair * 128 : pair * 128 + 128] = mixed[:half_slots].astype(BF)
                os_s[i, :, pair * 128 : pair * 128 + 128] = mixed[half_slots:].astype(BF)
            return carry

        lax.fori_loop(0, images, one_image, 0)
        o_pending = remote.start(os_s, or_s.at[l], core)
        local.wait("o")
        mine = pl.ds(pl.multiple_of(ci * half, half), half)
        other = pl.ds(pl.multiple_of((1 - ci) * half, half), half)
        o_s[:, mine] = om_s[...].astype(F32).reshape(rows, half).astype(BF)
        gather.need(first + 3)
        local.start(wp.at[l], p_out.at[l], ("w", "p", l))
        o_pending.wait_recv()
        o_s[:, other] = or_s[l].astype(F32).reshape(rows, half).astype(BF)
        local.start(o_s, o_out.at[l], "o")
        branch = dot(o_s[...], wp[l]) + vec(pb_ref, l)
        local.wait("r")
        r_s[...] = branch
        local.start(r_s, r_out.at[l], "r")
        local.wait("h1")
        h1_s[...] = (hidden + vec(as_ref, l) * branch).astype(BF)
        local.start(h1_s, h1_out.at[l], "h1")
        local.wait("n2")
        n2_s[...] = (
            rows_norm(h1_s[...].astype(F32)) * vec(g2_ref, l) + vec(b2_ref, l)
        ).astype(BF)
        local.start(n2_s, n2_out.at[l], "n2")
        local.wait("u")

        def store_slope(t):
            at = pl.ds(pl.multiple_of(t * tile, tile), tile)
            slot = lax.rem(t, 2)
            return pltpu.make_async_copy(slope_s.at[slot], slope_out.at[l, :, at], slope_sems.at[slot])

        for piece in range(2):
            gather.need(first + 4 + piece)

            def one_tile(t, carry):
                at = pl.ds(pl.multiple_of(t * tile, tile), tile)
                pre = dot(n2_s[...], w1[l, :, at]) + vec(fb_ref, l, at)
                cdf = 0.5 * (1.0 + lax.erf(pre * ROOT_HALF))
                u_s[:, at] = (pre * cdf).astype(BF)

                @pl.when(t >= 2)
                def _():
                    store_slope(t).wait()

                slope_s[lax.rem(t, 2)] = cdf + pre * jnp.exp(-0.5 * pre * pre) * INV_ROOT_2PI
                store_slope(t).start()
                return carry

            count = ff // tile // 2
            lax.fori_loop(piece * count, (piece + 1) * count, one_tile, 0)
        local.start(w1.at[l], f1_out.at[l], ("w", "1", l))
        local.start(u_s, u_out.at[l], "u")
        for t in (ff // tile - 2, ff // tile - 1):
            store_slope(t).wait()
        local.wait("m")
        local.wait("h")
        for piece in range(2):
            gather.need(first + 6 + piece)
            if l == layers - 1 and piece == 0:
                cot_sent = remote.start(cot_ref.at[others], cot_s.at[xi], across)
            at = slice(piece * half, (piece + 1) * half)
            branch = dot(u_s[...], w2[l, :, at]) + vec(mb_ref, l, at)
            m_s[:, at] = branch
            h_s[:, at] = (h1_s[:, at].astype(F32) + vec(ms_ref, l, at) * branch).astype(BF)
        local.start(w2.at[l], f2_out.at[l], ("w", "2", l))
        local.start(m_s, m_out.at[l], "m")
    final = h_s[...].astype(F32)
    place = lax.broadcasted_iota(jnp.int32, (half_slots, width), 0)
    slot = place + ci * part + jnp.where(place >= part, part, 0)
    local.wait("cot")
    cot_sent.wait_recv()
    upstream = join(cot_s)
    for i in range(images):
        shape = shape_ref[xi * images + i]
        count = sum(jnp.where(shape == s, r * c + 1, 0) for s, (r, c) in enumerate(GRIDS))
        at = i * half_slots
        for x in range(2):
            out_ref[x, i] = final[at + x * part : at + (x + 1) * part].astype(BF)
        e_ref[at : at + half_slots, :] = jnp.where(slot < count, upstream[at : at + half_slots], 0.0)
    remote.finish()
    local.finish()


def forward(shape_id, tokens, cotangent, owns, table, index, vectors):
    all_images, part, width = tokens.shape
    images = all_images // 2
    rows = images * 2 * part
    layers = owns[0].shape[0]
    half = width // 2
    half_slots = 2 * part
    slots = 2 * half_slots
    ff = owns[2].shape[2]
    heads = half // HEAD
    hbm, vm = pl.BlockSpec(memory_space=pl.ANY), pl.BlockSpec(memory_space=pltpu.VMEM)
    shape = jax.ShapeDtypeStruct
    sources, targets = bias_constants(slots, part)
    outs = [
        shape((2, images, part, width), BF),
        shape((rows, width), F32),
        shape((len(GRIDS), layers * heads, slots, slots), F32),
        shape((layers, rows, width), BF),
        shape((layers, rows, width), BF),
        shape((layers, 2, images, half_slots, 3 * half), BF),
        shape((layers, rows, width), BF),
        shape((layers, rows, width), F32),
        shape((layers, rows, width), BF),
        shape((layers, rows, width), BF),
        shape((layers, rows, ff), BF),
        shape((layers, rows, ff), F32),
        shape((layers, rows, width), F32),
        shape((layers, width, 3 * width), BF),
        shape((layers, width, width), BF),
        shape((layers, width, ff), BF),
        shape((layers, ff, width), BF),
    ]
    chunks = layers * len(CHUNKS)
    remote_count = chunks * 5 + 2 * layers + 2
    scratch = [
        pltpu.VMEM((layers, width, 3 * width), BF),
        pltpu.VMEM((layers, width, width), BF),
        pltpu.VMEM((layers, width, ff), BF),
        pltpu.VMEM((layers, ff, width), BF),
        pltpu.VMEM((rows, width), BF),
        pltpu.VMEM((rows, width), BF),
        pltpu.VMEM((rows, width), BF),
        pltpu.VMEM((rows, width), F32),
        pltpu.VMEM((rows, width), BF),
        pltpu.VMEM((rows, width), BF),
        pltpu.VMEM((rows, ff), BF),
        pltpu.VMEM((2, rows, half), F32),
        pltpu.VMEM((rows, width), F32),
        pltpu.VMEM((images, half_slots, 3 * half), BF),
        pltpu.VMEM((images, half_slots, 3 * half), BF),
        pltpu.VMEM((layers, images, half_slots, 3 * half), BF),
        pltpu.VMEM((images, half_slots, half), BF),
        pltpu.VMEM((images, half_slots, half), BF),
        pltpu.VMEM((layers, images, half_slots, half), BF),
        pltpu.VMEM((len(GRIDS), layers * heads, slots, slots), F32),
        pltpu.VMEM((layers * heads, slots, slots), F32),
        pltpu.VMEM((2, images, part, width), BF),
        pltpu.VMEM((2, images, part, width), BF),
        pltpu.SemaphoreType.DMA((remote_count,)),
        pltpu.SemaphoreType.DMA((remote_count,)),
        pltpu.SemaphoreType.DMA((chunks + 15 * layers + 4,)),
        pltpu.SemaphoreType.DMA((2,)),
    ]
    return pl.pallas_call(
        forward_kernel,
        out_shape=outs,
        in_specs=[SM] + [hbm] * 6 + [vm] * 15,
        out_specs=[vm] * 2 + [hbm] * 15,
        scratch_shapes=scratch,
        compiler_params=pltpu.CompilerParams(
            collective_id=0, has_side_effects=True, vmem_limit_bytes=60 * 2**20
        ),
    )(shape_id, tokens, cotangent, *owns, table, index, sources, targets, *vectors)


BEFORE = {
    (0, "im0"): ((0, 0, 1), (0, 1, 1)),
    (0, "im2"): ((0, 0, 2), (0, 1, 2), (0, 2, 1), (0, 3, 1)),
    (0, "sent4"): ((0, 0, 3), (0, 1, 3), (0, 2, 2), (0, 3, 2)),
    (1, "give0"): ((0, 0, 4), (0, 1, 4)),
    (1, "sent0"): ((0, 2, 3), (0, 3, 3), (0, 4, 1), (0, 5, 1)),
    (1, "give2"): ((0, 2, 4), (0, 3, 4)),
    (1, "sent2"): ((0, 4, 2), (0, 5, 2), (1, 0, 1), (1, 1, 1)),
    (1, "im0"): ((0, 4, 3), (0, 5, 3)),
    (1, "im2"): ((1, 0, 2), (1, 1, 2), (1, 2, 1), (1, 3, 1)),
    (1, "give4"): ((0, 4, 4), (0, 5, 4)),
    (1, "sent4"): (
        (1, 0, 3), (1, 1, 3), "fold0", (1, 2, 2), (1, 3, 2), "small1", "fold1", (1, 0, 4), (1, 1, 4), "small2", "fold2",
        "table1", (1, 4, 1), (1, 5, 1), "small3", "table2", (1, 2, 3), (1, 3, 3), "small4", (1, 4, 2), (1, 5, 2),
        "table3", (1, 2, 4), (1, 3, 4), "small5", (1, 4, 3), (1, 5, 3), "table4", (1, 4, 4), (1, 5, 4), "table5", "table6",
    ),
}


class HeadView:
    def __init__(self, ref):
        self.ref, self.per = ref, ref.shape[1]

    def __getitem__(self, at):
        return self.ref[(at[0] // self.per, at[0] % self.per) + tuple(at[1:])]

    def __setitem__(self, at, value):
        self.ref[(at[0] // self.per, at[0] % self.per) + tuple(at[1:])] = value


def backward_kernel(
    shape_ref, e_in, last_in, bias_in, h_in, n_in, heads_in, o_in, r_in, h1_in, n2_in, u_in, slope_in, m_in, q_in, p_in, f1_in, f2_in,
    g1_ref, as_ref, g2_ref, ms_ref, tgt_ref,
    out_ref, dx_ref, small_ref, matrix_ref, table_ref, other_ref, ds_out,
    e_s, h_s, n_s, heads_s, o_s, r_s, h1_s, n2_s, u_s, slope_s, m_s, wq, wp, w1, w2, bias_s,
    dm_s, cols_s, dz_s, dq_s, do_own, do_send, do_recv, dq_own, dq_send, dq_recv, ds_s,
    theirs, total, in1, in2, in3, in4, dx_send, dx_recv, small_in, table_in,
    send_sems, recv_sems, load_sems, bias_sems, ds_sems, slope_sems, back_sems, out_sems, credit,
):
    layers = q_in.shape[0]
    images, half_slots = do_own.shape[0], do_own.shape[1]
    rows, width = e_s.shape
    half = width // 2
    heads = half // HEAD
    block = width // 4
    cut = block // 2
    tile = half
    ff = u_s.shape[1]
    section, ci, yi, core, across, beside = ids()
    wide = lax.axis_index("wide")
    xi = section // 2
    z1, z2 = lax.rem(wide // 2, 2), lax.rem(wide // 4, 2)
    not_xi, not_yi, not_z1, not_z2, not_ci = 1 - xi, 1 - yi, 1 - z1, 1 - z2, 1 - ci
    near = {"wide": wide + 2 - 4 * z1}
    far = {"wide": wide + 4 - 8 * z2}
    greet((core, across, beside, near, far))

    def partner(c, stage):
        swap_xy = (core, across, beside, near, far) if c % 2 == 0 else (core, beside, across, near, far)
        return swap_xy[stage]

    def parts(c, stage):
        if stage == 0:
            return theirs.at[c % 2], total.at[c], total.at[c]
        if c % 2 == 0:
            if stage == 1:
                return total.at[c, not_xi], total.at[c, xi], in1.at[c]
            if stage == 2:
                return total.at[c, xi, :, :, not_yi], total.at[c, xi, :, :, yi], in2.at[c]
        else:
            if stage == 1:
                return total.at[c, :, :, :, not_yi], total.at[c, :, :, :, yi], in1.at[c]
            if stage == 2:
                return total.at[c, not_xi, :, :, yi], total.at[c, xi, :, :, yi], in2.at[c]
        if stage == 3:
            return total.at[c, xi, :, not_z1, yi], total.at[c, xi, :, z1, yi], in3.at[c]
        return total.at[c, xi, not_z2, z1, yi], total.at[c, xi, z2, z1, yi], in4.at[c]

    def link(turn, c, stage):
        at = (turn * 6 + c) * 5 + stage
        src, unused, dst = parts(c, stage)
        return pltpu.make_async_remote_copy(
            src_ref=src, dst_ref=dst, send_sem=send_sems.at[at], recv_sem=recv_sems.at[at],
            device_id=partner(c, stage), device_id_type=MESH,
        )

    def launch(turn, c, stage):
        if turn:
            pl.semaphore_wait(credit.at[c, stage], 1)
        link(turn, c, stage).start()

    def advance(turn, c, stage):
        link(turn, c, stage).wait_recv()
        unused, keep, came = parts(c, stage)
        summed = keep[...].astype(F32) + came[...].astype(F32)
        if stage < 4:
            keep[...] = summed.astype(BF)
            launch(turn, c, stage + 1)
            return
        matrix_ref[layers - 1 - turn, c] = summed
        for earlier in range(1, 5):
            link(turn, c, earlier).wait_send()
        if turn + 1 < layers:
            for earlier in range(5):
                pl.semaphore_signal(
                    credit.at[c, earlier], inc=1, device_id=partner(c, earlier), device_id_type=MESH
                )

    def hook(turn, name):
        for item in BEFORE.get((turn, name), ()):
            if isinstance(item, str):
                extras[item]()
            else:
                advance(*item)

    extra = layers * 30

    def exchange(index, src, dst, device=core):
        return pltpu.make_async_remote_copy(
            src_ref=src, dst_ref=dst, send_sem=send_sems.at[extra + index], recv_sem=recv_sems.at[extra + index],
            device_id=device, device_id_type=MESH,
        )

    five = (core, across, beside, near, far)

    def small_sum(k):
        return exchange(4 + k, small_ref, small_in.at[k], five[k])

    def small_step(k):
        def run():
            small_sum(k - 1).wait()
            small_ref[...] += small_in[k - 1]
            if k < 5:
                small_sum(k).start()

        return run

    def table_sum(k):
        if k == 4:
            return exchange(9 + k, table_ref, other_ref, core)
        return exchange(9 + k, table_ref, table_in.at[k], five[k + 1])

    def table_step(k):
        def run():
            if k > 1:
                table_sum(k - 2).wait()
                if k < 6:
                    table_ref[...] += table_in[k - 2]
            if k < 6:
                table_sum(k - 1).start()

        return run

    def fold_step(s):
        def run():
            if s == 0:
                for l in range(layers):
                    for i in range(images):
                        for copy in reload(l, i):
                            copy.wait()
            here = [jnp.where(shape_ref[xi * images + i] == s, 1.0, 0.0).astype(F32) for i in range(images)]

            def read(h):
                value = None
                for i in range(images):
                    row, lane = kept_place(h // heads, i, h % heads)
                    one = w2[row : row + slots, lane : lane + slots].astype(F32) * here[i]
                    value = one if value is None else value + one
                return value

            table_ref[s] = fold_scores(
                s, half_slots // 2, ci, read, tgt_ref, layers * heads, HeadView(bias_s), r_s, m_s
            )

        return run

    extras = {"small%d" % k: small_step(k) for k in range(1, 6)}
    extras.update({"table%d" % k: table_step(k) for k in range(1, 7)})
    extras.update({"fold%d" % s: fold_step(s) for s in range(3)})
    slots = 2 * half_slots

    def kept_place(l, i, h):
        at = (l * images + i) * heads + h
        return at // 3 * slots, at % 3 * 256

    def reload(l, i):
        copies = []
        for h in range(heads):
            row, lane = kept_place(l, i, h)
            place = w2.at[pl.ds(row, slots), pl.ds(lane, 256)]
            sem = back_sems.at[(l * images + i) * heads + h]
            copies.append(pltpu.make_async_copy(ds_out.at[l, i, h], place, sem))
        return copies

    def loads(names, l):
        table = {
            "m": (m_in, m_s), "u": (u_in, u_s), "w2": (f2_in, w2), "n2": (n2_in, n2_s),
            "w1": (f1_in, w1), "h1": (h1_in, h1_s), "r": (r_in, r_s), "wp": (p_in, wp), "heads": (heads_in, heads_s),
            "o": (o_in, o_s), "n": (n_in, n_s), "wq": (q_in, wq), "h": (h_in, h_s),
        }
        order = list(table)
        return [
            pltpu.make_async_copy(table[name][0].at[l], table[name][1], load_sems.at[order.index(name)])
            for name in names
        ]

    def begin(names, l):
        for copy in loads(names, l):
            copy.start()

    def have(name, l):
        loads((name,), l)[0].wait()

    feed = ("m", "u", "w2", "n2", "w1", "h1")
    attend = ("r", "wp", "heads", "o", "n", "wq", "h")

    def load_bias(l):
        return pltpu.make_async_copy(bias_in.at[:, pl.ds(l * heads, heads)], bias_s, bias_sems.at[0])

    def load_slope(l, t, slot):
        at = pl.ds(pl.multiple_of(t * tile, tile), tile)
        return pltpu.make_async_copy(slope_in.at[l, :, at], slope_s.at[slot], slope_sems.at[slot])

    def store_ds(l, i, slot):
        return pltpu.make_async_copy(ds_s.at[slot], ds_out.at[l, i], ds_sems.at[slot])

    last = layers - 1
    begin(feed, last)
    begin(attend, last)
    load_bias(last).start()
    first_load = pltpu.make_async_copy(e_in, e_s, out_sems.at[0])
    first_load.start()
    ours, theirs_images = pl.ds(xi * images, images), pl.ds(not_xi * images, images)
    out_keep = pltpu.make_async_copy(last_in.at[xi], out_ref.at[ours], out_sems.at[1])
    out_keep.start()
    out_send = exchange(14, last_in.at[not_xi], out_ref.at[ours], across)
    out_send.start()
    first_load.wait()
    small_ref[...] = jnp.zeros_like(small_ref)

    def note(l, row, value):
        small_ref[l, row : row + 1, :] = jnp.sum(value, axis=0, keepdims=True)

    def mine_first(low, top):
        return jnp.where(ci == 0, low, top)

    def norm_step(l, hidden, d_normed, gain_ref, row):
        hidden = hidden.astype(F32)
        centered = hidden - jnp.mean(hidden, axis=1, keepdims=True)
        inv = lax.rsqrt(jnp.mean(centered * centered, axis=1, keepdims=True) + EPS)
        xhat = centered * inv
        note(l, row, d_normed * xhat)
        note(l, row + 1, d_normed)
        dx = d_normed * gain_ref[...].astype(F32)[l : l + 1]
        mean_dx = jnp.mean(dx, axis=1, keepdims=True)
        mean_dxx = jnp.mean(dx * xhat, axis=1, keepdims=True)
        return e_s[...] + inv * (dx - mean_dx - xhat * mean_dxx)

    def give(turn, c):
        hook(turn, "give%d" % c)
        launch(turn, c, 0)
        launch(turn, c + 1, 0)

    def arrive(turn, c):
        link(turn, c, 0).wait_recv()
        link(turn, c + 1, 0).wait_recv()

    def go(turn, c):
        launch(turn, c, 1)
        launch(turn, c + 1, 1)
        link(turn, c, 0).wait_send()
        link(turn, c + 1, 0).wait_send()
        hook(turn, "sent%d" % c)

    def rounds(turn, c, product, side):
        for h in range(2):

            def one_x(x, carry):
                value = product(x, h).reshape(2, 2, 2, width // 8, half)
                if side:
                    theirs[h, x] = value.astype(BF)
                else:
                    total[c + h, x] = (value + total[c + h, x].astype(F32)).astype(BF)
                return carry

            lax.fori_loop(0, 2, one_x, 0)

    for turn in range(layers):
        l = last - turn
        have("m", l)
        up = e_s[...]
        note(l, 9, up * m_s[...])
        d_branch = (ms_ref[...].astype(F32)[l : l + 1] * up).astype(BF)
        dm_s[...] = d_branch
        d_branch = d_branch.astype(F32)
        note(l, 8, d_branch)
        sides = [
            jnp.concatenate(
                [
                    d_branch[:, (2 * x + c) * block + h * cut : (2 * x + c) * block + (h + 1) * cut]
                    for h in range(2)
                    for x in range(2)
                ],
                axis=1,
            )
            for c in range(2)
        ]
        cols_s[0] = mine_first(sides[0], sides[1]).astype(BF)
        cols_s[1] = mine_first(sides[1], sides[0]).astype(BF)
        have("u", l)

        def by_rows(side, first):
            def one(w, carry):
                at = pl.ds(pl.multiple_of(w * tile, tile), tile)
                value = dot(cols_s[side], u_s[:, at], 0, 0)
                w2_, w1_, w0_ = w // 4, lax.rem(w // 2, 2), lax.rem(w, 2)
                for h in range(2):
                    for x in range(2):
                        piece = value[(2 * h + x) * cut : (2 * h + x + 1) * cut]
                        if side:
                            theirs[h, x, w2_, w1_, w0_] = piece.astype(BF)
                        else:
                            total[h, x, w2_, w1_, w0_] = (
                                piece + total[h, x, w2_, w1_, w0_].astype(F32)
                            ).astype(BF)
                return carry

            lax.fori_loop(0, ff // tile, one, 0)

        load_slope(l, 0, 0).start()
        by_rows(1, 0)
        give(turn, 0)
        have("w2", l)

        def one_tile(t, carry):
            at = pl.ds(pl.multiple_of(t * tile, tile), tile)
            slot = lax.rem(t, 2)

            @pl.when(t + 1 < ff // tile)
            def _():
                load_slope(l, t + 1, 1 - slot).start()

            load_slope(l, t, slot).wait()
            d_pre = (dot(dm_s[...], w2[at, :], 1, 1) * slope_s[slot]).astype(BF)
            dz_s[:, at] = d_pre
            sums = jnp.sum(d_pre.astype(F32), axis=0, keepdims=True)
            small_ref[l, pl.ds(10 + t // 2, 1), pl.ds(pl.multiple_of(lax.rem(t, 2) * tile, tile), tile)] = sums
            return carry

        lax.fori_loop(0, ff // tile, one_tile, 0)
        arrive(turn, 0)
        by_rows(0, 0)
        go(turn, 0)
        have("n2", l)

        def of_first(side):
            def product(x, h):
                c = not_ci if side else ci
                at = pl.multiple_of((2 * x + c) * width + h * half, half)
                return dot(n2_s[...], dz_s[:, pl.ds(at, half)], 0, 0)

            return product

        rounds(turn, 2, of_first(1), 1)
        give(turn, 2)
        have("w1", l)
        have("h1", l)
        d_normed = jnp.concatenate(
            [dot(dz_s[...], w1[i * half : (i + 1) * half, :], 1, 1) for i in range(2)], axis=1
        )
        e_s[...] = norm_step(l, h1_s[...], d_normed, g2_ref, 6).astype(BF).astype(F32)
        have("r", l)
        up = e_s[...]
        note(l, 5, up * r_s[...])
        d_branch = (as_ref[...].astype(F32)[l : l + 1] * up).astype(BF)
        dm_s[...] = d_branch
        note(l, 4, d_branch.astype(F32))
        have("wp", l)
        if turn:
            exchange(2 * (turn - 1), do_send, do_recv).wait_send()
            exchange(2 * (turn - 1) + 1, dq_send, dq_recv).wait_send()
        for buffer, c in ((do_send, not_ci), (do_own, ci)):
            at = pl.ds(pl.multiple_of(c * half, half), half)
            value = dot(dm_s[...], wp[at, :], 1, 1)
            buffer[...] = value.reshape(images, half_slots, half).astype(BF)
            if buffer is do_send:
                exchange(2 * turn, do_send, do_recv).start()
        arrive(turn, 2)
        rounds(turn, 2, of_first(0), 0)
        go(turn, 2)
        if turn + 1 < layers:
            begin(feed, l - 1)
        have("heads", l)
        exchange(2 * turn, do_send, do_recv).wait_recv()
        lane = lax.broadcasted_iota(jnp.int32, (2 * half_slots, 128), 1)
        factor = HEAD**-0.5

        def one_image(i, carry):
            step = turn * images + i
            slot = lax.rem(step, 2)
            shape = shape_ref[xi * images + i]

            if turn:
                store_ds(l, i, slot).wait()
            else:

                @pl.when(i >= 2)
                def _():
                    store_ds(l, i, slot).wait()

            for pair in range(half // 128):
                at = pair * 128
                q, k, v = (
                    two_sides(
                        heads_s[0, i, :, w * half + at : w * half + at + 128],
                        heads_s[1, i, :, w * half + at : w * half + at + 128],
                    )
                    for w in range(3)
                )
                g = two_sides(do_own[i, :, at : at + 128], do_recv[i, :, at : at + 128])
                dqs, dks, dvs = [], [], []
                for e in range(2):
                    own = (lane // HEAD) == e
                    qm = jnp.where(own, q, jnp.zeros_like(q))
                    gm = jnp.where(own, g, jnp.zeros_like(g))
                    s = dot(qm, k, 1, 1) * factor + bias_s[shape, 2 * pair + e]
                    ex = jnp.exp(s - jnp.max(s, axis=1, keepdims=True))
                    p = ex / jnp.sum(ex, axis=1, keepdims=True)
                    dp = dot(gm, v, 1, 1)
                    ds = (p * (dp - jnp.sum(p * dp, axis=1, keepdims=True))).astype(BF)
                    ds_s[slot, 2 * pair + e, :, 0:slots] = ds
                    dvs.append(dot(p.astype(BF), g, 0, 0))
                    dqs.append(dot(ds, k))
                    dks.append(dot(ds, q, 0, 0))
                low = lane < HEAD
                for w, (zero, one, scale) in enumerate(
                    ((dqs[0], dqs[1], factor), (dks[0], dks[1], factor), (dvs[0], dvs[1], 1.0))
                ):
                    value = jnp.where(low, zero, one) * scale
                    dq_own[i, :, w * half + at : w * half + at + 128] = value[:half_slots].astype(BF)
                    dq_send[i, :, w * half + at : w * half + at + 128] = value[half_slots:].astype(BF)
            store_ds(l, i, slot).start()

            @pl.when(i == 0)
            def _():
                hook(turn, "im0")

            @pl.when(i == images - 1)
            def _():
                hook(turn, "im2")

            return carry

        load_bias(l).wait()
        lax.fori_loop(0, images, one_image, 0)
        if turn + 1 < layers:
            load_bias(l - 1).start()
        exchange(2 * turn + 1, dq_send, dq_recv).start()
        d_branch = dm_s[...].astype(F32)
        for w in range(3):
            at = pl.ds(pl.multiple_of(w * width + ci * half, half), half)
            dq_s[:, at] = dq_own[:, :, w * half : (w + 1) * half].astype(F32).reshape(rows, half).astype(BF)
        exchange(2 * turn + 1, dq_send, dq_recv).wait_recv()
        for w in range(3):
            at = pl.ds(pl.multiple_of(w * width + not_ci * half, half), half)
            dq_s[:, at] = (
                dq_recv[:, :, w * half : (w + 1) * half].astype(F32).reshape(rows, half).astype(BF)
            )
        note(l, 2, dq_s[:, 0:width].astype(F32))
        note(l, 3, dq_s[:, 2 * width : 3 * width].astype(F32))
        three = 3 * block
        for x in range(2):
            sides = []
            for c in range(2):
                s = 2 * x + c
                low, top = s * three // 128 * 128, -(-(s + 1) * three // 128) * 128
                d_part = dq_s[:, low:top].astype(F32)[:, s * three - low : (s + 1) * three - low]
                sides.append(jnp.concatenate([d_part, d_branch[:, s * block : (s + 1) * block]], axis=1))
            dz_s[:, x * width : (x + 1) * width] = mine_first(sides[0], sides[1]).astype(BF)
            dz_s[:, (2 + x) * width : (3 + x) * width] = mine_first(sides[1], sides[0]).astype(BF)
        have("n", l)
        have("o", l)

        def of_attention(side):
            def product(x, h):
                at = pl.multiple_of((2 * side + x) * width + h * half, half)
                right = dz_s[:, pl.ds(at, half)]
                if h == 0:
                    return dot(n_s[...], right, 0, 0)
                column = lax.broadcasted_iota(jnp.int32, (width, half), 1)
                return jnp.where(column < block, dot(n_s[...], right, 0, 0), dot(o_s[...], right, 0, 0))

            return product

        if turn + 1 == layers:
            for step in (layers * images - 2, layers * images - 1):
                store_ds(last - step // images, step % images, step % 2).wait()
            for done in range(layers):
                for i in range(images):
                    for copy in reload(done, i):
                        copy.start()
        rounds(turn, 4, of_attention(1), 1)
        give(turn, 4)
        have("wq", l)
        have("h", l)
        d_normed = jnp.concatenate(
            [dot(dq_s[...], wq[i * half : (i + 1) * half, :], 1, 1) for i in range(2)], axis=1
        )
        entering = norm_step(l, h_s[...], d_normed, g1_ref, 0)
        if l:
            e_s[...] = entering.astype(BF).astype(F32)
        else:
            for i in range(images):
                for x in range(2):
                    at = i * half_slots + x * (half_slots // 2)
                    value = entering[at : at + half_slots // 2]
                    dx_send[x, i] = value.astype(BF)

                    @pl.when(xi == x)
                    def _(value=value, i=i):
                        dx_ref[xi * images + i] = value

            dx_move = exchange(15, dx_send.at[not_xi], dx_recv, across)
            dx_move.start()
            small_sum(0).start()
        arrive(turn, 4)
        rounds(turn, 4, of_attention(0), 0)
        if turn + 1 < layers:
            begin(attend, l - 1)
        go(turn, 4)
    dx_move.wait()
    for i in range(images):
        dx_ref[not_xi * images + i] = dx_recv[i].astype(F32)
    out_keep.wait()
    out_send.wait()
    exchange(2 * layers - 2, do_send, do_recv).wait_send()
    exchange(2 * layers - 1, dq_send, dq_recv).wait_send()


def backward(shape_id, saved, vectors, images):
    e_first, last_blocks, bias_all, h_all, n_all = saved[:5]
    rows, width = e_first.shape
    layers, half, half_slots = n_all.shape[0], width // 2, rows // images
    ff = saved[10].shape[2]
    heads, slots, group, part = half // HEAD, 2 * half_slots, width // 8, half_slots // 2
    hbm, vm = pl.BlockSpec(memory_space=pl.ANY), pl.BlockSpec(memory_space=pltpu.VMEM)
    shape, v = jax.ShapeDtypeStruct, pltpu.VMEM
    shapes = len(GRIDS)
    unused, targets = bias_constants(slots, part)
    scratch = [
        v((rows, width), F32), v((rows, width), BF), v((rows, width), BF), v((2, images, half_slots, 3 * half), BF),
        v((rows, width), BF), v((rows, width), F32), v((rows, width), BF), v((rows, width), BF), v((rows, ff), BF),
        v((2, rows, half), F32), v((rows, width), F32), v((width, 3 * width), BF), v((width, width), BF),
        v((width, ff), BF), v((ff, width), BF), v((shapes, heads, slots, slots), F32),
        v((rows, width), BF), v((2, rows, half), BF), v((rows, ff), BF), v((rows, 3 * width), BF),
        v((images, half_slots, half), BF), v((images, half_slots, half), BF), v((images, half_slots, half), BF),
        v((images, half_slots, 3 * half), BF), v((images, half_slots, 3 * half), BF),
        v((images, half_slots, 3 * half), BF), v((2, heads, slots, 256), BF),
        v((2, 2, 2, 2, 2, group, half), BF), v((6, 2, 2, 2, 2, group, half), BF), v((6, 2, 2, 2, group, half), BF),
        v((6, 2, 2, group, half), BF), v((6, 2, group, half), BF), v((6, group, half), BF),
        v((2, images, part, width), BF), v((images, part, width), BF), v((5, layers, 16, width), F32),
        v((4, shapes, 16, LANES), F32),
        pltpu.SemaphoreType.DMA((layers * 30 + 16,)), pltpu.SemaphoreType.DMA((layers * 30 + 16,)),
        pltpu.SemaphoreType.DMA((14,)), pltpu.SemaphoreType.DMA((1,)), pltpu.SemaphoreType.DMA((2,)),
        pltpu.SemaphoreType.DMA((2,)), pltpu.SemaphoreType.DMA((layers * images * heads,)), pltpu.SemaphoreType.DMA((2,)),
        pltpu.SemaphoreType.REGULAR((6, 5)),
    ]
    return pl.pallas_call(
        backward_kernel,
        out_shape=[
            shape((2 * images, part, width), BF),
            shape((2 * images, part, width), F32),
            shape((layers, 16, width), F32),
            shape((layers, 6, group, half), F32),
            shape((shapes, 16, LANES), F32),
            shape((shapes, 16, LANES), F32),
            shape((layers, images, heads, slots, 256), BF),
        ],
        in_specs=[SM] + [hbm] * 17 + [vm] * 5,
        out_specs=[hbm] + [vm] * 5 + [hbm],
        scratch_shapes=scratch,
        compiler_params=pltpu.CompilerParams(
            collective_id=1, has_side_effects=True, vmem_limit_bytes=61 * 2**20
        ),
    )(shape_id, *saved, *vectors, targets)


def last_kernel(ci_ref, small_ref, matrix_ref, table_ref, other_ref, idx_ref, src_ref, *outs):
    layers, unused, group, half = matrix_ref.shape
    width, block = 2 * half, half // 2
    (g1, b1, wq, qb, vb, wp, pb, sa, table, g2, b2, w1, fb, w2, mb, sm) = outs
    for ref, row in ((g1, 0), (b1, 1), (qb, 2), (vb, 3), (pb, 4), (sa, 5), (g2, 6), (b2, 7), (mb, 8), (sm, 9)):
        ref[...] = jnp.concatenate([small_ref[l, row : row + 1, :] for l in range(layers)], axis=0)
    for l in range(layers):
        for t in range(fb.shape[1] // width):
            fb[l : l + 1, t * width : (t + 1) * width] = small_ref[l, 10 + t : 11 + t, :]
        w2[l] = jnp.concatenate([matrix_ref[l, 0], matrix_ref[l, 1]], axis=0).T
        w1[l, :, 0:half] = matrix_ref[l, 2]
        w1[l, :, half:width] = matrix_ref[l, 3]
        wq[l, :, 0:half] = matrix_ref[l, 4]
        wq[l, :, half : half + block] = matrix_ref[l, 5, :, 0:block]
        wp[l] = matrix_ref[l, 5, :, block:half]
    entries, heads = table.shape[1:]
    own = heads // 2
    both = [jnp.concatenate([table_ref[s], other_ref[s]], axis=0) for s in range(len(GRIDS))]
    rows = table_rows(both, idx_ref, src_ref, entries)
    for l in range(layers):
        mine, other = rows[l * own : (l + 1) * own], rows[16 + l * own : 16 + (l + 1) * own]
        first = ci_ref[0] == 0
        both = jnp.concatenate([jnp.where(first, mine, other), jnp.where(first, other, mine)], axis=0)
        pad = jnp.concatenate([both, jnp.zeros((16 - heads, entries), F32)], axis=0)
        table[l] = pad.T[:, :heads]


def last_form(ci, d_small, d_matrix, d_table, d_other, index, entries, heads, ff):
    layers, unused, group, half = d_matrix.shape
    width, block = 2 * half, half // 2
    shape = jax.ShapeDtypeStruct
    vector = shape((layers, width), F32)
    slots = index.shape[1] // 5
    sources, unused = bias_constants(slots, slots // 4)
    outs = [
        vector, vector, shape((layers, group, 3 * block), F32), vector, vector, shape((layers, group, block), F32),
        vector, vector, shape((layers, entries, heads), F32), vector, vector, shape((layers, group, width), F32),
        shape((layers, ff), F32), shape((layers, half, block), F32), vector, vector,
    ]
    return pl.pallas_call(
        last_kernel,
        out_shape=outs,
        in_specs=[SM] + [VM] * 6,
        out_specs=[VM] * 16,
        compiler_params=pltpu.CompilerParams(vmem_limit_bytes=40 * 2**20),
    )(ci, d_small, d_matrix, d_table, d_other, index, sources)


def attn_fwd_kernel(qkv_ref, bias_ref, o_ref):
    width = o_ref.shape[2]
    slots = o_ref.shape[1]
    lane = lax.broadcasted_iota(jnp.int32, (slots, 128), 1)
    for pair in range(width // 128):
        at = pair * 128
        q = qkv_ref[0, :, at : at + 128]
        k = qkv_ref[0, :, width + at : width + at + 128]
        v = qkv_ref[0, :, 2 * width + at : 2 * width + at + 128]
        outs = []
        for e in range(2):
            own = (lane // HEAD) == e
            qm = jnp.where(own, q, jnp.zeros_like(q))
            s = dot(qm, k, 1, 1) * HEAD**-0.5 + bias_ref[0, 2 * pair + e]
            ex = jnp.exp(s - jnp.max(s, axis=1, keepdims=True))
            p = ex / jnp.sum(ex, axis=1, keepdims=True)
            outs.append(dot(p.astype(BF), v))
        o_ref[0, :, at : at + 128] = jnp.where(lane < HEAD, outs[0], outs[1]).astype(BF)


def attn_fwd(qkv, bias):
    images, slots, wide = qkv.shape
    width = wide // 3
    heads = width // HEAD
    return pl.pallas_call(
        attn_fwd_kernel,
        grid=(images,),
        in_specs=[
            pl.BlockSpec((1, slots, wide), lambda i: (i, 0, 0)),
            pl.BlockSpec((1, heads, slots, slots), lambda i: (i, 0, 0, 0)),
        ],
        out_specs=pl.BlockSpec((1, slots, width), lambda i: (i, 0, 0)),
        out_shape=jax.ShapeDtypeStruct((images, slots, width), BF),
        compiler_params=pltpu.CompilerParams(vmem_limit_bytes=48 * 2**20),
    )(qkv, bias)


def bias_kernel(part, core_ref, table_ref, idx_ref, src_ref, tgt_ref, out_ref, nat_ref, wide_ref):
    make_bias(part, core_ref[0], table_ref, idx_ref, src_ref, tgt_ref, out_ref, nat_ref, wide_ref)


def bias_of(core, table, index, part):
    layers, unused, heads = table.shape
    own, slots = layers * (heads // 2), 4 * part
    sources, targets = bias_constants(slots, part)
    return pl.pallas_call(
        functools.partial(bias_kernel, part),
        out_shape=jax.ShapeDtypeStruct((len(GRIDS), own, slots, slots), F32),
        in_specs=[SM] + [VM] * 4,
        out_specs=VM,
        scratch_shapes=[pltpu.VMEM((own, slots, slots), F32), pltpu.VMEM((own * 24, LANES), F32)],
        compiler_params=pltpu.CompilerParams(vmem_limit_bytes=56 * 2**20),
    )(core, table, index, sources, targets)


def gather_rows(own, section, yi):
    depth = own.shape[0]
    cut = depth // 2
    beside = swap(own, "section", 1)
    first = swap(lax.dynamic_slice_in_dim(own, yi * cut, cut, 0), "section", 2)
    second = swap(first, "wide", 1)
    far = jnp.concatenate([pick(yi, first, second), pick(yi, second, first)], axis=0)
    far_beside = swap(far, "section", 1)
    whole = jnp.zeros((4 * depth, own.shape[1]), own.dtype)
    for r, piece in enumerate((own, beside, far, far_beside)):
        whole = lax.dynamic_update_slice_in_dim(whole, piece, (section ^ r) * depth, 0)
    return whole


def exchange_heads(value, ci, images):
    rows, width = value.shape
    half = width // 2
    keep = pick(ci, value[:, :half], value[:, half:])
    got = swap(pick(ci, value[:, half:], value[:, :half]), "section", 1)
    shape = (images, rows // images, half)
    return jnp.concatenate([keep.reshape(shape), got.reshape(shape)], axis=1)


def restore_heads(value, ci, blocks):
    images, slots, wide = value.shape
    rows, half = images * slots // 2, wide // blocks
    keep = value[:, : slots // 2].reshape(rows, wide)
    got = swap(value[:, slots // 2 :], "section", 1).reshape(rows, wide)
    pieces = []
    for b in range(blocks):
        a, o = keep[:, b * half : (b + 1) * half], got[:, b * half : (b + 1) * half]
        pieces += [pick(ci, a, o), pick(ci, o, a)]
    return jnp.concatenate(pieces, axis=1)


def norm(hidden, gain, offset):
    return (rows_norm(hidden.astype(F32)) * gain + offset).astype(BF)


def forward_general(hidden, owns, bias, vectors, images):
    section, wide = lax.axis_index("section"), lax.axis_index("wide")
    ci, yi = section % 2, wide % 2
    layers, width = owns[0].shape[0], hidden.shape[1]
    heads = width // 2 // HEAD
    kept = []
    for l in range(layers):
        gain1, offset1, q_b, v_b, proj_b, scale_a, gain2, offset2, fc1_b, fc2_b, scale_m = (
            v[l : l + 1].astype(F32) for v in vectors
        )
        wq, wp, w1, w2 = (gather_rows(own[l], section, yi) for own in owns)
        entering = hidden
        normed = norm(hidden, gain1, offset1)
        qkv = dot(normed, wq) + jnp.concatenate([q_b, jnp.zeros_like(q_b), v_b], axis=1)
        qkv = qkv.astype(BF)
        by_head = jnp.concatenate(
            [exchange_heads(qkv[:, b * width : (b + 1) * width], ci, images) for b in range(3)], axis=2
        )
        mixed = restore_heads(attn_fwd(by_head, bias[:, l * heads : (l + 1) * heads]), ci, 1)
        branch = dot(mixed, wp) + proj_b
        middle = (hidden.astype(F32) + scale_a * branch).astype(BF)
        normed2 = norm(middle, gain2, offset2)
        pre = dot(normed2, w1) + fc1_b
        cdf = 0.5 * (1.0 + lax.erf(pre * ROOT_HALF))
        act = (pre * cdf).astype(BF)
        slope = cdf + pre * jnp.exp(-0.5 * pre * pre) * INV_ROOT_2PI
        last = dot(act, w2) + fc2_b
        hidden = (middle.astype(F32) + scale_m * last).astype(BF)
        kept.append((entering, normed, by_head, mixed, branch, middle, normed2, act, slope, last, wq, wp, w1, w2))
    return hidden, list(zip(*kept))


def attn_bwd_kernel(qkv_ref, do_ref, bias_ref, dqkv_ref, ds_ref):
    width = do_ref.shape[2]
    slots = do_ref.shape[1]
    lane = lax.broadcasted_iota(jnp.int32, (slots, 128), 1)
    factor = HEAD**-0.5
    for pair in range(width // 128):
        at = pair * 128
        q, k, v = (qkv_ref[0, :, w * width + at : w * width + at + 128] for w in range(3))
        g = do_ref[0, :, at : at + 128]
        dqs, dks, dvs = [], [], []
        for e in range(2):
            own = (lane // HEAD) == e
            qm = jnp.where(own, q, jnp.zeros_like(q))
            gm = jnp.where(own, g, jnp.zeros_like(g))
            s = dot(qm, k, 1, 1) * factor + bias_ref[0, 2 * pair + e]
            ex = jnp.exp(s - jnp.max(s, axis=1, keepdims=True))
            p = ex / jnp.sum(ex, axis=1, keepdims=True)
            dp = dot(gm, v, 1, 1)
            ds = (p * (dp - jnp.sum(p * dp, axis=1, keepdims=True))).astype(BF)
            ds_ref[0, 2 * pair + e] = ds
            dvs.append(dot(p.astype(BF), g, 0, 0))
            dqs.append(dot(ds, k))
            dks.append(dot(ds, q, 0, 0))
        low = lane < HEAD
        for w, (zero, one, scale) in enumerate(
            ((dqs[0], dqs[1], factor), (dks[0], dks[1], factor), (dvs[0], dvs[1], 1.0))
        ):
            dqkv_ref[0, :, w * width + at : w * width + at + 128] = (
                jnp.where(low, zero, one) * scale
            ).astype(BF)


def attn_bwd(qkv, d_out, bias):
    images, slots, wide = qkv.shape
    width = wide // 3
    heads = width // HEAD
    one = lambda i: (i, 0, 0)
    return pl.pallas_call(
        attn_bwd_kernel,
        grid=(images,),
        in_specs=[
            pl.BlockSpec((1, slots, wide), one),
            pl.BlockSpec((1, slots, width), one),
            pl.BlockSpec((1, heads, slots, slots), lambda i: (i, 0, 0, 0)),
        ],
        out_specs=[
            pl.BlockSpec((1, slots, wide), one),
            pl.BlockSpec((1, heads, slots, slots), lambda i: (i, 0, 0, 0)),
        ],
        out_shape=[
            jax.ShapeDtypeStruct((images, slots, wide), BF),
            jax.ShapeDtypeStruct((images, heads, slots, slots), BF),
        ],
        compiler_params=pltpu.CompilerParams(vmem_limit_bytes=48 * 2**20),
    )(qkv, d_out, bias)


def norm_back(hidden, d_normed, gain):
    hidden = hidden.astype(F32)
    centered = hidden - jnp.mean(hidden, axis=1, keepdims=True)
    inv = lax.rsqrt(jnp.mean(centered * centered, axis=1, keepdims=True) + EPS)
    xhat = centered * inv
    dx = d_normed * gain
    mean_dx = jnp.mean(dx, axis=1, keepdims=True)
    mean_dxx = jnp.mean(dx * xhat, axis=1, keepdims=True)
    step = inv * (dx - mean_dx - xhat * mean_dxx)
    return step, jnp.sum(d_normed * xhat, axis=0), jnp.sum(d_normed, axis=0)


def backward_general(upstream, saved, bias, vectors, images):
    upstream = upstream.astype(BF)
    h_all, n_all, heads_all, o_all, r_all, h1_all, n2_all, u_all, slope_all, m_all = saved[:10]
    wq, wp, w1, w2 = saved[10:]
    gain1, scale_a, gain2, scale_m = (v.astype(F32) for v in vectors)
    section, wide = lax.axis_index("section"), lax.axis_index("wide")
    xi, ci = section // 2, section % 2
    wide_count = lax.axis_size("wide")
    layers = len(n_all)
    rows, width = upstream.shape
    half, half_slots = width // 2, rows // images
    heads = half // HEAD

    def columns(value, x, c):
        size = value.shape[1] // 4
        return value[:, (2 * x + c) * size : (2 * x + c + 1) * size]

    def add(a, b):
        return (a.astype(F32) + b.astype(F32)).astype(BF)

    def core_sum(left, right):
        own = [pick(ci, columns(right, x, 0), columns(right, x, 1)) for x in range(2)]
        other = [pick(ci, columns(right, x, 1), columns(right, x, 0)) for x in range(2)]
        got = swap(dot(left, jnp.concatenate(other, axis=1), 0, 0).astype(BF), "section", 1)
        return (dot(left, jnp.concatenate(own, axis=1), 0, 0) + got.astype(F32)).astype(BF)

    def x_step(value):
        size = value.shape[1] // 2
        low, top = value[:, :size], value[:, size:]
        return add(pick(xi, low, top), swap(pick(xi, top, low), "section", 2))

    def wide_steps(value):
        group = value.shape[0] // wide_count
        bit = 1
        while bit < wide_count:
            left = wide_count // bit
            cut = value.reshape(left // 2, 2, group, value.shape[-1])
            flag = (wide // bit) % 2
            keep = lax.dynamic_index_in_dim(cut, flag, 1, keepdims=False)
            send = lax.dynamic_index_in_dim(cut, 1 - flag, 1, keepdims=False)
            value = add(keep, swap(send, "wide", bit))
            bit *= 2
        return value.reshape(group, value.shape[-1])

    def x_first(left, right):
        return wide_steps(x_step(core_sum(left, right))).astype(F32)

    def wide_first(left, right):
        return x_step(wide_steps(core_sum(left, right))).astype(F32)

    small, matrices, d_scores = [None] * layers, [None] * layers, [None] * layers
    for l in reversed(range(layers)):
        up = upstream.astype(F32)
        d_mlp_scale = jnp.sum(up * m_all[l], axis=0)
        d_branch = (scale_m[l : l + 1] * up).astype(BF)
        d_fc2_b = jnp.sum(d_branch.astype(F32), axis=0)
        d_fc2 = wide_first(u_all[l], d_branch)
        d_pre = (dot(d_branch, w2[l], 1, 1) * slope_all[l]).astype(BF)
        d_fc1_b = jnp.sum(d_pre.astype(F32), axis=0).reshape(-1, width)
        d_fc1 = x_first(n2_all[l], d_pre)
        step, d_gain2, d_offset2 = norm_back(h1_all[l], dot(d_pre, w1[l], 1, 1), gain2[l : l + 1])
        up = (up + step).astype(BF).astype(F32)
        d_attn_scale = jnp.sum(up * r_all[l], axis=0)
        d_branch = (scale_a[l : l + 1] * up).astype(BF)
        d_proj_b = jnp.sum(d_branch.astype(F32), axis=0)
        d_proj = x_first(o_all[l], d_branch)
        d_mixed = exchange_heads(dot(d_branch, wp[l], 1, 1).astype(BF), ci, images)
        d_heads, d_scores[l] = attn_bwd(heads_all[l], d_mixed, bias[:, l * heads : (l + 1) * heads])
        d_qkv = restore_heads(d_heads, ci, 3)
        d_qkv_w = x_first(n_all[l], d_qkv)
        d_qkv_b = jnp.sum(d_qkv.astype(F32), axis=0)
        step, d_gain1, d_offset1 = norm_back(h_all[l], dot(d_qkv, wq[l], 1, 1), gain1[l : l + 1])
        entering = up + step
        upstream = entering.astype(BF)
        one = [d_gain1, d_offset1, d_qkv_b[:width], d_qkv_b[2 * width :], d_proj_b, d_attn_scale]
        one += [d_gain2, d_offset2, d_fc2_b, d_mlp_scale]
        one = jnp.concatenate([jnp.stack(one), d_fc1_b])
        small[l] = jnp.pad(one, ((0, 16 - one.shape[0]), (0, 0)))
        matrices[l] = (d_qkv_w, d_proj, d_fc1, d_fc2)
    matrices = [jnp.stack(group) for group in zip(*matrices)]
    return entering, jnp.stack(small), matrices, jnp.stack(d_scores)


def fold_kernel(part, core_ref, shape_ref, ds_ref, tgt_ref, out_ref, nat_ref, acc_ref, row_ref):
    layers, images, per_layer, slots = ds_ref.shape[:4]
    for s in range(len(GRIDS)):
        here = [jnp.where(shape_ref[i] == s, 1.0, 0.0).astype(F32) for i in range(images)]

        def read(h):
            return sum(ds_ref[h // per_layer, i, h % per_layer].astype(F32) * here[i] for i in range(images))

        out_ref[s] = fold_scores(
            s, part, core_ref[0], read, tgt_ref, layers * per_layer, nat_ref, acc_ref, row_ref
        )


def fold(core, shapes, d_scores, part):
    layers, images, per_layer, slots = d_scores.shape[:4]
    heads = layers * per_layer
    unused, targets = bias_constants(slots, part)
    return pl.pallas_call(
        functools.partial(fold_kernel, part),
        out_shape=jax.ShapeDtypeStruct((len(GRIDS), 16, LANES), F32),
        in_specs=[SM] * 2 + [VM] * 2,
        out_specs=VM,
        scratch_shapes=[
            pltpu.VMEM((heads, slots, slots), F32), pltpu.VMEM((heads * 24, LANES), F32),
            pltpu.VMEM((heads * 24, slots), F32),
        ],
        compiler_params=pltpu.CompilerParams(vmem_limit_bytes=56 * 2**20),
    )(core, shapes, d_scores, targets)


def table_kernel(table_ref, idx_ref, src_ref, out_ref):
    out_ref[...] = table_rows([table_ref[s] for s in range(len(GRIDS))], idx_ref, src_ref, out_ref.shape[1])


def table_form(d_table, index, entries):
    slots = index.shape[1] // 5
    sources, unused = bias_constants(slots, slots // 4)
    return pl.pallas_call(
        table_kernel,
        out_shape=jax.ShapeDtypeStruct((d_table.shape[1], entries), F32),
        in_specs=[VM] * 3,
        out_specs=VM,
        compiler_params=pltpu.CompilerParams(vmem_limit_bytes=40 * 2**20),
    )(d_table, index, sources)


def run_general(tokens, cotangent, shape_id, owns, table, index, vectors):
    section = lax.axis_index("section")
    xi, ci = section // 2, section % 2
    all_images, part, width = tokens.shape
    images = all_images // 2
    rows = images * 2 * part
    layers, entries, heads = table.shape
    own = heads // 2
    ff = owns[2].shape[2]

    def to_images(value):
        cut = value.reshape(2, images, part, width)
        keep = lax.dynamic_index_in_dim(cut, xi, 0, keepdims=False)
        got = swap(lax.dynamic_index_in_dim(cut, 1 - xi, 0, keepdims=False), "section", 2)
        both = jnp.concatenate([pick(xi, keep, got), pick(xi, got, keep)], axis=1)
        return both.reshape(rows, width)

    def to_slots(value):
        cut = value.reshape(images, 2, part, width)
        keep = lax.dynamic_index_in_dim(cut, xi, 1, keepdims=False)
        got = swap(lax.dynamic_index_in_dim(cut, 1 - xi, 1, keepdims=False), "section", 2)
        return jnp.concatenate([pick(xi, keep, got), pick(xi, got, keep)], axis=0)

    def all_sum(value, section_bits):
        for bit in section_bits:
            value = value + swap(value, "section", bit)
        bit = 1
        while bit < lax.axis_size("wide"):
            value = value + swap(value, "wide", bit)
            bit *= 2
        return value

    core = jnp.reshape(ci, (1,)).astype(jnp.int32)
    shapes = lax.dynamic_slice_in_dim(shape_id, xi * images, images, 0)
    bias_all = bias_of(core, table, index, part)
    bias = jnp.stack([lax.dynamic_index_in_dim(bias_all, shapes[i], 0, keepdims=False) for i in range(images)])
    hidden, saved = forward_general(to_images(tokens), owns, bias, vectors, images)
    place = jnp.arange(2 * part, dtype=jnp.int32)
    slot = place + ci * part + jnp.where(place >= part, part, 0)
    counts = sum(jnp.where(shapes == s, r * c + 1, 0) for s, (r, c) in enumerate(GRIDS))
    live = (slot[None, :] < counts[:, None]).reshape(rows, 1)
    upstream = jnp.where(live, to_images(cotangent), jnp.zeros((), BF))
    scales = (vectors[0], vectors[5], vectors[6], vectors[10])
    entering, d_small, matrices, d_scores = backward_general(upstream, saved, bias, scales, images)
    d_tokens = to_slots(entering.astype(BF)).astype(F32)
    d_small = all_sum(d_small.reshape(-1, width), (1, 2)).reshape(layers, 16, width)
    d_table = all_sum(fold(core, shapes, d_scores, part).reshape(-1, LANES), (2,)).reshape(-1, 16, LANES)
    other = swap(d_table, "section", 1)
    tables = [
        table_form(t, index, entries)[: layers * own].reshape(layers, own, entries)
        for t in (pick(ci, d_table, other), pick(ci, other, d_table))
    ]
    d_table = jnp.concatenate(tables, axis=1).transpose(0, 2, 1)
    wq, wp, w1, w2 = matrices
    fb = d_small[:, 10 : 10 + ff // width].reshape(layers, ff)
    g1, b1, qb, vb, pb, sa, g2, b2, mb, sm = (d_small[:, at] for at in range(10))
    return (to_slots(hidden), d_tokens, g1, b1, wq, qb, vb, wp, pb, sa, d_table, g2, b2, w1, fb, w2, mb, sm)


def shards(
    tokens,
    cotangent,
    shape_id,
    rel_index,
    norm1_gain,
    norm1_bias,
    qkv_weight,
    q_bias,
    v_bias,
    proj_weight,
    proj_bias,
    attn_scale,
    rel_table,
    norm2_gain,
    norm2_bias,
    fc1_weight,
    fc1_bias,
    fc2_weight,
    fc2_bias,
    mlp_scale,
):
    layers, entries, heads = rel_table.shape
    all_images, part, width = tokens.shape
    images = all_images // 2
    slots = 4 * part
    ff = fc1_weight.shape[2]
    index = jnp.stack(
        [
            jnp.concatenate(
                [rel_index[s, a * slots : (a + 1) * slots] for a in (0, 1, c, 1 + (r - 1) * c, r * c)]
            )
            for s, (r, c) in enumerate(GRIDS)
        ]
    )
    vectors = (
        norm1_gain, norm1_bias, q_bias, v_bias, proj_bias, attn_scale, norm2_gain, norm2_bias, fc1_bias, fc2_bias,
        mlp_scale,
    )
    owns = (qkv_weight, proj_weight, fc1_weight, fc2_weight)
    if layers != 2 or lax.axis_size("wide") != 8 or images * 2 * part > 320:
        return run_general(tokens, cotangent, shape_id, owns, rel_table, index, vectors)
    blocks, upstream, *saved = forward(shape_id, tokens, cotangent, owns, rel_table, index, vectors)
    scales = (norm1_gain, attn_scale, norm2_gain, mlp_scale)
    saved = [upstream, blocks] + saved
    out, d_tokens, d_small, d_matrix, d_table, d_other, unused = backward(shape_id, saved, scales, images)
    core = jnp.reshape(lax.axis_index("section") % 2, (1,)).astype(jnp.int32)
    return (out, d_tokens, *last_form(core, d_small, d_matrix, d_table, d_other, index, entries, heads, ff))


def solution(mesh):
    return jax.shard_map(
        shards,
        mesh=mesh,
        in_specs=(
            P("wide", "section", None),
            P("wide", "section", None),
            P("wide"),
            P(),
            P(),
            P(),
            P(None, "section", None),
            P(),
            P(),
            P(None, "section", None),
            P(),
            P(),
            P(),
            P(),
            P(),
            P(None, "section", None),
            P(),
            P(None, "section", None),
            P(),
            P(),
        ),
        out_specs=(
            P("wide", "section", None),
            P("wide", "section", None),
            P(),
            P(),
            P(None, "wide", "section"),
            P(),
            P(),
            P(None, "wide", "section"),
            P(),
            P(),
            P(),
            P(),
            P(),
            P(None, "wide", "section"),
            P(),
            P(None, "wide", "section"),
            P(),
            P(),
        ),
        check_vma=False,
    )
```

```python
import functools

import numpy as np
import jax
import jax.numpy as jnp
from jax import lax
from jax.experimental import pallas as pl
from jax.experimental.pallas import tpu as pltpu
from jax.sharding import PartitionSpec as P

GRIDS = ((14, 14), (10, 20), (8, 24))
EPS = 1e-06
DEAD = -1e30
ROOT_HALF = 0.7071067811865476
INV_ROOT_2PI = 0.3989422804014327
HEAD = 64
BF = jnp.bfloat16
F32 = jnp.float32


def swap(value, axis, bit):
    count = lax.axis_size(axis)
    return lax.ppermute(value, axis, [(i, i ^ bit) for i in range(count)])


def pick(flag, zero, one):
    return jnp.where(flag == 0, zero, one)


def dot(a, b, ca=1, cb=0, **kw):
    return lax.dot_general(a, b, (((ca,), (cb,)), ((), ())), preferred_element_type=F32, **kw)


LANES = 768

def up8(n): return -(-n//8)*8

def offset_sources(rows, cols, slots):
    pitch, span = 2 * cols - 1, 2 * rows - 1
    source = np.full((1, LANES), -1, np.int32)
    for j in range(span):
        r, rk = (0, j - (rows - 1)) if j >= rows - 1 else (rows - 1, j)
        for t in range(pitch):
            c, ck = (0, t - (cols - 1)) if t >= cols - 1 else (cols - 1, t)
            which = 1 + (1 if r else 0) * 2 + (1 if c else 0)
            source[0, j * pitch + t] = which * slots + 1 + rk * cols + ck
    length = pitch * span
    source[0, length : length + 4] = (0, 1, slots, slots - 1)
    return source

def key_targets(rows, cols, slots):
    pitch, length = 2 * cols - 1, (2 * cols - 1) * (2 * rows - 1)
    out = np.zeros((3, slots), np.int32)
    for k in range(slots):
        if k == 0:
            out[:, k] = length + 2, 0, length
        elif k <= rows * cols:
            rk, ck = divmod(k - 1, cols)
            out[:, k] = (rows - 1 + rk) * pitch + ck, pitch, length + 1
        else:
            out[:, k] = length + 3, 0, length + 3
    return out

def lane_onehot(target, dtype):
    n = target.shape[1]
    number = lax.broadcasted_iota(jnp.int32, (LANES, n), 0)
    return jnp.where(number == target, 1.0, 0.0).astype(dtype)

def block_order(core):
    return (0, 2, 1, 3) if core == 0 else (1, 3, 0, 2)

def bias_constants(slots, part):
    sources = np.concatenate([offset_sources(r, c, slots) for r, c in GRIDS])
    natural = np.stack([key_targets(r, c, slots) for r, c in GRIDS]).reshape(3, 3, 4, part)
    targets = np.stack([natural[:, :, list(block_order(c))].reshape(3, 3, slots) for c in range(2)])
    return jnp.asarray(sources), jnp.asarray(targets)


def make_bias(part, ci, table_ref, idx_ref, src_ref, tgt_ref, out_ref, nat_ref, wide_ref, between=None):
    layers, entries, all_heads = table_ref.shape
    own = all_heads // 2
    heads, slots = out_ref.shape[1:3]
    for s, (rows, cols) in enumerate(GRIDS):
        length = (2 * cols - 1) * (2 * rows - 1)
        step = up8(cols)
        count = rows * cols + 1
        pairs = idx_ref.shape[1]
        target = jnp.where(ci == 0, tgt_ref[0, s], tgt_ref[1, s])
        number = lax.broadcasted_iota(jnp.int32, (entries, pairs), 0)
        hot = jnp.where(number == idx_ref[s : s + 1, :], 1.0, 0.0).astype(BF)
        looked = []
        for l in range(layers):
            both = dot(table_ref[l], hot, 0, 0)
            looked.append(jnp.where(ci == 0, both[:own], both[own:]))
        looked = jnp.concatenate(looked + [jnp.zeros((16 - heads, pairs), F32)], axis=0).astype(BF)
        place = lax.broadcasted_iota(jnp.int32, (pairs, LANES), 0)
        hot = jnp.where(place == src_ref[s : s + 1, :], 1.0, 0.0).astype(BF)
        offsets = dot(looked, hot)
        turned = pltpu.roll(offsets, LANES - (cols - 1), 1)
        tail = lax.broadcasted_iota(jnp.int32, (step, LANES), 1) >= length
        for h in range(heads):
            row = jnp.broadcast_to(offsets[h : h + 1], (step, LANES))
            rolled = jnp.broadcast_to(turned[h : h + 1], (step, LANES))
            rolled = pltpu.roll(rolled, 0, 1, stride=1, stride_axis=0)
            wide_ref[h * step : (h + 1) * step, :] = jnp.where(tail, row, rolled)
        shifted = wide_ref[0 : heads * step, :].astype(BF)
        for r in range(rows):
            patch = dot(shifted, lane_onehot(target[0:1] - r * target[1:2], BF))
            for h in range(heads):
                nat_ref[h, 1 + r * cols : 1 + (r + 1) * cols, :] = patch[h * step : h * step + cols]
        first = dot(offsets.astype(BF), lane_onehot(target[2:3], BF))
        live = jnp.broadcast_to(target[2:3] < length + 2, (part, slots))
        for h in range(heads):
            nat_ref[h, 0:1, :] = first[h : h + 1]
            nat_ref[h, count:, :] = jnp.broadcast_to(
                offsets[h : h + 1, length + 3 : length + 4], (slots - count, slots)
            )
        for core in range(2):

            @pl.when(ci == core)
            def _(core=core):
                for h in range(heads):
                    for j, b in enumerate(block_order(core)):
                        block = nat_ref[h, b * part : (b + 1) * part, :]
                        out_ref[s, h, j * part : (j + 1) * part, :] = jnp.where(live, block, DEAD)

        if between is not None:
            between("bias%d" % s)


def exact_dot(value, hot, ca, cb):
    high = value.astype(BF)
    rest = value - high.astype(F32)
    middle = rest.astype(BF)
    low = (rest - middle.astype(F32)).astype(BF)
    n = value.shape[0]
    out = dot(jnp.concatenate([high, middle, low], axis=0), hot, ca, cb)
    return out[:n] + (out[n : 2 * n] + out[2 * n :])


def fold_scores(s, part, ci, read, tgt_ref, heads, nat_ref, acc_ref, row_ref):
    rows, cols = GRIDS[s]
    slots = 4 * part
    length = (2 * cols - 1) * (2 * rows - 1)
    step = up8(cols)
    count = rows * cols + 1
    target = jnp.where(ci == 0, tgt_ref[0, s], tgt_ref[1, s])

    def stack(pieces):
        return jnp.concatenate(pieces + [jnp.zeros((16 - heads,) + pieces[0].shape[1:], F32)], axis=0)

    for core in range(2):

        @pl.when(ci == core)
        def _(core=core):
            for h in range(heads):
                value = read(h)
                for j, b in enumerate(block_order(core)):
                    nat_ref[h, b * part : (b + 1) * part, :] = value[j * part : (j + 1) * part]

    acc_ref[0 : heads * step, :] = jnp.zeros((heads * step, LANES), F32)
    row_ref[0 : heads * step, 0:slots] = jnp.zeros((heads * step, slots), F32)
    for r in range(rows):
        for h in range(heads):
            row_ref[h * step : h * step + cols, 0:slots] = nat_ref[h, 1 + r * cols : 1 + (r + 1) * cols, :]
        hot = lane_onehot(target[0:1] - r * target[1:2], BF)
        acc_ref[0 : heads * step, :] += dot(row_ref[0 : heads * step, 0:slots].astype(BF), hot, 1, 1)
    lane = lax.broadcasted_iota(jnp.int32, (16, LANES), 1)
    offsets = jnp.zeros((16, LANES), F32)
    for c in range(cols):
        part_c = stack([acc_ref[h * step + c : h * step + c + 1, :] for h in range(heads)])
        back = pltpu.roll(part_c, cols - 1 - c, 1)
        offsets += jnp.where(lane >= length, part_c, back)
    first = stack([nat_ref[h, 0:1, :] for h in range(heads)])
    offsets += exact_dot(first, lane_onehot(target[2:3], BF), 1, 1)
    rest = stack(
        [
            jnp.sum(jnp.sum(nat_ref[h, count:, :], axis=0, keepdims=True), axis=1, keepdims=True)
            for h in range(heads)
        ]
    )
    return offsets + jnp.where(lane == length + 3, rest, 0.0)


def table_rows(offsets, idx_ref, src_ref, entries):
    total = None
    pairs = idx_ref.shape[1]
    for s in range(len(GRIDS)):
        place = lax.broadcasted_iota(jnp.int32, (pairs, LANES), 0)
        hot = jnp.where(place == src_ref[s : s + 1, :], 1.0, 0.0).astype(BF)
        looked = exact_dot(offsets[s], hot, 1, 1)
        number = lax.broadcasted_iota(jnp.int32, (entries, pairs), 0)
        hot = jnp.where(number == idx_ref[s : s + 1, :], 1.0, 0.0).astype(BF)
        value = exact_dot(looked, hot, 1, 1)
        total = value if total is None else total + value
    return total


VM = pl.BlockSpec(memory_space=pltpu.VMEM)
SM = pl.BlockSpec(memory_space=pltpu.SMEM)


MESH = pl.DeviceIdType.MESH


def ids():
    section, wide = lax.axis_index("section"), lax.axis_index("wide")
    ci, yi = lax.rem(section, 2), lax.rem(wide, 2)
    core = {"section": section + 1 - 2 * ci}
    across = {"section": lax.rem(section + 2, 4)}
    beside = {"wide": wide + 1 - 2 * yi}
    return section, ci, yi, core, across, beside


def greet(partners):
    barrier = pltpu.get_barrier_semaphore()
    for device in partners:
        pl.semaphore_signal(barrier, inc=1, device_id=device, device_id_type=MESH)
    pl.semaphore_wait(barrier, len(partners))


class Remote:
    def __init__(self, send, recv):
        self.send, self.recv, self.used, self.open = send, recv, 0, []

    def start(self, src, dst, device):
        copy = pltpu.make_async_remote_copy(
            src_ref=src, dst_ref=dst, send_sem=self.send.at[self.used],
            recv_sem=self.recv.at[self.used], device_id=device, device_id_type=MESH,
        )
        self.used += 1
        copy.start()
        self.open.append(copy)
        return copy

    def sent(self, copy):
        if any(copy is other for other in self.open):
            copy.wait_send()
            self.open = [other for other in self.open if other is not copy]

    def finish(self):
        for copy in self.open:
            copy.wait_send()
        self.open = []


class Local:
    def __init__(self, sems):
        self.sems, self.used, self.open = sems, 0, {}

    def start(self, src, dst, name=None):
        copy = pltpu.make_async_copy(src, dst, self.sems.at[self.used])
        self.open[name if name is not None else self.used] = copy
        self.used += 1
        copy.start()

    def wait(self, name):
        if name in self.open:
            self.open.pop(name).wait()

    def finish(self):
        for name in list(self.open):
            self.wait(name)


CHUNKS = (("q", 0, 1152), ("q", 1152, 1152), ("p", 0, 768), ("1", 0, 1536), ("1", 1536, 1536), ("2", 0, 384), ("2", 384, 384))


def plan_gather(chunks, per_layer):
    layers = chunks // per_layer
    points = [("bias0", 1, 0, 0, 0), ("bias1", 2, 0, 0, 0), ("bias2", 3, 1, 0, 0)]
    for l in range(layers):
        base = l * per_layer
        clock = 17 if l == 0 else 55
        for name, after, whole in (
            ("norm1", 0, base + 2), ("qkv", 9, 0), ("swap", 11, 0), ("im0", 13, 0), ("im1", 16, 0), ("im2", 18, 0),
            ("proj", 20, base + 3), ("norm2", 23, base + 4), ("up", 26, base + 5), ("down0", 30, base + 6),
            ("down1", 32, base + 7),
        ):
            t = clock + after
            points.append((name + str(l), int((t - 8) / 4.3), int((t - 15) / 4.3), int((t - 20) / 4.3), whole))
    plan, a, b, d, ready = {}, 0, 0, 0, 0
    for name, want_a, want_b, want_d, whole in points:
        want_a = max(want_a, min(whole + 2, chunks)) if whole else want_a
        want_b = max(want_b, min(whole + 1, chunks)) if whole else want_b
        want_d = max(want_d, whole)
        steps = []
        while a < min(want_a, chunks) or b < min(want_b, chunks) or d < min(want_d, chunks):
            if a < min(max(want_a, want_b, want_d), chunks) and a <= b + 2:
                steps.append(("a", a))
                a += 1
            elif b < min(max(want_b, want_d), a) and b <= d + 2:
                steps.append(("b", b))
                b += 1
            elif d < min(want_d, b):
                steps.append(("d", d))
                d += 1
            elif b < a:
                steps.append(("b", b))
                b += 1
            else:
                steps.append(("a", a))
                a += 1
        while ready < whole:
            steps.append(("whole", ready))
            ready += 1
        plan[name] = steps
    return plan


class Gather:
    KINDS = ("x", "xd", "c", "y", "z", "d", "cx", "cy", "cz", "cd")

    def __init__(self, where, near, z1, own, whole, sems, local_sems, layers):
        self.section, self.ci, self.yi, self.core, self.across, self.beside = where
        self.near, self.z1 = near, z1
        self.own, self.whole, self.sems, self.local_sems = own, whole, sems, local_sems
        self.chunks = [(l,) + chunk for l in range(layers) for chunk in CHUNKS]
        self.plan = plan_gather(len(self.chunks), len(CHUNKS))
        for k in range(len(self.chunks)):
            self.copy(k, "x").start()
            if self.mode(k) == "direct":
                self.copy(k, "xd").start()
        for k in range(len(CHUNKS)):
            self.begin_core(k)

    def mode(self, k):
        if k < 2 or k == len(self.chunks) - 1:
            return "direct"
        return "even" if k % 2 == 0 else "odd"

    def kinds(self, k):
        return [q for q in self.KINDS if q != ("d" if self.mode(k) == "direct" else "xd")]

    def rows(self, name, shard, quarter=None):
        depth = self.own[name].shape[1]
        if quarter is None:
            return pl.ds(pl.multiple_of(shard * depth, depth), depth)
        number = {
            "x": 2 * self.yi + self.z1,
            "y": 2 * (1 - self.yi) + self.z1,
            "z": 2 * self.yi + 1 - self.z1,
            "d": 2 * (1 - self.yi) + 1 - self.z1,
        }[quarter]
        cut = depth // 4
        return pl.ds(pl.multiple_of(shard * depth + number * cut, cut), cut)

    def copy(self, k, kind):
        l, name, at, size = self.chunks[k]
        cols = pl.ds(at, size)
        own, whole = self.own[name], self.whole[name]
        far = lax.rem(self.section + 2, 4)
        if kind == "c":
            src, dst, device = own.at[l, :, cols], whole.at[l, self.rows(name, self.section), cols], self.core
        elif kind in ("x", "xd"):
            quarter = kind[-1]
            src = own.at[l, self.rows(name, 0, quarter), cols]
            dst, device = whole.at[l, self.rows(name, self.section, quarter), cols], self.across
        else:
            quarter = {"y": "x", "z": "x", "d": "y" if self.mode(k) == "even" else "z"}.get(kind, kind[-1])
            device = {"y": self.beside, "z": self.near}.get(kind, self.core)
            if kind == "d":
                device = self.near if self.mode(k) == "even" else self.beside
            src = dst = whole.at[l, self.rows(name, far, quarter), cols]
        at = k * len(self.KINDS) + self.KINDS.index(kind)
        return pltpu.make_async_remote_copy(
            src_ref=src, dst_ref=dst, send_sem=self.sems[0].at[at], recv_sem=self.sems[1].at[at], device_id=device,
            device_id_type=MESH,
        )

    def own_copy(self, k):
        l, name, at, size = self.chunks[k]
        cols = pl.ds(at, size)
        place = self.whole[name].at[l, self.rows(name, self.section), cols]
        return pltpu.make_async_copy(self.own[name].at[l, :, cols], place, self.local_sems.at[k])

    def begin_core(self, k):
        self.copy(k, "c").start()
        self.own_copy(k).start()

    def at(self, point):
        for step, k in self.plan[point]:
            if step == "a":
                self.copy(k, "x").wait_recv()
                for kind in ("y", "z", "cx"):
                    self.copy(k, kind).start()
                if k + len(CHUNKS) < len(self.chunks):
                    self.begin_core(k + len(CHUNKS))
            elif step == "b":
                mode = self.mode(k)
                for kind, turn in (("y", "even"), ("z", "odd")):
                    self.copy(k, kind).wait_recv()
                    if mode == turn:
                        self.copy(k, "d").start()
                    self.copy(k, "c" + kind).start()
            elif step == "d":
                self.copy(k, "xd" if self.mode(k) == "direct" else "d").wait_recv()
                self.copy(k, "cd").start()
            else:
                self.own_copy(k).wait()
                for kind in ("c", "cx", "cy", "cz", "cd"):
                    self.copy(k, kind).wait_recv()

    def finish(self):
        for k in range(len(self.chunks)):
            for kind in self.kinds(k):
                self.copy(k, kind).wait_send()


def rows_norm(value):
    centered = value - jnp.mean(value, axis=1, keepdims=True)
    return centered * lax.rsqrt(jnp.mean(centered * centered, axis=1, keepdims=True) + EPS)


def two_sides(left, right):
    return jnp.concatenate([left.astype(F32), right.astype(F32)], axis=0).astype(BF)


def forward_kernel(
    shape_ref, tokens_ref, cot_ref, q_own, p_own, f1_own, f2_own, table_ref, idx_ref, src_ref, tgt_ref,
    g1_ref, b1_ref, qb_ref, vb_ref, pb_ref, as_ref, g2_ref, b2_ref, fb_ref, mb_ref, ms_ref,
    out_ref, e_ref, bias_out, h_out, n_out, heads_out, o_out, r_out, h1_out, n2_out, u_out, slope_out, m_out,
    q_out, p_out, f1_out, f2_out,
    wq, wp, w1, w2, h_s, n_s, o_s, r_s, h1_s, n2_s, u_s, slope_s, m_s,
    own_s, send_s, recv_s, om_s, os_s, or_s, bias_s, nat_s, tok_s, cot_s,
    send_sems, recv_sems, local_sems, slope_sems, gather_send, gather_recv, gather_local,
):
    layers = q_own.shape[0]
    images, half_slots = own_s.shape[0], own_s.shape[1]
    rows, width = h_s.shape
    half = width // 2
    heads = half // HEAD
    ff = u_s.shape[1]
    part = half_slots // 2
    tile = half
    where = ids()
    section, ci, yi, core, across, beside = where
    wide = lax.axis_index("wide")
    z1 = lax.rem(wide // 2, 2)
    near = {"wide": wide + 2 - 4 * z1}
    greet((core, across, beside, near))
    remote, local = Remote(send_sems, recv_sems), Local(local_sems)
    xi = section // 2
    ours, others = pl.ds(xi * images, images), pl.ds((1 - xi) * images, images)
    tokens_sent = remote.start(tokens_ref.at[others], tok_s.at[xi], across)
    local.start(tokens_ref.at[ours], tok_s.at[xi], "tokens")
    local.start(cot_ref.at[ours], cot_s.at[xi], "cot")
    whole = {"q": wq, "p": wp, "1": w1, "2": w2}
    gather = Gather(
        where, near, z1, {"q": q_own, "p": p_own, "1": f1_own, "2": f2_own}, whole,
        (gather_send, gather_recv), gather_local, layers,
    )

    def vec(ref, l, at=slice(None)):
        return ref[:, at].astype(F32)[l : l + 1]

    def join(blocks):
        return jnp.concatenate([blocks[x, i].astype(F32) for i in range(images) for x in range(2)], axis=0)

    make_bias(part, ci, table_ref, idx_ref, src_ref, tgt_ref, bias_s, nat_s, r_s, gather.at)
    local.start(bias_s, bias_out)
    local.wait("tokens")
    tokens_sent.wait_recv()
    h_s[...] = join(tok_s).astype(BF)
    lane = lax.broadcasted_iota(jnp.int32, (2 * half_slots, 128), 1)
    for l in range(layers):
        hidden = h_s[...].astype(F32)
        local.start(h_s, h_out.at[l], "h")
        local.wait("n")
        n_s[...] = (rows_norm(hidden) * vec(g1_ref, l) + vec(b1_ref, l)).astype(BF)
        local.start(n_s, n_out.at[l], "n")
        gather.at("norm1%d" % l)
        local.start(wq.at[l], q_out.at[l], ("w", "q", l))
        if l:
            remote.sent(pending)
            local.wait("own")
        for side, buffer in ((1, send_s), (0, own_s)):
            for which in range(3):
                at = pl.multiple_of(which * width + lax.rem(ci + side, 2) * half, half)
                value = dot(n_s[...], wq[l, :, pl.ds(at, half)])
                if which != 1:
                    at = pl.multiple_of(lax.rem(ci + side, 2) * half, half)
                    value = value + vec(qb_ref if which == 0 else vb_ref, l, pl.ds(at, half))
                buffer[:, :, which * half : (which + 1) * half] = value.reshape(
                    images, half_slots, half
                ).astype(BF)
            if side:
                pending = remote.start(send_s, recv_s.at[l], core)
                gather.at("qkv%d" % l)
        local.start(own_s, heads_out.at[l, 0], "own")
        gather.at("swap%d" % l)
        pending.wait_recv()
        local.start(recv_s.at[l], heads_out.at[l, 1])
        if l:
            remote.sent(o_pending)

        def one_image(i, carry):
            shape = shape_ref[xi * images + i]
            for pair in range(half // 128):
                q, k, v = (
                    two_sides(
                        own_s[i, :, w * half + pair * 128 : w * half + pair * 128 + 128],
                        recv_s[l, i, :, w * half + pair * 128 : w * half + pair * 128 + 128],
                    )
                    for w in range(3)
                )
                outs = []
                for e in range(2):
                    qm = jnp.where((lane // HEAD) == e, q, jnp.zeros_like(q))
                    s = dot(qm, k, 1, 1) * HEAD**-0.5 + bias_s[shape, l * heads + 2 * pair + e]
                    ex = jnp.exp(s - jnp.max(s, axis=1, keepdims=True))
                    p = ex / jnp.sum(ex, axis=1, keepdims=True)
                    outs.append(dot(p.astype(BF), v))
                mixed = jnp.where(lane < HEAD, outs[0], outs[1])
                om_s[i, :, pair * 128 : pair * 128 + 128] = mixed[:half_slots].astype(BF)
                os_s[i, :, pair * 128 : pair * 128 + 128] = mixed[half_slots:].astype(BF)
            for number in range(3):

                @pl.when(i == number)
                def _(number=number):
                    gather.at("im%d%d" % (number, l))

            return carry

        lax.fori_loop(0, images, one_image, 0)
        o_pending = remote.start(os_s, or_s.at[l], core)
        local.wait("o")
        mine = pl.ds(pl.multiple_of(ci * half, half), half)
        other = pl.ds(pl.multiple_of((1 - ci) * half, half), half)
        o_s[:, mine] = om_s[...].astype(F32).reshape(rows, half).astype(BF)
        gather.at("proj%d" % l)
        local.start(wp.at[l], p_out.at[l], ("w", "p", l))
        o_pending.wait_recv()
        o_s[:, other] = or_s[l].astype(F32).reshape(rows, half).astype(BF)
        local.start(o_s, o_out.at[l], "o")
        branch = dot(o_s[...], wp[l]) + vec(pb_ref, l)
        local.wait("r")
        r_s[...] = branch
        local.start(r_s, r_out.at[l], "r")
        local.wait("h1")
        h1_s[...] = (hidden + vec(as_ref, l) * branch).astype(BF)
        local.start(h1_s, h1_out.at[l], "h1")
        local.wait("n2")
        n2_s[...] = (
            rows_norm(h1_s[...].astype(F32)) * vec(g2_ref, l) + vec(b2_ref, l)
        ).astype(BF)
        local.start(n2_s, n2_out.at[l], "n2")
        local.wait("u")

        def store_slope(t):
            at = pl.ds(pl.multiple_of(t * tile, tile), tile)
            slot = lax.rem(t, 2)
            return pltpu.make_async_copy(slope_s.at[slot], slope_out.at[l, :, at], slope_sems.at[slot])

        for piece in range(2):
            gather.at(("norm2%d", "up%d")[piece] % l)

            def one_tile(t, carry):
                at = pl.ds(pl.multiple_of(t * tile, tile), tile)
                pre = dot(n2_s[...], w1[l, :, at]) + vec(fb_ref, l, at)
                cdf = 0.5 * (1.0 + lax.erf(pre * ROOT_HALF))
                u_s[:, at] = (pre * cdf).astype(BF)

                @pl.when(t >= 2)
                def _():
                    store_slope(t).wait()

                slope_s[lax.rem(t, 2)] = cdf + pre * jnp.exp(-0.5 * pre * pre) * INV_ROOT_2PI
                store_slope(t).start()
                return carry

            count = ff // tile // 2
            lax.fori_loop(piece * count, (piece + 1) * count, one_tile, 0)
        local.start(w1.at[l], f1_out.at[l], ("w", "1", l))
        local.start(u_s, u_out.at[l], "u")
        for t in (ff // tile - 2, ff // tile - 1):
            store_slope(t).wait()
        local.wait("m")
        local.wait("h")
        for piece in range(2):
            gather.at("down%d%d" % (piece, l))
            if l == layers - 1 and piece == 0:
                cot_sent = remote.start(cot_ref.at[others], cot_s.at[xi], across)
            at = slice(piece * half, (piece + 1) * half)
            branch = dot(u_s[...], w2[l, :, at]) + vec(mb_ref, l, at)
            m_s[:, at] = branch
            h_s[:, at] = (h1_s[:, at].astype(F32) + vec(ms_ref, l, at) * branch).astype(BF)
        local.start(w2.at[l], f2_out.at[l], ("w", "2", l))
        local.start(m_s, m_out.at[l], "m")
    final = h_s[...].astype(F32)
    place = lax.broadcasted_iota(jnp.int32, (half_slots, width), 0)
    slot = place + ci * part + jnp.where(place >= part, part, 0)
    local.wait("cot")
    cot_sent.wait_recv()
    upstream = join(cot_s)
    for i in range(images):
        shape = shape_ref[xi * images + i]
        count = sum(jnp.where(shape == s, r * c + 1, 0) for s, (r, c) in enumerate(GRIDS))
        at = i * half_slots
        for x in range(2):
            out_ref[x, i] = final[at + x * part : at + (x + 1) * part].astype(BF)
        e_ref[at : at + half_slots, :] = jnp.where(slot < count, upstream[at : at + half_slots], 0.0)
    gather.finish()
    remote.finish()
    local.finish()


def forward(shape_id, tokens, cotangent, owns, table, index, vectors):
    all_images, part, width = tokens.shape
    images = all_images // 2
    rows = images * 2 * part
    layers = owns[0].shape[0]
    half = width // 2
    half_slots = 2 * part
    slots = 2 * half_slots
    ff = owns[2].shape[2]
    heads = half // HEAD
    hbm, vm = pl.BlockSpec(memory_space=pl.ANY), pl.BlockSpec(memory_space=pltpu.VMEM)
    shape = jax.ShapeDtypeStruct
    sources, targets = bias_constants(slots, part)
    outs = [
        shape((2, images, part, width), BF),
        shape((rows, width), F32),
        shape((len(GRIDS), layers * heads, slots, slots), F32),
        shape((layers, rows, width), BF),
        shape((layers, rows, width), BF),
        shape((layers, 2, images, half_slots, 3 * half), BF),
        shape((layers, rows, width), BF),
        shape((layers, rows, width), F32),
        shape((layers, rows, width), BF),
        shape((layers, rows, width), BF),
        shape((layers, rows, ff), BF),
        shape((layers, rows, ff), F32),
        shape((layers, rows, width), F32),
        shape((layers, width, 3 * width), BF),
        shape((layers, width, width), BF),
        shape((layers, width, ff), BF),
        shape((layers, ff, width), BF),
    ]
    chunks = layers * len(CHUNKS)
    remote_count = 2 * layers + 2
    scratch = [
        pltpu.VMEM((layers, width, 3 * width), BF),
        pltpu.VMEM((layers, width, width), BF),
        pltpu.VMEM((layers, width, ff), BF),
        pltpu.VMEM((layers, ff, width), BF),
        pltpu.VMEM((rows, width), BF),
        pltpu.VMEM((rows, width), BF),
        pltpu.VMEM((rows, width), BF),
        pltpu.VMEM((rows, width), F32),
        pltpu.VMEM((rows, width), BF),
        pltpu.VMEM((rows, width), BF),
        pltpu.VMEM((rows, ff), BF),
        pltpu.VMEM((2, rows, half), F32),
        pltpu.VMEM((rows, width), F32),
        pltpu.VMEM((images, half_slots, 3 * half), BF),
        pltpu.VMEM((images, half_slots, 3 * half), BF),
        pltpu.VMEM((layers, images, half_slots, 3 * half), BF),
        pltpu.VMEM((images, half_slots, half), BF),
        pltpu.VMEM((images, half_slots, half), BF),
        pltpu.VMEM((layers, images, half_slots, half), BF),
        pltpu.VMEM((len(GRIDS), layers * heads, slots, slots), F32),
        pltpu.VMEM((layers * heads, slots, slots), F32),
        pltpu.VMEM((2, images, part, width), BF),
        pltpu.VMEM((2, images, part, width), BF),
        pltpu.SemaphoreType.DMA((remote_count,)),
        pltpu.SemaphoreType.DMA((remote_count,)),
        pltpu.SemaphoreType.DMA((15 * layers + 4,)),
        pltpu.SemaphoreType.DMA((2,)),
        pltpu.SemaphoreType.DMA((chunks * 10,)),
        pltpu.SemaphoreType.DMA((chunks * 10,)),
        pltpu.SemaphoreType.DMA((chunks,)),
    ]
    return pl.pallas_call(
        forward_kernel,
        out_shape=outs,
        in_specs=[SM] + [hbm] * 6 + [vm] * 15,
        out_specs=[vm] * 2 + [hbm] * 15,
        scratch_shapes=scratch,
        compiler_params=pltpu.CompilerParams(
            collective_id=0, has_side_effects=True, vmem_limit_bytes=60 * 2**20
        ),
    )(shape_id, tokens, cotangent, *owns, table, index, sources, targets, *vectors)


SCHEDULE = {
    (0, "im0"): ((0, 1, 1),),
    (0, "im2"): ((0, 0, 1),),
    (0, "give4"): ((0, 2, 1), (0, 3, 1),),
    (0, "dn"): ((0, 1, 2), (0, 0, 2),),
    (0, "go4"): ((0, 1, 3),),
    (1, "setup"): ((0, 0, 3), (0, 3, 2), (0, 0, 4),),
    (1, "fc2t"): ((0, 2, 2), (0, 1, 4),),
    (1, "give0"): ((0, 3, 3), (0, 5, 1), (0, 4, 1),),
    (1, "dz"): ((0, 2, 3),),
    (1, "go0"): ((0, 3, 4),),
    (1, "fc1t"): ((0, 4, 2), (0, 2, 4),),
    (1, "dmix"): ((0, 5, 2),),
    (1, "exch"): ((1, 0, 1),),
    (1, "im0"): ((1, 1, 1), (0, 5, 3),),
    (1, "im1"): ((0, 4, 3),),
    (1, "attt"): ((0, 4, 4), (0, 5, 4), (1, 2, 1),),
    (1, "give4"): ((1, 1, 2), (1, 0, 2), (1, 3, 1),),
    (1, "dn"): ((1, 1, 3),),
    (1, "go4"): ((1, 2, 2), (1, 3, 2), "fold0", "small1", (1, 2, 3), (1, 0, 3), "fold2", "fold1", (1, 5, 1), (1, 4, 1), "table1", (1, 0, 4), "small2", "table2", (1, 5, 2), "small3", (1, 3, 3), "table3", (1, 2, 4), (1, 4, 2), "small4", (1, 1, 4), "table4", (1, 5, 3), "dxgo", (1, 4, 3), (1, 3, 4), "table5", "table6", (1, 5, 4), (1, 4, 4), "small5",),
}


class HeadView:
    def __init__(self, ref):
        self.ref, self.per = ref, ref.shape[1]

    def __getitem__(self, at):
        return self.ref[(at[0] // self.per, at[0] % self.per) + tuple(at[1:])]

    def __setitem__(self, at, value):
        self.ref[(at[0] // self.per, at[0] % self.per) + tuple(at[1:])] = value


def backward_kernel(
    shape_ref, e_in, last_in, bias_in, h_in, n_in, heads_in, o_in, r_in, h1_in, n2_in, u_in, slope_in, m_in, q_in, p_in, f1_in, f2_in,
    g1_ref, as_ref, g2_ref, ms_ref, tgt_ref,
    out_ref, dx_ref, small_ref, matrix_ref, table_ref, other_ref, ds_out,
    e_s, h_s, n_s, heads_s, o_s, r_s, h1_s, n2_s, u_s, slope_s, m_s, wq, wp, w1, w2, bias_s,
    dm_s, cols_s, dz_s, dq_s, do_own, do_send, do_recv, dq_own, dq_send, dq_recv, ds_s,
    theirs, total, in1, in2, in3, in4, dx_send, dx_recv, small_in, table_in,
    send_sems, recv_sems, load_sems, bias_sems, ds_sems, slope_sems, back_sems, out_sems, credit,
):
    layers = q_in.shape[0]
    images, half_slots = do_own.shape[0], do_own.shape[1]
    rows, width = e_s.shape
    half = width // 2
    heads = half // HEAD
    block = width // 4
    cut = block // 2
    tile = half
    ff = u_s.shape[1]
    section, ci, yi, core, across, beside = ids()
    wide = lax.axis_index("wide")
    xi = section // 2
    z1, z2 = lax.rem(wide // 2, 2), lax.rem(wide // 4, 2)
    not_xi, not_yi, not_z1, not_z2, not_ci = 1 - xi, 1 - yi, 1 - z1, 1 - z2, 1 - ci
    near = {"wide": wide + 2 - 4 * z1}
    far = {"wide": wide + 4 - 8 * z2}
    greet((core, across, beside, near, far))

    def partner(c, stage):
        swap_xy = (core, across, beside, near, far) if c % 2 == 0 else (core, beside, across, near, far)
        return swap_xy[stage]

    def parts(c, stage):
        if stage == 0:
            return theirs.at[c % 2], total.at[c], total.at[c]
        if c % 2 == 0:
            if stage == 1:
                return total.at[c, not_xi], total.at[c, xi], in1.at[c]
            if stage == 2:
                return total.at[c, xi, :, :, not_yi], total.at[c, xi, :, :, yi], in2.at[c]
        else:
            if stage == 1:
                return total.at[c, :, :, :, not_yi], total.at[c, :, :, :, yi], in1.at[c]
            if stage == 2:
                return total.at[c, not_xi, :, :, yi], total.at[c, xi, :, :, yi], in2.at[c]
        if stage == 3:
            return total.at[c, xi, :, not_z1, yi], total.at[c, xi, :, z1, yi], in3.at[c]
        return total.at[c, xi, not_z2, z1, yi], total.at[c, xi, z2, z1, yi], in4.at[c]

    def link(turn, c, stage):
        at = (turn * 6 + c) * 5 + stage
        src, unused, dst = parts(c, stage)
        return pltpu.make_async_remote_copy(
            src_ref=src, dst_ref=dst, send_sem=send_sems.at[at], recv_sem=recv_sems.at[at],
            device_id=partner(c, stage), device_id_type=MESH,
        )

    def launch(turn, c, stage):
        if turn:
            pl.semaphore_wait(credit.at[c, stage], 1)
        link(turn, c, stage).start()

    def advance(turn, c, stage):
        link(turn, c, stage).wait_recv()
        unused, keep, came = parts(c, stage)
        summed = keep[...].astype(F32) + came[...].astype(F32)
        if stage < 4:
            keep[...] = summed.astype(BF)
            launch(turn, c, stage + 1)
            return
        matrix_ref[layers - 1 - turn, c] = summed
        for earlier in range(1, 5):
            link(turn, c, earlier).wait_send()
        if turn + 1 < layers:
            for earlier in range(5):
                pl.semaphore_signal(
                    credit.at[c, earlier], inc=1, device_id=partner(c, earlier), device_id_type=MESH
                )

    def hook(turn, name):
        for item in SCHEDULE.get((turn, name), ()):
            if isinstance(item, str):
                extras[item]()
            else:
                advance(*item)

    extra = layers * 30

    def exchange(index, src, dst, device=core):
        return pltpu.make_async_remote_copy(
            src_ref=src, dst_ref=dst, send_sem=send_sems.at[extra + index], recv_sem=recv_sems.at[extra + index],
            device_id=device, device_id_type=MESH,
        )

    small_order, table_order = (core, near, far, beside, across), (near, far, beside, across)

    def small_sum(k):
        return exchange(4 + k, small_ref, small_in.at[k], small_order[k])

    def small_step(k):
        def run():
            small_sum(k - 1).wait()
            small_ref[...] += small_in[k - 1]
            if k < 5:
                small_sum(k).start()

        return run

    def table_sum(k):
        if k == 4:
            return exchange(9 + k, table_ref, other_ref, core)
        return exchange(9 + k, table_ref, table_in.at[k], table_order[k])

    def table_step(k):
        def run():
            if k > 1:
                table_sum(k - 2).wait()
                if k < 6:
                    table_ref[...] += table_in[k - 2]
            if k < 6:
                table_sum(k - 1).start()

        return run

    def fold_step(s):
        def run():
            here = [jnp.where(shape_ref[xi * images + i] == s, 1.0, 0.0).astype(F32) for i in range(images)]

            def read(h):
                value = None
                for i in range(images):
                    row, lane = kept_place(h // heads, i, h % heads)
                    one = w2[row : row + slots, lane : lane + slots].astype(F32) * here[i]
                    value = one if value is None else value + one
                return value

            table_ref[s] = fold_scores(
                s, half_slots // 2, ci, read, tgt_ref, layers * heads, HeadView(bias_s), r_s, m_s
            )

        return run

    extras = {"small%d" % k: small_step(k) for k in range(1, 6)}
    extras.update({"table%d" % k: table_step(k) for k in range(1, 7)})
    extras.update({"fold%d" % s: fold_step(s) for s in range(3)})
    extras["dxgo"] = lambda: exchange(15, dx_send.at[not_xi], dx_recv, across).start()
    slots = 2 * half_slots

    def kept_place(l, i, h):
        at = (l * images + i) * heads + h
        return at // 3 * slots, at % 3 * 256

    def reload(l, i):
        copies = []
        for h in range(heads):
            row, lane = kept_place(l, i, h)
            place = w2.at[pl.ds(row, slots), pl.ds(lane, 256)]
            sem = back_sems.at[(l * images + i) * heads + h]
            copies.append(pltpu.make_async_copy(ds_out.at[l, i, h], place, sem))
        return copies

    def loads(names, l):
        table = {
            "m": (m_in, m_s), "u": (u_in, u_s), "w2": (f2_in, w2), "n2": (n2_in, n2_s),
            "w1": (f1_in, w1), "h1": (h1_in, h1_s), "r": (r_in, r_s), "wp": (p_in, wp), "heads": (heads_in, heads_s),
            "o": (o_in, o_s), "n": (n_in, n_s), "wq": (q_in, wq), "h": (h_in, h_s),
        }
        order = list(table)
        return [
            pltpu.make_async_copy(table[name][0].at[l], table[name][1], load_sems.at[order.index(name)])
            for name in names
        ]

    def begin(names, l):
        for copy in loads(names, l):
            copy.start()

    def have(name, l):
        loads((name,), l)[0].wait()

    feed = ("m", "u", "w2", "n2", "w1", "h1")
    attend = ("r", "wp", "heads", "o", "n", "wq", "h")

    def load_bias(l):
        return pltpu.make_async_copy(bias_in.at[:, pl.ds(l * heads, heads)], bias_s, bias_sems.at[0])

    def load_slope(l, t, slot):
        at = pl.ds(pl.multiple_of(t * tile, tile), tile)
        return pltpu.make_async_copy(slope_in.at[l, :, at], slope_s.at[slot], slope_sems.at[slot])

    def store_ds(l, i, slot):
        return pltpu.make_async_copy(ds_s.at[slot], ds_out.at[l, i], ds_sems.at[slot])

    last = layers - 1
    begin(feed, last)
    begin(attend, last)
    load_bias(last).start()
    first_load = pltpu.make_async_copy(e_in, e_s, out_sems.at[0])
    first_load.start()
    ours, theirs_images = pl.ds(xi * images, images), pl.ds(not_xi * images, images)
    out_keep = pltpu.make_async_copy(last_in.at[xi], out_ref.at[ours], out_sems.at[1])
    out_keep.start()
    out_send = exchange(14, last_in.at[not_xi], out_ref.at[ours], across)
    out_send.start()
    first_load.wait()
    small_ref[...] = jnp.zeros_like(small_ref)

    def note(l, row, value):
        small_ref[l, row : row + 1, :] = jnp.sum(value, axis=0, keepdims=True)

    def mine_first(low, top):
        return jnp.where(ci == 0, low, top)

    def norm_step(l, hidden, d_normed, gain_ref, row):
        hidden = hidden.astype(F32)
        centered = hidden - jnp.mean(hidden, axis=1, keepdims=True)
        inv = lax.rsqrt(jnp.mean(centered * centered, axis=1, keepdims=True) + EPS)
        xhat = centered * inv
        note(l, row, d_normed * xhat)
        note(l, row + 1, d_normed)
        dx = d_normed * gain_ref[...].astype(F32)[l : l + 1]
        mean_dx = jnp.mean(dx, axis=1, keepdims=True)
        mean_dxx = jnp.mean(dx * xhat, axis=1, keepdims=True)
        return e_s[...] + inv * (dx - mean_dx - xhat * mean_dxx)

    def give(turn, c):
        launch(turn, c, 0)
        launch(turn, c + 1, 0)
        hook(turn, "give%d" % c)

    def arrive(turn, c):
        link(turn, c, 0).wait_recv()
        link(turn, c + 1, 0).wait_recv()

    def go(turn, c):
        launch(turn, c, 1)
        launch(turn, c + 1, 1)
        link(turn, c, 0).wait_send()
        link(turn, c + 1, 0).wait_send()
        hook(turn, "go%d" % c)

    def rounds(turn, c, product, side):
        for h in range(2):

            def one_x(x, carry):
                value = product(x, h).reshape(2, 2, 2, width // 8, half)
                if side:
                    theirs[h, x] = value.astype(BF)
                else:
                    total[c + h, x] = (value + total[c + h, x].astype(F32)).astype(BF)
                return carry

            lax.fori_loop(0, 2, one_x, 0)

    for turn in range(layers):
        l = last - turn
        have("m", l)
        up = e_s[...]
        note(l, 9, up * m_s[...])
        d_branch = (ms_ref[...].astype(F32)[l : l + 1] * up).astype(BF)
        dm_s[...] = d_branch
        d_branch = d_branch.astype(F32)
        note(l, 8, d_branch)
        sides = [
            jnp.concatenate(
                [
                    d_branch[:, (2 * x + c) * block + h * cut : (2 * x + c) * block + (h + 1) * cut]
                    for h in range(2)
                    for x in range(2)
                ],
                axis=1,
            )
            for c in range(2)
        ]
        cols_s[0] = mine_first(sides[0], sides[1]).astype(BF)
        cols_s[1] = mine_first(sides[1], sides[0]).astype(BF)
        have("u", l)
        hook(turn, "setup")

        def by_rows(side, first):
            def one(w, carry):
                at = pl.ds(pl.multiple_of(w * tile, tile), tile)
                value = dot(cols_s[side], u_s[:, at], 0, 0)
                w2_, w1_, w0_ = w // 4, lax.rem(w // 2, 2), lax.rem(w, 2)
                for h in range(2):
                    for x in range(2):
                        piece = value[(2 * h + x) * cut : (2 * h + x + 1) * cut]
                        if side:
                            theirs[h, x, w2_, w1_, w0_] = piece.astype(BF)
                        else:
                            total[h, x, w2_, w1_, w0_] = (
                                piece + total[h, x, w2_, w1_, w0_].astype(F32)
                            ).astype(BF)
                return carry

            lax.fori_loop(0, ff // tile, one, 0)

        load_slope(l, 0, 0).start()
        by_rows(1, 0)
        hook(turn, "fc2t")
        give(turn, 0)
        have("w2", l)

        def one_tile(t, carry):
            at = pl.ds(pl.multiple_of(t * tile, tile), tile)
            slot = lax.rem(t, 2)

            @pl.when(t + 1 < ff // tile)
            def _():
                load_slope(l, t + 1, 1 - slot).start()

            load_slope(l, t, slot).wait()
            d_pre = (dot(dm_s[...], w2[at, :], 1, 1) * slope_s[slot]).astype(BF)
            dz_s[:, at] = d_pre
            sums = jnp.sum(d_pre.astype(F32), axis=0, keepdims=True)
            small_ref[l, pl.ds(10 + t // 2, 1), pl.ds(pl.multiple_of(lax.rem(t, 2) * tile, tile), tile)] = sums
            return carry

        lax.fori_loop(0, ff // tile, one_tile, 0)
        hook(turn, "dz")
        arrive(turn, 0)
        by_rows(0, 0)
        go(turn, 0)
        have("n2", l)

        def of_first(side):
            def product(x, h):
                c = not_ci if side else ci
                at = pl.multiple_of((2 * x + c) * width + h * half, half)
                return dot(n2_s[...], dz_s[:, pl.ds(at, half)], 0, 0)

            return product

        rounds(turn, 2, of_first(1), 1)
        hook(turn, "fc1t")
        give(turn, 2)
        have("w1", l)
        have("h1", l)
        d_normed = jnp.concatenate(
            [dot(dz_s[...], w1[i * half : (i + 1) * half, :], 1, 1) for i in range(2)], axis=1
        )
        e_s[...] = norm_step(l, h1_s[...], d_normed, g2_ref, 6).astype(BF).astype(F32)
        hook(turn, "dn2")
        have("r", l)
        up = e_s[...]
        note(l, 5, up * r_s[...])
        d_branch = (as_ref[...].astype(F32)[l : l + 1] * up).astype(BF)
        dm_s[...] = d_branch
        note(l, 4, d_branch.astype(F32))
        have("wp", l)
        if turn:
            exchange(2 * (turn - 1), do_send, do_recv).wait_send()
            exchange(2 * (turn - 1) + 1, dq_send, dq_recv).wait_send()
        for buffer, c in ((do_send, not_ci), (do_own, ci)):
            at = pl.ds(pl.multiple_of(c * half, half), half)
            value = dot(dm_s[...], wp[at, :], 1, 1)
            buffer[...] = value.reshape(images, half_slots, half).astype(BF)
            if buffer is do_send:
                exchange(2 * turn, do_send, do_recv).start()
        hook(turn, "dmix")
        arrive(turn, 2)
        rounds(turn, 2, of_first(0), 0)
        go(turn, 2)
        if turn + 1 < layers:
            begin(feed, l - 1)
        have("heads", l)
        exchange(2 * turn, do_send, do_recv).wait_recv()
        lane = lax.broadcasted_iota(jnp.int32, (2 * half_slots, 128), 1)
        factor = HEAD**-0.5

        def one_image(i, carry):
            step = turn * images + i
            slot = lax.rem(step, 2)
            shape = shape_ref[xi * images + i]

            if turn:
                store_ds(l, i, slot).wait()
            else:

                @pl.when(i >= 2)
                def _():
                    store_ds(l, i, slot).wait()

            for pair in range(half // 128):
                at = pair * 128
                q, k, v = (
                    two_sides(
                        heads_s[0, i, :, w * half + at : w * half + at + 128],
                        heads_s[1, i, :, w * half + at : w * half + at + 128],
                    )
                    for w in range(3)
                )
                g = two_sides(do_own[i, :, at : at + 128], do_recv[i, :, at : at + 128])
                dqs, dks, dvs = [], [], []
                for e in range(2):
                    own = (lane // HEAD) == e
                    qm = jnp.where(own, q, jnp.zeros_like(q))
                    gm = jnp.where(own, g, jnp.zeros_like(g))
                    s = dot(qm, k, 1, 1) * factor + bias_s[shape, 2 * pair + e]
                    ex = jnp.exp(s - jnp.max(s, axis=1, keepdims=True))
                    p = ex / jnp.sum(ex, axis=1, keepdims=True)
                    dp = dot(gm, v, 1, 1)
                    ds = (p * (dp - jnp.sum(p * dp, axis=1, keepdims=True))).astype(BF)
                    ds_s[slot, 2 * pair + e, :, 0:slots] = ds
                    dvs.append(dot(p.astype(BF), g, 0, 0))
                    dqs.append(dot(ds, k))
                    dks.append(dot(ds, q, 0, 0))
                low = lane < HEAD
                for w, (zero, one, scale) in enumerate(
                    ((dqs[0], dqs[1], factor), (dks[0], dks[1], factor), (dvs[0], dvs[1], 1.0))
                ):
                    value = jnp.where(low, zero, one) * scale
                    dq_own[i, :, w * half + at : w * half + at + 128] = value[:half_slots].astype(BF)
                    dq_send[i, :, w * half + at : w * half + at + 128] = value[half_slots:].astype(BF)
            store_ds(l, i, slot).start()

            for number in range(3):
                if (turn, "im%d" % number) in SCHEDULE:

                    @pl.when(i == number)
                    def _(number=number):
                        hook(turn, "im%d" % number)

            return carry

        load_bias(l).wait()
        hook(turn, "exch")
        lax.fori_loop(0, images, one_image, 0)
        if turn + 1 < layers:
            load_bias(l - 1).start()
        exchange(2 * turn + 1, dq_send, dq_recv).start()
        d_branch = dm_s[...].astype(F32)
        for w in range(3):
            at = pl.ds(pl.multiple_of(w * width + ci * half, half), half)
            dq_s[:, at] = dq_own[:, :, w * half : (w + 1) * half].astype(F32).reshape(rows, half).astype(BF)
        exchange(2 * turn + 1, dq_send, dq_recv).wait_recv()
        for w in range(3):
            at = pl.ds(pl.multiple_of(w * width + not_ci * half, half), half)
            dq_s[:, at] = (
                dq_recv[:, :, w * half : (w + 1) * half].astype(F32).reshape(rows, half).astype(BF)
            )
        note(l, 2, dq_s[:, 0:width].astype(F32))
        note(l, 3, dq_s[:, 2 * width : 3 * width].astype(F32))
        three = 3 * block
        for x in range(2):
            sides = []
            for c in range(2):
                s = 2 * x + c
                low, top = s * three // 128 * 128, -(-(s + 1) * three // 128) * 128
                d_part = dq_s[:, low:top].astype(F32)[:, s * three - low : (s + 1) * three - low]
                sides.append(jnp.concatenate([d_part, d_branch[:, s * block : (s + 1) * block]], axis=1))
            dz_s[:, x * width : (x + 1) * width] = mine_first(sides[0], sides[1]).astype(BF)
            dz_s[:, (2 + x) * width : (3 + x) * width] = mine_first(sides[1], sides[0]).astype(BF)
        have("n", l)
        have("o", l)

        def of_attention(side):
            def product(x, h):
                at = pl.multiple_of((2 * side + x) * width + h * half, half)
                right = dz_s[:, pl.ds(at, half)]
                if h == 0:
                    return dot(n_s[...], right, 0, 0)
                column = lax.broadcasted_iota(jnp.int32, (width, half), 1)
                return jnp.where(column < block, dot(n_s[...], right, 0, 0), dot(o_s[...], right, 0, 0))

            return product

        hook(turn, "asm")
        if turn + 1 == layers:
            for step in (layers * images - 2, layers * images - 1):
                store_ds(last - step // images, step % images, step % 2).wait()
            for done in range(layers):
                for i in range(images):
                    for copy in reload(done, i):
                        copy.start()
        rounds(turn, 4, of_attention(1), 1)
        hook(turn, "attt")
        give(turn, 4)
        have("wq", l)
        have("h", l)
        d_normed = jnp.concatenate(
            [dot(dq_s[...], wq[i * half : (i + 1) * half, :], 1, 1) for i in range(2)], axis=1
        )
        entering = norm_step(l, h_s[...], d_normed, g1_ref, 0)
        if l:
            e_s[...] = entering.astype(BF).astype(F32)
        else:
            for i in range(images):
                for x in range(2):
                    at = i * half_slots + x * (half_slots // 2)
                    value = entering[at : at + half_slots // 2]
                    dx_send[x, i] = value.astype(BF)

                    @pl.when(xi == x)
                    def _(value=value, i=i):
                        dx_ref[xi * images + i] = value

            small_sum(0).start()
        hook(turn, "dn")
        arrive(turn, 4)
        rounds(turn, 4, of_attention(0), 0)
        if turn + 1 < layers:
            begin(attend, l - 1)
        else:
            for done in range(layers):
                for i in range(images):
                    for copy in reload(done, i):
                        copy.wait()
        go(turn, 4)
    exchange(15, dx_send.at[not_xi], dx_recv, across).wait()
    for i in range(images):
        dx_ref[not_xi * images + i] = dx_recv[i].astype(F32)
    out_keep.wait()
    out_send.wait()
    exchange(2 * layers - 2, do_send, do_recv).wait_send()
    exchange(2 * layers - 1, dq_send, dq_recv).wait_send()


def backward(shape_id, saved, vectors, images):
    e_first, last_blocks, bias_all, h_all, n_all = saved[:5]
    rows, width = e_first.shape
    layers, half, half_slots = n_all.shape[0], width // 2, rows // images
    ff = saved[10].shape[2]
    heads, slots, group, part = half // HEAD, 2 * half_slots, width // 8, half_slots // 2
    hbm, vm = pl.BlockSpec(memory_space=pl.ANY), pl.BlockSpec(memory_space=pltpu.VMEM)
    shape, v = jax.ShapeDtypeStruct, pltpu.VMEM
    shapes = len(GRIDS)
    unused, targets = bias_constants(slots, part)
    scratch = [
        v((rows, width), F32), v((rows, width), BF), v((rows, width), BF), v((2, images, half_slots, 3 * half), BF),
        v((rows, width), BF), v((rows, width), F32), v((rows, width), BF), v((rows, width), BF), v((rows, ff), BF),
        v((2, rows, half), F32), v((rows, width), F32), v((width, 3 * width), BF), v((width, width), BF),
        v((width, ff), BF), v((ff, width), BF), v((shapes, heads, slots, slots), F32),
        v((rows, width), BF), v((2, rows, half), BF), v((rows, ff), BF), v((rows, 3 * width), BF),
        v((images, half_slots, half), BF), v((images, half_slots, half), BF), v((images, half_slots, half), BF),
        v((images, half_slots, 3 * half), BF), v((images, half_slots, 3 * half), BF),
        v((images, half_slots, 3 * half), BF), v((2, heads, slots, 256), BF),
        v((2, 2, 2, 2, 2, group, half), BF), v((6, 2, 2, 2, 2, group, half), BF), v((6, 2, 2, 2, group, half), BF),
        v((6, 2, 2, group, half), BF), v((6, 2, group, half), BF), v((6, group, half), BF),
        v((2, images, part, width), BF), v((images, part, width), BF), v((5, layers, 16, width), F32),
        v((4, shapes, 16, LANES), F32),
        pltpu.SemaphoreType.DMA((layers * 30 + 16,)), pltpu.SemaphoreType.DMA((layers * 30 + 16,)),
        pltpu.SemaphoreType.DMA((14,)), pltpu.SemaphoreType.DMA((1,)), pltpu.SemaphoreType.DMA((2,)),
        pltpu.SemaphoreType.DMA((2,)), pltpu.SemaphoreType.DMA((layers * images * heads,)), pltpu.SemaphoreType.DMA((2,)),
        pltpu.SemaphoreType.REGULAR((6, 5)),
    ]
    return pl.pallas_call(
        backward_kernel,
        out_shape=[
            shape((2 * images, part, width), BF),
            shape((2 * images, part, width), F32),
            shape((layers, 16, width), F32),
            shape((layers, 6, group, half), F32),
            shape((shapes, 16, LANES), F32),
            shape((shapes, 16, LANES), F32),
            shape((layers, images, heads, slots, 256), BF),
        ],
        in_specs=[SM] + [hbm] * 17 + [vm] * 5,
        out_specs=[hbm] + [vm] * 5 + [hbm],
        scratch_shapes=scratch,
        compiler_params=pltpu.CompilerParams(
            collective_id=1, has_side_effects=True, vmem_limit_bytes=61 * 2**20
        ),
    )(shape_id, *saved, *vectors, targets)


def last_kernel(ci_ref, small_ref, matrix_ref, table_ref, other_ref, idx_ref, src_ref, *outs):
    layers, unused, group, half = matrix_ref.shape
    width, block = 2 * half, half // 2
    (g1, b1, wq, qb, vb, wp, pb, sa, table, g2, b2, w1, fb, w2, mb, sm) = outs
    for ref, row in ((g1, 0), (b1, 1), (qb, 2), (vb, 3), (pb, 4), (sa, 5), (g2, 6), (b2, 7), (mb, 8), (sm, 9)):
        ref[...] = jnp.concatenate([small_ref[l, row : row + 1, :] for l in range(layers)], axis=0)
    for l in range(layers):
        for t in range(fb.shape[1] // width):
            fb[l : l + 1, t * width : (t + 1) * width] = small_ref[l, 10 + t : 11 + t, :]
        w2[l] = jnp.concatenate([matrix_ref[l, 0], matrix_ref[l, 1]], axis=0).T
        w1[l, :, 0:half] = matrix_ref[l, 2]
        w1[l, :, half:width] = matrix_ref[l, 3]
        wq[l, :, 0:half] = matrix_ref[l, 4]
        wq[l, :, half : half + block] = matrix_ref[l, 5, :, 0:block]
        wp[l] = matrix_ref[l, 5, :, block:half]
    entries, heads = table.shape[1:]
    own = heads // 2
    both = [jnp.concatenate([table_ref[s], other_ref[s]], axis=0) for s in range(len(GRIDS))]
    rows = table_rows(both, idx_ref, src_ref, entries)
    for l in range(layers):
        mine, other = rows[l * own : (l + 1) * own], rows[16 + l * own : 16 + (l + 1) * own]
        first = ci_ref[0] == 0
        both = jnp.concatenate([jnp.where(first, mine, other), jnp.where(first, other, mine)], axis=0)
        pad = jnp.concatenate([both, jnp.zeros((16 - heads, entries), F32)], axis=0)
        table[l] = pad.T[:, :heads]


def last_form(ci, d_small, d_matrix, d_table, d_other, index, entries, heads, ff):
    layers, unused, group, half = d_matrix.shape
    width, block = 2 * half, half // 2
    shape = jax.ShapeDtypeStruct
    vector = shape((layers, width), F32)
    slots = index.shape[1] // 5
    sources, unused = bias_constants(slots, slots // 4)
    outs = [
        vector, vector, shape((layers, group, 3 * block), F32), vector, vector, shape((layers, group, block), F32),
        vector, vector, shape((layers, entries, heads), F32), vector, vector, shape((layers, group, width), F32),
        shape((layers, ff), F32), shape((layers, half, block), F32), vector, vector,
    ]
    return pl.pallas_call(
        last_kernel,
        out_shape=outs,
        in_specs=[SM] + [VM] * 6,
        out_specs=[VM] * 16,
        compiler_params=pltpu.CompilerParams(vmem_limit_bytes=40 * 2**20),
    )(ci, d_small, d_matrix, d_table, d_other, index, sources)


def attn_fwd_kernel(qkv_ref, bias_ref, o_ref):
    width = o_ref.shape[2]
    slots = o_ref.shape[1]
    lane = lax.broadcasted_iota(jnp.int32, (slots, 128), 1)
    for pair in range(width // 128):
        at = pair * 128
        q = qkv_ref[0, :, at : at + 128]
        k = qkv_ref[0, :, width + at : width + at + 128]
        v = qkv_ref[0, :, 2 * width + at : 2 * width + at + 128]
        outs = []
        for e in range(2):
            own = (lane // HEAD) == e
            qm = jnp.where(own, q, jnp.zeros_like(q))
            s = dot(qm, k, 1, 1) * HEAD**-0.5 + bias_ref[0, 2 * pair + e]
            ex = jnp.exp(s - jnp.max(s, axis=1, keepdims=True))
            p = ex / jnp.sum(ex, axis=1, keepdims=True)
            outs.append(dot(p.astype(BF), v))
        o_ref[0, :, at : at + 128] = jnp.where(lane < HEAD, outs[0], outs[1]).astype(BF)


def attn_fwd(qkv, bias):
    images, slots, wide = qkv.shape
    width = wide // 3
    heads = width // HEAD
    return pl.pallas_call(
        attn_fwd_kernel,
        grid=(images,),
        in_specs=[
            pl.BlockSpec((1, slots, wide), lambda i: (i, 0, 0)),
            pl.BlockSpec((1, heads, slots, slots), lambda i: (i, 0, 0, 0)),
        ],
        out_specs=pl.BlockSpec((1, slots, width), lambda i: (i, 0, 0)),
        out_shape=jax.ShapeDtypeStruct((images, slots, width), BF),
        compiler_params=pltpu.CompilerParams(vmem_limit_bytes=48 * 2**20),
    )(qkv, bias)


def bias_kernel(part, core_ref, table_ref, idx_ref, src_ref, tgt_ref, out_ref, nat_ref, wide_ref):
    make_bias(part, core_ref[0], table_ref, idx_ref, src_ref, tgt_ref, out_ref, nat_ref, wide_ref)


def bias_of(core, table, index, part):
    layers, unused, heads = table.shape
    own, slots = layers * (heads // 2), 4 * part
    sources, targets = bias_constants(slots, part)
    return pl.pallas_call(
        functools.partial(bias_kernel, part),
        out_shape=jax.ShapeDtypeStruct((len(GRIDS), own, slots, slots), F32),
        in_specs=[SM] + [VM] * 4,
        out_specs=VM,
        scratch_shapes=[pltpu.VMEM((own, slots, slots), F32), pltpu.VMEM((own * 24, LANES), F32)],
        compiler_params=pltpu.CompilerParams(vmem_limit_bytes=56 * 2**20),
    )(core, table, index, sources, targets)


def gather_rows(own, section, yi):
    depth = own.shape[0]
    cut = depth // 2
    beside = swap(own, "section", 1)
    first = swap(lax.dynamic_slice_in_dim(own, yi * cut, cut, 0), "section", 2)
    second = swap(first, "wide", 1)
    far = jnp.concatenate([pick(yi, first, second), pick(yi, second, first)], axis=0)
    far_beside = swap(far, "section", 1)
    whole = jnp.zeros((4 * depth, own.shape[1]), own.dtype)
    for r, piece in enumerate((own, beside, far, far_beside)):
        whole = lax.dynamic_update_slice_in_dim(whole, piece, (section ^ r) * depth, 0)
    return whole


def exchange_heads(value, ci, images):
    rows, width = value.shape
    half = width // 2
    keep = pick(ci, value[:, :half], value[:, half:])
    got = swap(pick(ci, value[:, half:], value[:, :half]), "section", 1)
    shape = (images, rows // images, half)
    return jnp.concatenate([keep.reshape(shape), got.reshape(shape)], axis=1)


def restore_heads(value, ci, blocks):
    images, slots, wide = value.shape
    rows, half = images * slots // 2, wide // blocks
    keep = value[:, : slots // 2].reshape(rows, wide)
    got = swap(value[:, slots // 2 :], "section", 1).reshape(rows, wide)
    pieces = []
    for b in range(blocks):
        a, o = keep[:, b * half : (b + 1) * half], got[:, b * half : (b + 1) * half]
        pieces += [pick(ci, a, o), pick(ci, o, a)]
    return jnp.concatenate(pieces, axis=1)


def norm(hidden, gain, offset):
    return (rows_norm(hidden.astype(F32)) * gain + offset).astype(BF)


def forward_general(hidden, owns, bias, vectors, images):
    section, wide = lax.axis_index("section"), lax.axis_index("wide")
    ci, yi = section % 2, wide % 2
    layers, width = owns[0].shape[0], hidden.shape[1]
    heads = width // 2 // HEAD
    kept = []
    for l in range(layers):
        gain1, offset1, q_b, v_b, proj_b, scale_a, gain2, offset2, fc1_b, fc2_b, scale_m = (
            v[l : l + 1].astype(F32) for v in vectors
        )
        wq, wp, w1, w2 = (gather_rows(own[l], section, yi) for own in owns)
        entering = hidden
        normed = norm(hidden, gain1, offset1)
        qkv = dot(normed, wq) + jnp.concatenate([q_b, jnp.zeros_like(q_b), v_b], axis=1)
        qkv = qkv.astype(BF)
        by_head = jnp.concatenate(
            [exchange_heads(qkv[:, b * width : (b + 1) * width], ci, images) for b in range(3)], axis=2
        )
        mixed = restore_heads(attn_fwd(by_head, bias[:, l * heads : (l + 1) * heads]), ci, 1)
        branch = dot(mixed, wp) + proj_b
        middle = (hidden.astype(F32) + scale_a * branch).astype(BF)
        normed2 = norm(middle, gain2, offset2)
        pre = dot(normed2, w1) + fc1_b
        cdf = 0.5 * (1.0 + lax.erf(pre * ROOT_HALF))
        act = (pre * cdf).astype(BF)
        slope = cdf + pre * jnp.exp(-0.5 * pre * pre) * INV_ROOT_2PI
        last = dot(act, w2) + fc2_b
        hidden = (middle.astype(F32) + scale_m * last).astype(BF)
        kept.append((entering, normed, by_head, mixed, branch, middle, normed2, act, slope, last, wq, wp, w1, w2))
    return hidden, list(zip(*kept))


def attn_bwd_kernel(qkv_ref, do_ref, bias_ref, dqkv_ref, ds_ref):
    width = do_ref.shape[2]
    slots = do_ref.shape[1]
    lane = lax.broadcasted_iota(jnp.int32, (slots, 128), 1)
    factor = HEAD**-0.5
    for pair in range(width // 128):
        at = pair * 128
        q, k, v = (qkv_ref[0, :, w * width + at : w * width + at + 128] for w in range(3))
        g = do_ref[0, :, at : at + 128]
        dqs, dks, dvs = [], [], []
        for e in range(2):
            own = (lane // HEAD) == e
            qm = jnp.where(own, q, jnp.zeros_like(q))
            gm = jnp.where(own, g, jnp.zeros_like(g))
            s = dot(qm, k, 1, 1) * factor + bias_ref[0, 2 * pair + e]
            ex = jnp.exp(s - jnp.max(s, axis=1, keepdims=True))
            p = ex / jnp.sum(ex, axis=1, keepdims=True)
            dp = dot(gm, v, 1, 1)
            ds = (p * (dp - jnp.sum(p * dp, axis=1, keepdims=True))).astype(BF)
            ds_ref[0, 2 * pair + e] = ds
            dvs.append(dot(p.astype(BF), g, 0, 0))
            dqs.append(dot(ds, k))
            dks.append(dot(ds, q, 0, 0))
        low = lane < HEAD
        for w, (zero, one, scale) in enumerate(
            ((dqs[0], dqs[1], factor), (dks[0], dks[1], factor), (dvs[0], dvs[1], 1.0))
        ):
            dqkv_ref[0, :, w * width + at : w * width + at + 128] = (
                jnp.where(low, zero, one) * scale
            ).astype(BF)


def attn_bwd(qkv, d_out, bias):
    images, slots, wide = qkv.shape
    width = wide // 3
    heads = width // HEAD
    one = lambda i: (i, 0, 0)
    return pl.pallas_call(
        attn_bwd_kernel,
        grid=(images,),
        in_specs=[
            pl.BlockSpec((1, slots, wide), one),
            pl.BlockSpec((1, slots, width), one),
            pl.BlockSpec((1, heads, slots, slots), lambda i: (i, 0, 0, 0)),
        ],
        out_specs=[
            pl.BlockSpec((1, slots, wide), one),
            pl.BlockSpec((1, heads, slots, slots), lambda i: (i, 0, 0, 0)),
        ],
        out_shape=[
            jax.ShapeDtypeStruct((images, slots, wide), BF),
            jax.ShapeDtypeStruct((images, heads, slots, slots), BF),
        ],
        compiler_params=pltpu.CompilerParams(vmem_limit_bytes=48 * 2**20),
    )(qkv, d_out, bias)


def norm_back(hidden, d_normed, gain):
    hidden = hidden.astype(F32)
    centered = hidden - jnp.mean(hidden, axis=1, keepdims=True)
    inv = lax.rsqrt(jnp.mean(centered * centered, axis=1, keepdims=True) + EPS)
    xhat = centered * inv
    dx = d_normed * gain
    mean_dx = jnp.mean(dx, axis=1, keepdims=True)
    mean_dxx = jnp.mean(dx * xhat, axis=1, keepdims=True)
    step = inv * (dx - mean_dx - xhat * mean_dxx)
    return step, jnp.sum(d_normed * xhat, axis=0), jnp.sum(d_normed, axis=0)


def backward_general(upstream, saved, bias, vectors, images):
    upstream = upstream.astype(BF)
    h_all, n_all, heads_all, o_all, r_all, h1_all, n2_all, u_all, slope_all, m_all = saved[:10]
    wq, wp, w1, w2 = saved[10:]
    gain1, scale_a, gain2, scale_m = (v.astype(F32) for v in vectors)
    section, wide = lax.axis_index("section"), lax.axis_index("wide")
    xi, ci = section // 2, section % 2
    wide_count = lax.axis_size("wide")
    layers = len(n_all)
    rows, width = upstream.shape
    half, half_slots = width // 2, rows // images
    heads = half // HEAD

    def columns(value, x, c):
        size = value.shape[1] // 4
        return value[:, (2 * x + c) * size : (2 * x + c + 1) * size]

    def add(a, b):
        return (a.astype(F32) + b.astype(F32)).astype(BF)

    def core_sum(left, right):
        own = [pick(ci, columns(right, x, 0), columns(right, x, 1)) for x in range(2)]
        other = [pick(ci, columns(right, x, 1), columns(right, x, 0)) for x in range(2)]
        got = swap(dot(left, jnp.concatenate(other, axis=1), 0, 0).astype(BF), "section", 1)
        return (dot(left, jnp.concatenate(own, axis=1), 0, 0) + got.astype(F32)).astype(BF)

    def x_step(value):
        size = value.shape[1] // 2
        low, top = value[:, :size], value[:, size:]
        return add(pick(xi, low, top), swap(pick(xi, top, low), "section", 2))

    def wide_steps(value):
        group = value.shape[0] // wide_count
        bit = 1
        while bit < wide_count:
            left = wide_count // bit
            cut = value.reshape(left // 2, 2, group, value.shape[-1])
            flag = (wide // bit) % 2
            keep = lax.dynamic_index_in_dim(cut, flag, 1, keepdims=False)
            send = lax.dynamic_index_in_dim(cut, 1 - flag, 1, keepdims=False)
            value = add(keep, swap(send, "wide", bit))
            bit *= 2
        return value.reshape(group, value.shape[-1])

    def x_first(left, right):
        return wide_steps(x_step(core_sum(left, right))).astype(F32)

    def wide_first(left, right):
        return x_step(wide_steps(core_sum(left, right))).astype(F32)

    small, matrices, d_scores = [None] * layers, [None] * layers, [None] * layers
    for l in reversed(range(layers)):
        up = upstream.astype(F32)
        d_mlp_scale = jnp.sum(up * m_all[l], axis=0)
        d_branch = (scale_m[l : l + 1] * up).astype(BF)
        d_fc2_b = jnp.sum(d_branch.astype(F32), axis=0)
        d_fc2 = wide_first(u_all[l], d_branch)
        d_pre = (dot(d_branch, w2[l], 1, 1) * slope_all[l]).astype(BF)
        d_fc1_b = jnp.sum(d_pre.astype(F32), axis=0).reshape(-1, width)
        d_fc1 = x_first(n2_all[l], d_pre)
        step, d_gain2, d_offset2 = norm_back(h1_all[l], dot(d_pre, w1[l], 1, 1), gain2[l : l + 1])
        up = (up + step).astype(BF).astype(F32)
        d_attn_scale = jnp.sum(up * r_all[l], axis=0)
        d_branch = (scale_a[l : l + 1] * up).astype(BF)
        d_proj_b = jnp.sum(d_branch.astype(F32), axis=0)
        d_proj = x_first(o_all[l], d_branch)
        d_mixed = exchange_heads(dot(d_branch, wp[l], 1, 1).astype(BF), ci, images)
        d_heads, d_scores[l] = attn_bwd(heads_all[l], d_mixed, bias[:, l * heads : (l + 1) * heads])
        d_qkv = restore_heads(d_heads, ci, 3)
        d_qkv_w = x_first(n_all[l], d_qkv)
        d_qkv_b = jnp.sum(d_qkv.astype(F32), axis=0)
        step, d_gain1, d_offset1 = norm_back(h_all[l], dot(d_qkv, wq[l], 1, 1), gain1[l : l + 1])
        entering = up + step
        upstream = entering.astype(BF)
        one = [d_gain1, d_offset1, d_qkv_b[:width], d_qkv_b[2 * width :], d_proj_b, d_attn_scale]
        one += [d_gain2, d_offset2, d_fc2_b, d_mlp_scale]
        one = jnp.concatenate([jnp.stack(one), d_fc1_b])
        small[l] = jnp.pad(one, ((0, 16 - one.shape[0]), (0, 0)))
        matrices[l] = (d_qkv_w, d_proj, d_fc1, d_fc2)
    matrices = [jnp.stack(group) for group in zip(*matrices)]
    return entering, jnp.stack(small), matrices, jnp.stack(d_scores)


def fold_kernel(part, core_ref, shape_ref, ds_ref, tgt_ref, out_ref, nat_ref, acc_ref, row_ref):
    layers, images, per_layer, slots = ds_ref.shape[:4]
    for s in range(len(GRIDS)):
        here = [jnp.where(shape_ref[i] == s, 1.0, 0.0).astype(F32) for i in range(images)]

        def read(h):
            return sum(ds_ref[h // per_layer, i, h % per_layer].astype(F32) * here[i] for i in range(images))

        out_ref[s] = fold_scores(
            s, part, core_ref[0], read, tgt_ref, layers * per_layer, nat_ref, acc_ref, row_ref
        )


def fold(core, shapes, d_scores, part):
    layers, images, per_layer, slots = d_scores.shape[:4]
    heads = layers * per_layer
    unused, targets = bias_constants(slots, part)
    return pl.pallas_call(
        functools.partial(fold_kernel, part),
        out_shape=jax.ShapeDtypeStruct((len(GRIDS), 16, LANES), F32),
        in_specs=[SM] * 2 + [VM] * 2,
        out_specs=VM,
        scratch_shapes=[
            pltpu.VMEM((heads, slots, slots), F32), pltpu.VMEM((heads * 24, LANES), F32),
            pltpu.VMEM((heads * 24, slots), F32),
        ],
        compiler_params=pltpu.CompilerParams(vmem_limit_bytes=56 * 2**20),
    )(core, shapes, d_scores, targets)


def table_kernel(table_ref, idx_ref, src_ref, out_ref):
    out_ref[...] = table_rows([table_ref[s] for s in range(len(GRIDS))], idx_ref, src_ref, out_ref.shape[1])


def table_form(d_table, index, entries):
    slots = index.shape[1] // 5
    sources, unused = bias_constants(slots, slots // 4)
    return pl.pallas_call(
        table_kernel,
        out_shape=jax.ShapeDtypeStruct((d_table.shape[1], entries), F32),
        in_specs=[VM] * 3,
        out_specs=VM,
        compiler_params=pltpu.CompilerParams(vmem_limit_bytes=40 * 2**20),
    )(d_table, index, sources)


def run_general(tokens, cotangent, shape_id, owns, table, index, vectors):
    section = lax.axis_index("section")
    xi, ci = section // 2, section % 2
    all_images, part, width = tokens.shape
    images = all_images // 2
    rows = images * 2 * part
    layers, entries, heads = table.shape
    own = heads // 2
    ff = owns[2].shape[2]

    def to_images(value):
        cut = value.reshape(2, images, part, width)
        keep = lax.dynamic_index_in_dim(cut, xi, 0, keepdims=False)
        got = swap(lax.dynamic_index_in_dim(cut, 1 - xi, 0, keepdims=False), "section", 2)
        both = jnp.concatenate([pick(xi, keep, got), pick(xi, got, keep)], axis=1)
        return both.reshape(rows, width)

    def to_slots(value):
        cut = value.reshape(images, 2, part, width)
        keep = lax.dynamic_index_in_dim(cut, xi, 1, keepdims=False)
        got = swap(lax.dynamic_index_in_dim(cut, 1 - xi, 1, keepdims=False), "section", 2)
        return jnp.concatenate([pick(xi, keep, got), pick(xi, got, keep)], axis=0)

    def all_sum(value, section_bits):
        for bit in section_bits:
            value = value + swap(value, "section", bit)
        bit = 1
        while bit < lax.axis_size("wide"):
            value = value + swap(value, "wide", bit)
            bit *= 2
        return value

    core = jnp.reshape(ci, (1,)).astype(jnp.int32)
    shapes = lax.dynamic_slice_in_dim(shape_id, xi * images, images, 0)
    bias_all = bias_of(core, table, index, part)
    bias = jnp.stack([lax.dynamic_index_in_dim(bias_all, shapes[i], 0, keepdims=False) for i in range(images)])
    hidden, saved = forward_general(to_images(tokens), owns, bias, vectors, images)
    place = jnp.arange(2 * part, dtype=jnp.int32)
    slot = place + ci * part + jnp.where(place >= part, part, 0)
    counts = sum(jnp.where(shapes == s, r * c + 1, 0) for s, (r, c) in enumerate(GRIDS))
    live = (slot[None, :] < counts[:, None]).reshape(rows, 1)
    upstream = jnp.where(live, to_images(cotangent), jnp.zeros((), BF))
    scales = (vectors[0], vectors[5], vectors[6], vectors[10])
    entering, d_small, matrices, d_scores = backward_general(upstream, saved, bias, scales, images)
    d_tokens = to_slots(entering.astype(BF)).astype(F32)
    d_small = all_sum(d_small.reshape(-1, width), (1, 2)).reshape(layers, 16, width)
    d_table = all_sum(fold(core, shapes, d_scores, part).reshape(-1, LANES), (2,)).reshape(-1, 16, LANES)
    other = swap(d_table, "section", 1)
    tables = [
        table_form(t, index, entries)[: layers * own].reshape(layers, own, entries)
        for t in (pick(ci, d_table, other), pick(ci, other, d_table))
    ]
    d_table = jnp.concatenate(tables, axis=1).transpose(0, 2, 1)
    wq, wp, w1, w2 = matrices
    fb = d_small[:, 10 : 10 + ff // width].reshape(layers, ff)
    g1, b1, qb, vb, pb, sa, g2, b2, mb, sm = (d_small[:, at] for at in range(10))
    return (to_slots(hidden), d_tokens, g1, b1, wq, qb, vb, wp, pb, sa, d_table, g2, b2, w1, fb, w2, mb, sm)


def shards(
    tokens,
    cotangent,
    shape_id,
    rel_index,
    norm1_gain,
    norm1_bias,
    qkv_weight,
    q_bias,
    v_bias,
    proj_weight,
    proj_bias,
    attn_scale,
    rel_table,
    norm2_gain,
    norm2_bias,
    fc1_weight,
    fc1_bias,
    fc2_weight,
    fc2_bias,
    mlp_scale,
):
    layers, entries, heads = rel_table.shape
    all_images, part, width = tokens.shape
    images = all_images // 2
    slots = 4 * part
    ff = fc1_weight.shape[2]
    index = jnp.stack(
        [
            jnp.concatenate(
                [rel_index[s, a * slots : (a + 1) * slots] for a in (0, 1, c, 1 + (r - 1) * c, r * c)]
            )
            for s, (r, c) in enumerate(GRIDS)
        ]
    )
    vectors = (
        norm1_gain, norm1_bias, q_bias, v_bias, proj_bias, attn_scale, norm2_gain, norm2_bias, fc1_bias, fc2_bias,
        mlp_scale,
    )
    owns = (qkv_weight, proj_weight, fc1_weight, fc2_weight)
    if layers != 2 or lax.axis_size("wide") != 8 or images * 2 * part > 320:
        return run_general(tokens, cotangent, shape_id, owns, rel_table, index, vectors)
    blocks, upstream, *saved = forward(shape_id, tokens, cotangent, owns, rel_table, index, vectors)
    scales = (norm1_gain, attn_scale, norm2_gain, mlp_scale)
    saved = [upstream, blocks] + saved
    out, d_tokens, d_small, d_matrix, d_table, d_other, unused = backward(shape_id, saved, scales, images)
    core = jnp.reshape(lax.axis_index("section") % 2, (1,)).astype(jnp.int32)
    return (out, d_tokens, *last_form(core, d_small, d_matrix, d_table, d_other, index, entries, heads, ff))


def solution(mesh):
    return jax.shard_map(
        shards,
        mesh=mesh,
        in_specs=(
            P("wide", "section", None),
            P("wide", "section", None),
            P("wide"),
            P(),
            P(),
            P(),
            P(None, "section", None),
            P(),
            P(),
            P(None, "section", None),
            P(),
            P(),
            P(),
            P(),
            P(),
            P(None, "section", None),
            P(),
            P(None, "section", None),
            P(),
            P(),
        ),
        out_specs=(
            P("wide", "section", None),
            P("wide", "section", None),
            P(),
            P(),
            P(None, "wide", "section"),
            P(),
            P(),
            P(None, "wide", "section"),
            P(),
            P(),
            P(),
            P(),
            P(),
            P(None, "wide", "section"),
            P(),
            P(None, "wide", "section"),
            P(),
            P(),
        ),
        check_vma=False,
    )
```

```python
import functools

import numpy as np
import jax
import jax.numpy as jnp
from jax import lax
from jax.experimental import pallas as pl
from jax.experimental.pallas import tpu as pltpu
from jax.sharding import PartitionSpec as P

GRIDS = ((14, 14), (10, 20), (8, 24))
EPS = 1e-06
DEAD = -1e30
ROOT_HALF = 0.7071067811865476
INV_ROOT_2PI = 0.3989422804014327
HEAD = 64
BF = jnp.bfloat16
F32 = jnp.float32


def swap(value, axis, bit):
    count = lax.axis_size(axis)
    return lax.ppermute(value, axis, [(i, i ^ bit) for i in range(count)])


def pick(flag, zero, one):
    return jnp.where(flag == 0, zero, one)


def dot(a, b, ca=1, cb=0, **kw):
    return lax.dot_general(a, b, (((ca,), (cb,)), ((), ())), preferred_element_type=F32, **kw)


LANES = 768

def up8(n): return -(-n//8)*8

def offset_sources(rows, cols, slots):
    pitch, span = 2 * cols - 1, 2 * rows - 1
    source = np.full((1, LANES), -1, np.int32)
    for j in range(span):
        r, rk = (0, j - (rows - 1)) if j >= rows - 1 else (rows - 1, j)
        for t in range(pitch):
            c, ck = (0, t - (cols - 1)) if t >= cols - 1 else (cols - 1, t)
            which = 1 + (1 if r else 0) * 2 + (1 if c else 0)
            source[0, j * pitch + t] = which * slots + 1 + rk * cols + ck
    length = pitch * span
    source[0, length : length + 4] = (0, 1, slots, slots - 1)
    return source

def key_targets(rows, cols, slots):
    pitch, length = 2 * cols - 1, (2 * cols - 1) * (2 * rows - 1)
    out = np.zeros((3, slots), np.int32)
    for k in range(slots):
        if k == 0:
            out[:, k] = length + 2, 0, length
        elif k <= rows * cols:
            rk, ck = divmod(k - 1, cols)
            out[:, k] = (rows - 1 + rk) * pitch + ck, pitch, length + 1
        else:
            out[:, k] = length + 3, 0, length + 3
    return out

def lane_onehot(target, dtype):
    n = target.shape[1]
    number = lax.broadcasted_iota(jnp.int32, (LANES, n), 0)
    return jnp.where(number == target, 1.0, 0.0).astype(dtype)

def block_order(core):
    return (0, 2, 1, 3) if core == 0 else (1, 3, 0, 2)

def bias_constants(slots, part):
    sources = np.concatenate([offset_sources(r, c, slots) for r, c in GRIDS])
    natural = np.stack([key_targets(r, c, slots) for r, c in GRIDS]).reshape(3, 3, 4, part)
    targets = np.stack([natural[:, :, list(block_order(c))].reshape(3, 3, slots) for c in range(2)])
    return jnp.asarray(sources), jnp.asarray(targets)


def make_bias(part, ci, table_ref, idx_ref, src_ref, tgt_ref, out_ref, nat_ref, wide_ref, between=None):
    layers, entries, all_heads = table_ref.shape
    own = all_heads // 2
    heads, slots = out_ref.shape[1:3]
    for s, (rows, cols) in enumerate(GRIDS):
        length = (2 * cols - 1) * (2 * rows - 1)
        step = up8(cols)
        count = rows * cols + 1
        pairs = idx_ref.shape[1]
        target = jnp.where(ci == 0, tgt_ref[0, s], tgt_ref[1, s])
        number = lax.broadcasted_iota(jnp.int32, (entries, pairs), 0)
        hot = jnp.where(number == idx_ref[s : s + 1, :], 1.0, 0.0).astype(BF)
        looked = []
        for l in range(layers):
            both = dot(table_ref[l], hot, 0, 0)
            looked.append(jnp.where(ci == 0, both[:own], both[own:]))
        looked = jnp.concatenate(looked + [jnp.zeros((16 - heads, pairs), F32)], axis=0).astype(BF)
        place = lax.broadcasted_iota(jnp.int32, (pairs, LANES), 0)
        hot = jnp.where(place == src_ref[s : s + 1, :], 1.0, 0.0).astype(BF)
        offsets = dot(looked, hot)
        turned = pltpu.roll(offsets, LANES - (cols - 1), 1)
        tail = lax.broadcasted_iota(jnp.int32, (step, LANES), 1) >= length
        for h in range(heads):
            row = jnp.broadcast_to(offsets[h : h + 1], (step, LANES))
            rolled = jnp.broadcast_to(turned[h : h + 1], (step, LANES))
            rolled = pltpu.roll(rolled, 0, 1, stride=1, stride_axis=0)
            wide_ref[h * step : (h + 1) * step, :] = jnp.where(tail, row, rolled)
        shifted = wide_ref[0 : heads * step, :].astype(BF)
        for r in range(rows):
            patch = dot(shifted, lane_onehot(target[0:1] - r * target[1:2], BF))
            for h in range(heads):
                nat_ref[h, 1 + r * cols : 1 + (r + 1) * cols, :] = patch[h * step : h * step + cols]
        first = dot(offsets.astype(BF), lane_onehot(target[2:3], BF))
        live = jnp.broadcast_to(target[2:3] < length + 2, (part, slots))
        for h in range(heads):
            nat_ref[h, 0:1, :] = first[h : h + 1]
            nat_ref[h, count:, :] = jnp.broadcast_to(
                offsets[h : h + 1, length + 3 : length + 4], (slots - count, slots)
            )
        for core in range(2):

            @pl.when(ci == core)
            def _(core=core):
                for h in range(heads):
                    for j, b in enumerate(block_order(core)):
                        block = nat_ref[h, b * part : (b + 1) * part, :]
                        out_ref[s, h, j * part : (j + 1) * part, :] = jnp.where(live, block, DEAD)

        if between is not None:
            between("bias%d" % s)


def exact_dot(value, hot, ca, cb):
    high = value.astype(BF)
    rest = value - high.astype(F32)
    middle = rest.astype(BF)
    low = (rest - middle.astype(F32)).astype(BF)
    n = value.shape[0]
    out = dot(jnp.concatenate([high, middle, low], axis=0), hot, ca, cb)
    return out[:n] + (out[n : 2 * n] + out[2 * n :])


def fold_scores(s, part, ci, read, tgt_ref, heads, nat_ref, acc_ref, row_ref):
    rows, cols = GRIDS[s]
    slots = 4 * part
    length = (2 * cols - 1) * (2 * rows - 1)
    step = up8(cols)
    count = rows * cols + 1
    target = jnp.where(ci == 0, tgt_ref[0, s], tgt_ref[1, s])

    def stack(pieces):
        return jnp.concatenate(pieces + [jnp.zeros((16 - heads,) + pieces[0].shape[1:], F32)], axis=0)

    for core in range(2):

        @pl.when(ci == core)
        def _(core=core):
            for h in range(heads):
                value = read(h)
                for j, b in enumerate(block_order(core)):
                    nat_ref[h, b * part : (b + 1) * part, :] = value[j * part : (j + 1) * part]

    acc_ref[0 : heads * step, :] = jnp.zeros((heads * step, LANES), F32)
    row_ref[0 : heads * step, 0:slots] = jnp.zeros((heads * step, slots), F32)
    for r in range(rows):
        for h in range(heads):
            row_ref[h * step : h * step + cols, 0:slots] = nat_ref[h, 1 + r * cols : 1 + (r + 1) * cols, :]
        hot = lane_onehot(target[0:1] - r * target[1:2], BF)
        acc_ref[0 : heads * step, :] += dot(row_ref[0 : heads * step, 0:slots].astype(BF), hot, 1, 1)
    lane = lax.broadcasted_iota(jnp.int32, (16, LANES), 1)
    offsets = jnp.zeros((16, LANES), F32)
    for c in range(cols):
        part_c = stack([acc_ref[h * step + c : h * step + c + 1, :] for h in range(heads)])
        back = pltpu.roll(part_c, cols - 1 - c, 1)
        offsets += jnp.where(lane >= length, part_c, back)
    first = stack([nat_ref[h, 0:1, :] for h in range(heads)])
    offsets += exact_dot(first, lane_onehot(target[2:3], BF), 1, 1)
    rest = stack(
        [
            jnp.sum(jnp.sum(nat_ref[h, count:, :], axis=0, keepdims=True), axis=1, keepdims=True)
            for h in range(heads)
        ]
    )
    return offsets + jnp.where(lane == length + 3, rest, 0.0)


def table_rows(offsets, idx_ref, src_ref, entries):
    total = None
    pairs = idx_ref.shape[1]
    for s in range(len(GRIDS)):
        place = lax.broadcasted_iota(jnp.int32, (pairs, LANES), 0)
        hot = jnp.where(place == src_ref[s : s + 1, :], 1.0, 0.0).astype(BF)
        looked = exact_dot(offsets[s], hot, 1, 1)
        number = lax.broadcasted_iota(jnp.int32, (entries, pairs), 0)
        hot = jnp.where(number == idx_ref[s : s + 1, :], 1.0, 0.0).astype(BF)
        value = exact_dot(looked, hot, 1, 1)
        total = value if total is None else total + value
    return total


VM = pl.BlockSpec(memory_space=pltpu.VMEM)
SM = pl.BlockSpec(memory_space=pltpu.SMEM)


MESH = pl.DeviceIdType.MESH


def ids():
    section, wide = lax.axis_index("section"), lax.axis_index("wide")
    ci, yi = lax.rem(section, 2), lax.rem(wide, 2)
    core = {"section": section + 1 - 2 * ci}
    across = {"section": lax.rem(section + 2, 4)}
    beside = {"wide": wide + 1 - 2 * yi}
    return section, ci, yi, core, across, beside


def greet(partners):
    barrier = pltpu.get_barrier_semaphore()
    for device in partners:
        pl.semaphore_signal(barrier, inc=1, device_id=device, device_id_type=MESH)
    pl.semaphore_wait(barrier, len(partners))


class Remote:
    def __init__(self, send, recv):
        self.send, self.recv, self.used, self.open = send, recv, 0, []

    def start(self, src, dst, device):
        copy = pltpu.make_async_remote_copy(
            src_ref=src, dst_ref=dst, send_sem=self.send.at[self.used],
            recv_sem=self.recv.at[self.used], device_id=device, device_id_type=MESH,
        )
        self.used += 1
        copy.start()
        self.open.append(copy)
        return copy

    def sent(self, copy):
        if any(copy is other for other in self.open):
            copy.wait_send()
            self.open = [other for other in self.open if other is not copy]

    def finish(self):
        for copy in self.open:
            copy.wait_send()
        self.open = []


class Local:
    def __init__(self, sems):
        self.sems, self.used, self.open = sems, 0, {}

    def start(self, src, dst, name=None):
        copy = pltpu.make_async_copy(src, dst, self.sems.at[self.used])
        self.open[name if name is not None else self.used] = copy
        self.used += 1
        copy.start()

    def wait(self, name):
        if name in self.open:
            self.open.pop(name).wait()

    def finish(self):
        for name in list(self.open):
            self.wait(name)


CHUNKS = (("q", 0, 1152), ("q", 1152, 1152), ("p", 0, 768), ("1", 0, 1536), ("1", 1536, 1536), ("2", 0, 384), ("2", 384, 384))


def plan_gather(chunks, per_layer):
    layers = chunks // per_layer
    points = [("bias0", 1, 0, 0, 0), ("bias1", 2, 0, 0, 0), ("bias2", 3, 1, 0, 0)]
    for l in range(layers):
        base = l * per_layer
        clock = 22 if l == 0 else 62
        for name, after, whole in (
            ("norm1", 0, base + 2), ("qkv", 9, 0), ("swap", 11, 0), ("im0", 13, 0), ("im1", 16, 0), ("im2", 18, 0),
            ("proj", 20, base + 3), ("norm2", 23, base + 4), ("up", 26, base + 5), ("down0", 30, base + 6),
            ("down1", 32, base + 7),
        ):
            t = clock + after
            points.append((name + str(l), int((t - 12.5) / 3.5), int((t - 18) / 4), int((t - 24) / 4), whole))
    plan, a, b, d, ready = {}, 0, 0, 0, 0
    for name, want_a, want_b, want_d, whole in points:
        want_a = max(want_a, min(whole + 2, chunks)) if whole else want_a
        want_b = max(want_b, min(whole + 1, chunks)) if whole else want_b
        want_d = max(want_d, whole)
        steps = []
        while a < min(want_a, chunks) or b < min(want_b, chunks) or d < min(want_d, chunks):
            if a < min(max(want_a, want_b, want_d), chunks) and a <= b + 2:
                steps.append(("a", a))
                a += 1
            elif b < min(max(want_b, want_d), a) and b <= d + 2:
                steps.append(("b", b))
                b += 1
            elif d < min(want_d, b):
                steps.append(("d", d))
                d += 1
            elif b < a:
                steps.append(("b", b))
                b += 1
            else:
                steps.append(("a", a))
                a += 1
        while ready < whole:
            steps.append(("whole", ready))
            ready += 1
        plan[name] = steps
    return plan


class Gather:
    KINDS = ("x", "xd", "c", "y", "z", "d", "cx", "cy", "cz", "cd")

    def __init__(self, where, near, z1, own, whole, sems, local_sems, layers):
        self.section, self.ci, self.yi, self.core, self.across, self.beside = where
        self.near, self.z1 = near, z1
        self.own, self.whole, self.sems, self.local_sems = own, whole, sems, local_sems
        self.chunks = [(l,) + chunk for l in range(layers) for chunk in CHUNKS]
        self.plan = plan_gather(len(self.chunks), len(CHUNKS))
        for k in range(len(self.chunks)):
            self.copy(k, "x").start()
            if self.mode(k) == "direct":
                self.copy(k, "xd").start()
        for k in range(len(CHUNKS)):
            self.begin_core(k)

    def mode(self, k):
        if k < 2 or k == len(self.chunks) - 1:
            return "direct"
        return "even" if k % 2 == 0 else "odd"

    def kinds(self, k):
        return [q for q in self.KINDS if q != ("d" if self.mode(k) == "direct" else "xd")]

    def rows(self, name, shard, quarter=None):
        depth = self.own[name].shape[1]
        if quarter is None:
            return pl.ds(pl.multiple_of(shard * depth, depth), depth)
        number = {
            "x": 2 * self.yi + self.z1,
            "y": 2 * (1 - self.yi) + self.z1,
            "z": 2 * self.yi + 1 - self.z1,
            "d": 2 * (1 - self.yi) + 1 - self.z1,
        }[quarter]
        cut = depth // 4
        return pl.ds(pl.multiple_of(shard * depth + number * cut, cut), cut)

    def copy(self, k, kind):
        l, name, at, size = self.chunks[k]
        cols = pl.ds(at, size)
        own, whole = self.own[name], self.whole[name]
        far = lax.rem(self.section + 2, 4)
        if kind == "c":
            src, dst, device = own.at[l, :, cols], whole.at[l, self.rows(name, self.section), cols], self.core
        elif kind in ("x", "xd"):
            quarter = kind[-1]
            src = own.at[l, self.rows(name, 0, quarter), cols]
            dst, device = whole.at[l, self.rows(name, self.section, quarter), cols], self.across
        else:
            quarter = {"y": "x", "z": "x", "d": "y" if self.mode(k) == "even" else "z"}.get(kind, kind[-1])
            device = {"y": self.beside, "z": self.near}.get(kind, self.core)
            if kind == "d":
                device = self.near if self.mode(k) == "even" else self.beside
            src = dst = whole.at[l, self.rows(name, far, quarter), cols]
        at = k * len(self.KINDS) + self.KINDS.index(kind)
        return pltpu.make_async_remote_copy(
            src_ref=src, dst_ref=dst, send_sem=self.sems[0].at[at], recv_sem=self.sems[1].at[at], device_id=device,
            device_id_type=MESH,
        )

    def own_copy(self, k):
        l, name, at, size = self.chunks[k]
        cols = pl.ds(at, size)
        place = self.whole[name].at[l, self.rows(name, self.section), cols]
        return pltpu.make_async_copy(self.own[name].at[l, :, cols], place, self.local_sems.at[k])

    def begin_core(self, k):
        self.copy(k, "c").start()
        self.own_copy(k).start()

    def at(self, point):
        for step, k in self.plan[point]:
            if step == "a":
                self.copy(k, "x").wait_recv()
                for kind in ("y", "z", "cx"):
                    self.copy(k, kind).start()
                if k + len(CHUNKS) < len(self.chunks):
                    self.begin_core(k + len(CHUNKS))
            elif step == "b":
                mode = self.mode(k)
                for kind, turn in (("y", "even"), ("z", "odd")):
                    self.copy(k, kind).wait_recv()
                    if mode == turn:
                        self.copy(k, "d").start()
                    self.copy(k, "c" + kind).start()
            elif step == "d":
                self.copy(k, "xd" if self.mode(k) == "direct" else "d").wait_recv()
                self.copy(k, "cd").start()
            else:
                self.own_copy(k).wait()
                for kind in ("c", "cx", "cy", "cz", "cd"):
                    self.copy(k, kind).wait_recv()

    def finish(self):
        for k in range(len(self.chunks)):
            for kind in self.kinds(k):
                self.copy(k, kind).wait_send()


def rows_norm(value):
    centered = value - jnp.mean(value, axis=1, keepdims=True)
    return centered * lax.rsqrt(jnp.mean(centered * centered, axis=1, keepdims=True) + EPS)


def two_sides(left, right):
    return jnp.concatenate([left.astype(F32), right.astype(F32)], axis=0).astype(BF)


def forward_kernel(
    shape_ref, tokens_ref, cot_ref, q_own, p_own, f1_own, f2_own, table_ref, idx_ref, src_ref, tgt_ref,
    g1_ref, b1_ref, qb_ref, vb_ref, pb_ref, as_ref, g2_ref, b2_ref, fb_ref, mb_ref, ms_ref,
    out_ref, e_ref, bias_out, h_out, n_out, heads_out, o_out, r_out, h1_out, n2_out, u_out, slope_out, m_out,
    q_out, p_out, f1_out, f2_out,
    wq, wp, w1, w2, h_s, n_s, o_s, r_s, h1_s, n2_s, u_s, slope_s, m_s,
    own_s, send_s, recv_s, om_s, os_s, or_s, bias_s, nat_s, tok_s, cot_s,
    send_sems, recv_sems, local_sems, slope_sems, gather_send, gather_recv, gather_local,
):
    layers = q_own.shape[0]
    images, half_slots = own_s.shape[0], own_s.shape[1]
    rows, width = h_s.shape
    half = width // 2
    heads = half // HEAD
    ff = u_s.shape[1]
    part = half_slots // 2
    tile = half
    where = ids()
    section, ci, yi, core, across, beside = where
    wide = lax.axis_index("wide")
    z1 = lax.rem(wide // 2, 2)
    near = {"wide": wide + 2 - 4 * z1}
    greet((core, across, beside, near))
    remote, local = Remote(send_sems, recv_sems), Local(local_sems)
    xi = section // 2
    ours, others = pl.ds(xi * images, images), pl.ds((1 - xi) * images, images)
    tokens_sent = remote.start(tokens_ref.at[others], tok_s.at[xi], across)
    local.start(tokens_ref.at[ours], tok_s.at[xi], "tokens")
    local.start(cot_ref.at[ours], cot_s.at[xi], "cot")
    whole = {"q": wq, "p": wp, "1": w1, "2": w2}
    gather = Gather(
        where, near, z1, {"q": q_own, "p": p_own, "1": f1_own, "2": f2_own}, whole,
        (gather_send, gather_recv), gather_local, layers,
    )

    def vec(ref, l, at=slice(None)):
        return ref[:, at].astype(F32)[l : l + 1]

    def join(blocks):
        return jnp.concatenate([blocks[x, i].astype(F32) for i in range(images) for x in range(2)], axis=0)

    make_bias(part, ci, table_ref, idx_ref, src_ref, tgt_ref, bias_s, nat_s, r_s, gather.at)
    local.start(bias_s, bias_out)
    local.wait("tokens")
    tokens_sent.wait_recv()
    h_s[...] = join(tok_s).astype(BF)
    lane = lax.broadcasted_iota(jnp.int32, (2 * half_slots, 128), 1)
    for l in range(layers):
        hidden = h_s[...].astype(F32)
        local.start(h_s, h_out.at[l], "h")
        local.wait("n")
        n_s[...] = (rows_norm(hidden) * vec(g1_ref, l) + vec(b1_ref, l)).astype(BF)
        local.start(n_s, n_out.at[l], "n")
        gather.at("norm1%d" % l)
        local.start(wq.at[l], q_out.at[l], ("w", "q", l))
        if l:
            remote.sent(pending)
            local.wait("own")
        for side, buffer in ((1, send_s), (0, own_s)):
            for which in range(3):
                at = pl.multiple_of(which * width + lax.rem(ci + side, 2) * half, half)
                value = dot(n_s[...], wq[l, :, pl.ds(at, half)])
                if which != 1:
                    at = pl.multiple_of(lax.rem(ci + side, 2) * half, half)
                    value = value + vec(qb_ref if which == 0 else vb_ref, l, pl.ds(at, half))
                buffer[:, :, which * half : (which + 1) * half] = value.reshape(
                    images, half_slots, half
                ).astype(BF)
            if side:
                pending = remote.start(send_s, recv_s.at[l], core)
                gather.at("qkv%d" % l)
        local.start(own_s, heads_out.at[l, 0], "own")
        gather.at("swap%d" % l)
        pending.wait_recv()
        local.start(recv_s.at[l], heads_out.at[l, 1])
        if l:
            remote.sent(o_pending)

        def one_image(i, carry):
            shape = shape_ref[xi * images + i]
            for pair in range(half // 128):
                q, k, v = (
                    two_sides(
                        own_s[i, :, w * half + pair * 128 : w * half + pair * 128 + 128],
                        recv_s[l, i, :, w * half + pair * 128 : w * half + pair * 128 + 128],
                    )
                    for w in range(3)
                )
                outs = []
                for e in range(2):
                    qm = jnp.where((lane // HEAD) == e, q, jnp.zeros_like(q))
                    s = dot(qm, k, 1, 1) * HEAD**-0.5 + bias_s[shape, l * heads + 2 * pair + e]
                    ex = jnp.exp(s - jnp.max(s, axis=1, keepdims=True))
                    p = ex / jnp.sum(ex, axis=1, keepdims=True)
                    outs.append(dot(p.astype(BF), v))
                mixed = jnp.where(lane < HEAD, outs[0], outs[1])
                om_s[i, :, pair * 128 : pair * 128 + 128] = mixed[:half_slots].astype(BF)
                os_s[i, :, pair * 128 : pair * 128 + 128] = mixed[half_slots:].astype(BF)
            for number in range(3):

                @pl.when(i == number)
                def _(number=number):
                    gather.at("im%d%d" % (number, l))

            return carry

        lax.fori_loop(0, images, one_image, 0)
        o_pending = remote.start(os_s, or_s.at[l], core)
        local.wait("o")
        mine = pl.ds(pl.multiple_of(ci * half, half), half)
        other = pl.ds(pl.multiple_of((1 - ci) * half, half), half)
        o_s[:, mine] = om_s[...].astype(F32).reshape(rows, half).astype(BF)
        gather.at("proj%d" % l)
        local.start(wp.at[l], p_out.at[l], ("w", "p", l))
        o_pending.wait_recv()
        o_s[:, other] = or_s[l].astype(F32).reshape(rows, half).astype(BF)
        local.start(o_s, o_out.at[l], "o")
        branch = dot(o_s[...], wp[l]) + vec(pb_ref, l)
        local.wait("r")
        r_s[...] = branch
        local.start(r_s, r_out.at[l], "r")
        local.wait("h1")
        h1_s[...] = (hidden + vec(as_ref, l) * branch).astype(BF)
        local.start(h1_s, h1_out.at[l], "h1")
        local.wait("n2")
        n2_s[...] = (
            rows_norm(h1_s[...].astype(F32)) * vec(g2_ref, l) + vec(b2_ref, l)
        ).astype(BF)
        local.start(n2_s, n2_out.at[l], "n2")
        local.wait("u")

        def store_slope(t):
            at = pl.ds(pl.multiple_of(t * tile, tile), tile)
            slot = lax.rem(t, 2)
            return pltpu.make_async_copy(slope_s.at[slot], slope_out.at[l, :, at], slope_sems.at[slot])

        for piece in range(2):
            gather.at(("norm2%d", "up%d")[piece] % l)

            def one_tile(t, carry):
                at = pl.ds(pl.multiple_of(t * tile, tile), tile)
                pre = dot(n2_s[...], w1[l, :, at]) + vec(fb_ref, l, at)
                cdf = 0.5 * (1.0 + lax.erf(pre * ROOT_HALF))
                u_s[:, at] = (pre * cdf).astype(BF)

                @pl.when(t >= 2)
                def _():
                    store_slope(t).wait()

                slope_s[lax.rem(t, 2)] = cdf + pre * jnp.exp(-0.5 * pre * pre) * INV_ROOT_2PI
                store_slope(t).start()
                return carry

            count = ff // tile // 2
            lax.fori_loop(piece * count, (piece + 1) * count, one_tile, 0)
        local.start(w1.at[l], f1_out.at[l], ("w", "1", l))
        local.start(u_s, u_out.at[l], "u")
        for t in (ff // tile - 2, ff // tile - 1):
            store_slope(t).wait()
        local.wait("m")
        local.wait("h")
        for piece in range(2):
            gather.at("down%d%d" % (piece, l))
            if l == layers - 1 and piece == 0:
                cot_sent = remote.start(cot_ref.at[others], cot_s.at[xi], across)
            at = slice(piece * half, (piece + 1) * half)
            branch = dot(u_s[...], w2[l, :, at]) + vec(mb_ref, l, at)
            m_s[:, at] = branch
            h_s[:, at] = (h1_s[:, at].astype(F32) + vec(ms_ref, l, at) * branch).astype(BF)
        local.start(w2.at[l], f2_out.at[l], ("w", "2", l))
        local.start(m_s, m_out.at[l], "m")
    final = h_s[...].astype(F32)
    place = lax.broadcasted_iota(jnp.int32, (half_slots, width), 0)
    slot = place + ci * part + jnp.where(place >= part, part, 0)
    local.wait("cot")
    cot_sent.wait_recv()
    upstream = join(cot_s)
    for i in range(images):
        shape = shape_ref[xi * images + i]
        count = sum(jnp.where(shape == s, r * c + 1, 0) for s, (r, c) in enumerate(GRIDS))
        at = i * half_slots
        for x in range(2):
            out_ref[x, i] = final[at + x * part : at + (x + 1) * part].astype(BF)
        e_ref[at : at + half_slots, :] = jnp.where(slot < count, upstream[at : at + half_slots], 0.0)
    gather.finish()
    remote.finish()
    local.finish()


def forward(shape_id, tokens, cotangent, owns, table, index, vectors):
    all_images, part, width = tokens.shape
    images = all_images // 2
    rows = images * 2 * part
    layers = owns[0].shape[0]
    half = width // 2
    half_slots = 2 * part
    slots = 2 * half_slots
    ff = owns[2].shape[2]
    heads = half // HEAD
    hbm, vm = pl.BlockSpec(memory_space=pl.ANY), pl.BlockSpec(memory_space=pltpu.VMEM)
    shape = jax.ShapeDtypeStruct
    sources, targets = bias_constants(slots, part)
    outs = [
        shape((2, images, part, width), BF),
        shape((rows, width), F32),
        shape((len(GRIDS), layers * heads, slots, slots), F32),
        shape((layers, rows, width), BF),
        shape((layers, rows, width), BF),
        shape((layers, 2, images, half_slots, 3 * half), BF),
        shape((layers, rows, width), BF),
        shape((layers, rows, width), F32),
        shape((layers, rows, width), BF),
        shape((layers, rows, width), BF),
        shape((layers, rows, ff), BF),
        shape((layers, rows, ff), F32),
        shape((layers, rows, width), F32),
        shape((layers, width, 3 * width), BF),
        shape((layers, width, width), BF),
        shape((layers, width, ff), BF),
        shape((layers, ff, width), BF),
    ]
    chunks = layers * len(CHUNKS)
    remote_count = 2 * layers + 2
    scratch = [
        pltpu.VMEM((layers, width, 3 * width), BF),
        pltpu.VMEM((layers, width, width), BF),
        pltpu.VMEM((layers, width, ff), BF),
        pltpu.VMEM((layers, ff, width), BF),
        pltpu.VMEM((rows, width), BF),
        pltpu.VMEM((rows, width), BF),
        pltpu.VMEM((rows, width), BF),
        pltpu.VMEM((rows, width), F32),
        pltpu.VMEM((rows, width), BF),
        pltpu.VMEM((rows, width), BF),
        pltpu.VMEM((rows, ff), BF),
        pltpu.VMEM((2, rows, half), F32),
        pltpu.VMEM((rows, width), F32),
        pltpu.VMEM((images, half_slots, 3 * half), BF),
        pltpu.VMEM((images, half_slots, 3 * half), BF),
        pltpu.VMEM((layers, images, half_slots, 3 * half), BF),
        pltpu.VMEM((images, half_slots, half), BF),
        pltpu.VMEM((images, half_slots, half), BF),
        pltpu.VMEM((layers, images, half_slots, half), BF),
        pltpu.VMEM((len(GRIDS), layers * heads, slots, slots), F32),
        pltpu.VMEM((layers * heads, slots, slots), F32),
        pltpu.VMEM((2, images, part, width), BF),
        pltpu.VMEM((2, images, part, width), BF),
        pltpu.SemaphoreType.DMA((remote_count,)),
        pltpu.SemaphoreType.DMA((remote_count,)),
        pltpu.SemaphoreType.DMA((15 * layers + 4,)),
        pltpu.SemaphoreType.DMA((2,)),
        pltpu.SemaphoreType.DMA((chunks * 10,)),
        pltpu.SemaphoreType.DMA((chunks * 10,)),
        pltpu.SemaphoreType.DMA((chunks,)),
    ]
    return pl.pallas_call(
        forward_kernel,
        out_shape=outs,
        in_specs=[SM] + [hbm] * 6 + [vm] * 15,
        out_specs=[vm] * 2 + [hbm] * 15,
        scratch_shapes=scratch,
        compiler_params=pltpu.CompilerParams(
            collective_id=0, has_side_effects=True, vmem_limit_bytes=60 * 2**20
        ),
    )(shape_id, tokens, cotangent, *owns, table, index, sources, targets, *vectors)


SCHEDULE = {
    (0, "im0"): ((0, 1, 1),),
    (0, "im2"): ((0, 0, 1),),
    (0, "give4"): ((0, 2, 1), (0, 3, 1),),
    (0, "dn"): ((0, 1, 2), (0, 0, 2),),
    (0, "go4"): ((0, 1, 3),),
    (1, "setup"): ((0, 0, 3), (0, 3, 2), (0, 0, 4),),
    (1, "fc2t"): ((0, 2, 2), (0, 1, 4),),
    (1, "give0"): ((0, 3, 3), (0, 5, 1), (0, 4, 1),),
    (1, "dz"): ((0, 2, 3),),
    (1, "go0"): ((0, 3, 4),),
    (1, "fc1t"): ((0, 4, 2), (0, 2, 4),),
    (1, "dmix"): ((0, 5, 2),),
    (1, "exch"): ((1, 0, 1),),
    (1, "im0"): ((1, 1, 1), (0, 5, 3),),
    (1, "im1"): ((0, 4, 3),),
    (1, "attt"): ((0, 4, 4), (0, 5, 4), (1, 2, 1),),
    (1, "give4"): ((1, 1, 2), (1, 0, 2), (1, 3, 1),),
    (1, "dn"): ((1, 1, 3),),
    (1, "go4"): ((1, 2, 2), (1, 3, 2), "fold0", "small1", (1, 2, 3), (1, 0, 3), "fold2", "fold1", (1, 5, 1), (1, 4, 1), "table1", (1, 0, 4), "small2", "table2", (1, 5, 2), "small3", (1, 3, 3), "table3", (1, 2, 4), (1, 4, 2), "small4", (1, 1, 4), "table4", (1, 5, 3), "dxgo", (1, 4, 3), (1, 3, 4), "table5", "table6", (1, 5, 4), (1, 4, 4), "small5",),
}


class HeadView:
    def __init__(self, ref):
        self.ref, self.per = ref, ref.shape[1]

    def __getitem__(self, at):
        return self.ref[(at[0] // self.per, at[0] % self.per) + tuple(at[1:])]

    def __setitem__(self, at, value):
        self.ref[(at[0] // self.per, at[0] % self.per) + tuple(at[1:])] = value


def backward_kernel(
    shape_ref, e_in, last_in, bias_in, h_in, n_in, heads_in, o_in, r_in, h1_in, n2_in, u_in, slope_in, m_in, q_in, p_in, f1_in, f2_in,
    g1_ref, as_ref, g2_ref, ms_ref, tgt_ref,
    out_ref, dx_ref, small_ref, matrix_ref, table_ref, other_ref, ds_out,
    e_s, h_s, n_s, heads_s, o_s, r_s, h1_s, n2_s, u_s, slope_s, m_s, wq, wp, w1, w2, bias_s,
    dm_s, cols_s, dz_s, dq_s, do_own, do_send, do_recv, dq_own, dq_send, dq_recv, ds_s,
    theirs, total, in1, in2, in3, in4, dx_send, dx_recv, small_in, table_in,
    send_sems, recv_sems, load_sems, bias_sems, ds_sems, slope_sems, back_sems, out_sems, credit,
):
    layers = q_in.shape[0]
    images, half_slots = do_own.shape[0], do_own.shape[1]
    rows, width = e_s.shape
    half = width // 2
    heads = half // HEAD
    block = width // 4
    cut = block // 2
    tile = half
    ff = u_s.shape[1]
    section, ci, yi, core, across, beside = ids()
    wide = lax.axis_index("wide")
    xi = section // 2
    z1, z2 = lax.rem(wide // 2, 2), lax.rem(wide // 4, 2)
    not_xi, not_yi, not_z1, not_z2, not_ci = 1 - xi, 1 - yi, 1 - z1, 1 - z2, 1 - ci
    near = {"wide": wide + 2 - 4 * z1}
    far = {"wide": wide + 4 - 8 * z2}
    greet((core, across, beside, near, far))

    def partner(c, stage):
        swap_xy = (core, across, beside, near, far) if c % 2 == 0 else (core, beside, across, near, far)
        return swap_xy[stage]

    def parts(c, stage):
        if stage == 0:
            return theirs.at[c % 2], total.at[c], total.at[c]
        if c % 2 == 0:
            if stage == 1:
                return total.at[c, not_xi], total.at[c, xi], in1.at[c]
            if stage == 2:
                return total.at[c, xi, :, :, not_yi], total.at[c, xi, :, :, yi], in2.at[c]
        else:
            if stage == 1:
                return total.at[c, :, :, :, not_yi], total.at[c, :, :, :, yi], in1.at[c]
            if stage == 2:
                return total.at[c, not_xi, :, :, yi], total.at[c, xi, :, :, yi], in2.at[c]
        if stage == 3:
            return total.at[c, xi, :, not_z1, yi], total.at[c, xi, :, z1, yi], in3.at[c]
        return total.at[c, xi, not_z2, z1, yi], total.at[c, xi, z2, z1, yi], in4.at[c]

    def link(turn, c, stage):
        at = (turn * 6 + c) * 5 + stage
        src, unused, dst = parts(c, stage)
        return pltpu.make_async_remote_copy(
            src_ref=src, dst_ref=dst, send_sem=send_sems.at[at], recv_sem=recv_sems.at[at],
            device_id=partner(c, stage), device_id_type=MESH,
        )

    def launch(turn, c, stage):
        if turn:
            pl.semaphore_wait(credit.at[c, stage], 1)
        link(turn, c, stage).start()

    def advance(turn, c, stage):
        link(turn, c, stage).wait_recv()
        unused, keep, came = parts(c, stage)
        summed = keep[...].astype(F32) + came[...].astype(F32)
        if stage < 4:
            keep[...] = summed.astype(BF)
            launch(turn, c, stage + 1)
            return
        matrix_ref[layers - 1 - turn, c] = summed
        for earlier in range(1, 5):
            link(turn, c, earlier).wait_send()
        if turn + 1 < layers:
            for earlier in range(5):
                pl.semaphore_signal(
                    credit.at[c, earlier], inc=1, device_id=partner(c, earlier), device_id_type=MESH
                )

    def hook(turn, name):
        for item in SCHEDULE.get((turn, name), ()):
            if isinstance(item, str):
                extras[item]()
            else:
                advance(*item)

    extra = layers * 30

    def exchange(index, src, dst, device=core):
        return pltpu.make_async_remote_copy(
            src_ref=src, dst_ref=dst, send_sem=send_sems.at[extra + index], recv_sem=recv_sems.at[extra + index],
            device_id=device, device_id_type=MESH,
        )

    small_order, table_order = (core, near, far, beside, across), (near, far, beside, across)

    def small_sum(k):
        return exchange(4 + k, small_ref, small_in.at[k], small_order[k])

    def small_step(k):
        def run():
            small_sum(k - 1).wait()
            small_ref[...] += small_in[k - 1]
            if k < 5:
                small_sum(k).start()

        return run

    def table_sum(k):
        if k == 4:
            return exchange(9 + k, table_ref, other_ref, core)
        return exchange(9 + k, table_ref, table_in.at[k], table_order[k])

    def table_step(k):
        def run():
            if k > 1:
                table_sum(k - 2).wait()
                if k < 6:
                    table_ref[...] += table_in[k - 2]
            if k < 6:
                table_sum(k - 1).start()

        return run

    def fold_step(s):
        def run():
            here = [jnp.where(shape_ref[xi * images + i] == s, 1.0, 0.0).astype(F32) for i in range(images)]

            def read(h):
                value = None
                for i in range(images):
                    row, lane = kept_place(h // heads, i, h % heads)
                    one = w2[row : row + slots, lane : lane + slots].astype(F32) * here[i]
                    value = one if value is None else value + one
                return value

            table_ref[s] = fold_scores(
                s, half_slots // 2, ci, read, tgt_ref, layers * heads, HeadView(bias_s), r_s, m_s
            )

        return run

    extras = {"small%d" % k: small_step(k) for k in range(1, 6)}
    extras.update({"table%d" % k: table_step(k) for k in range(1, 7)})
    extras.update({"fold%d" % s: fold_step(s) for s in range(3)})
    extras["dxgo"] = lambda: exchange(15, dx_send.at[not_xi], dx_recv, across).start()
    slots = 2 * half_slots

    def kept_place(l, i, h):
        at = (l * images + i) * heads + h
        return at // 3 * slots, at % 3 * 256

    def reload(l, i):
        copies = []
        for h in range(heads):
            row, lane = kept_place(l, i, h)
            place = w2.at[pl.ds(row, slots), pl.ds(lane, 256)]
            sem = back_sems.at[(l * images + i) * heads + h]
            copies.append(pltpu.make_async_copy(ds_out.at[l, i, h], place, sem))
        return copies

    def loads(names, l):
        table = {
            "m": (m_in, m_s), "u": (u_in, u_s), "w2": (f2_in, w2), "n2": (n2_in, n2_s),
            "w1": (f1_in, w1), "h1": (h1_in, h1_s), "r": (r_in, r_s), "wp": (p_in, wp), "heads": (heads_in, heads_s),
            "o": (o_in, o_s), "n": (n_in, n_s), "wq": (q_in, wq), "h": (h_in, h_s),
        }
        order = list(table)
        return [
            pltpu.make_async_copy(table[name][0].at[l], table[name][1], load_sems.at[order.index(name)])
            for name in names
        ]

    def begin(names, l):
        for copy in loads(names, l):
            copy.start()

    def have(name, l):
        loads((name,), l)[0].wait()

    feed = ("u", "m", "w2", "n2", "w1", "h1")
    attend = ("r", "wp", "heads", "o", "n", "wq", "h")

    def load_bias(l):
        return pltpu.make_async_copy(bias_in.at[:, pl.ds(l * heads, heads)], bias_s, bias_sems.at[0])

    def load_slope(l, t, slot):
        at = pl.ds(pl.multiple_of(t * tile, tile), tile)
        return pltpu.make_async_copy(slope_in.at[l, :, at], slope_s.at[slot], slope_sems.at[slot])

    def store_ds(l, i, slot):
        return pltpu.make_async_copy(ds_s.at[slot], ds_out.at[l, i], ds_sems.at[slot])

    last = layers - 1
    begin(feed, last)
    begin(attend, last)
    load_bias(last).start()
    first_load = pltpu.make_async_copy(e_in, e_s, out_sems.at[0])
    first_load.start()
    ours, theirs_images = pl.ds(xi * images, images), pl.ds(not_xi * images, images)
    out_keep = pltpu.make_async_copy(last_in.at[xi], out_ref.at[ours], out_sems.at[1])
    out_keep.start()
    out_send = exchange(14, last_in.at[not_xi], out_ref.at[ours], across)
    out_send.start()
    first_load.wait()
    small_ref[...] = jnp.zeros_like(small_ref)

    def note(l, row, value):
        small_ref[l, row : row + 1, :] = jnp.sum(value, axis=0, keepdims=True)

    def mine_first(low, top):
        return jnp.where(ci == 0, low, top)

    def norm_step(l, hidden, d_normed, gain_ref, row):
        hidden = hidden.astype(F32)
        centered = hidden - jnp.mean(hidden, axis=1, keepdims=True)
        inv = lax.rsqrt(jnp.mean(centered * centered, axis=1, keepdims=True) + EPS)
        xhat = centered * inv
        note(l, row, d_normed * xhat)
        note(l, row + 1, d_normed)
        dx = d_normed * gain_ref[...].astype(F32)[l : l + 1]
        mean_dx = jnp.mean(dx, axis=1, keepdims=True)
        mean_dxx = jnp.mean(dx * xhat, axis=1, keepdims=True)
        return e_s[...] + inv * (dx - mean_dx - xhat * mean_dxx)

    def give(turn, c):
        launch(turn, c, 0)
        launch(turn, c + 1, 0)
        hook(turn, "give%d" % c)

    def arrive(turn, c):
        link(turn, c, 0).wait_recv()
        link(turn, c + 1, 0).wait_recv()

    def go(turn, c):
        launch(turn, c, 1)
        launch(turn, c + 1, 1)
        link(turn, c, 0).wait_send()
        link(turn, c + 1, 0).wait_send()
        hook(turn, "go%d" % c)

    def rounds(turn, c, product, side):
        for h in range(2):

            def one_x(x, carry):
                value = product(x, h).reshape(2, 2, 2, width // 8, half)
                if side:
                    theirs[h, x] = value.astype(BF)
                else:
                    total[c + h, x] = (value + total[c + h, x].astype(F32)).astype(BF)
                return carry

            lax.fori_loop(0, 2, one_x, 0)

    for turn in range(layers):
        l = last - turn
        up = e_s[...]
        d_branch = (ms_ref[...].astype(F32)[l : l + 1] * up).astype(BF)
        dm_s[...] = d_branch
        d_branch = d_branch.astype(F32)
        note(l, 8, d_branch)
        sides = [
            jnp.concatenate(
                [
                    d_branch[:, (2 * x + c) * block + h * cut : (2 * x + c) * block + (h + 1) * cut]
                    for h in range(2)
                    for x in range(2)
                ],
                axis=1,
            )
            for c in range(2)
        ]
        cols_s[0] = mine_first(sides[0], sides[1]).astype(BF)
        cols_s[1] = mine_first(sides[1], sides[0]).astype(BF)
        have("u", l)
        hook(turn, "setup")

        def by_rows(side, first):
            def one(w, carry):
                at = pl.ds(pl.multiple_of(w * tile, tile), tile)
                value = dot(cols_s[side], u_s[:, at], 0, 0)
                w2_, w1_, w0_ = w // 4, lax.rem(w // 2, 2), lax.rem(w, 2)
                for h in range(2):
                    for x in range(2):
                        piece = value[(2 * h + x) * cut : (2 * h + x + 1) * cut]
                        if side:
                            theirs[h, x, w2_, w1_, w0_] = piece.astype(BF)
                        else:
                            total[h, x, w2_, w1_, w0_] = (
                                piece + total[h, x, w2_, w1_, w0_].astype(F32)
                            ).astype(BF)
                return carry

            lax.fori_loop(0, ff // tile, one, 0)

        load_slope(l, 0, 0).start()
        by_rows(1, 0)
        hook(turn, "fc2t")
        give(turn, 0)
        have("m", l)
        note(l, 9, e_s[...] * m_s[...])
        have("w2", l)

        def one_tile(t, carry):
            at = pl.ds(pl.multiple_of(t * tile, tile), tile)
            slot = lax.rem(t, 2)

            @pl.when(t + 1 < ff // tile)
            def _():
                load_slope(l, t + 1, 1 - slot).start()

            load_slope(l, t, slot).wait()
            d_pre = (dot(dm_s[...], w2[at, :], 1, 1) * slope_s[slot]).astype(BF)
            dz_s[:, at] = d_pre
            sums = jnp.sum(d_pre.astype(F32), axis=0, keepdims=True)
            small_ref[l, pl.ds(10 + t // 2, 1), pl.ds(pl.multiple_of(lax.rem(t, 2) * tile, tile), tile)] = sums
            return carry

        lax.fori_loop(0, ff // tile, one_tile, 0)
        hook(turn, "dz")
        arrive(turn, 0)
        by_rows(0, 0)
        go(turn, 0)
        have("n2", l)

        def of_first(side):
            def product(x, h):
                c = not_ci if side else ci
                at = pl.multiple_of((2 * x + c) * width + h * half, half)
                return dot(n2_s[...], dz_s[:, pl.ds(at, half)], 0, 0)

            return product

        rounds(turn, 2, of_first(1), 1)
        hook(turn, "fc1t")
        give(turn, 2)
        have("w1", l)
        have("h1", l)
        d_normed = jnp.concatenate(
            [dot(dz_s[...], w1[i * half : (i + 1) * half, :], 1, 1) for i in range(2)], axis=1
        )
        e_s[...] = norm_step(l, h1_s[...], d_normed, g2_ref, 6).astype(BF).astype(F32)
        hook(turn, "dn2")
        have("r", l)
        up = e_s[...]
        note(l, 5, up * r_s[...])
        d_branch = (as_ref[...].astype(F32)[l : l + 1] * up).astype(BF)
        dm_s[...] = d_branch
        note(l, 4, d_branch.astype(F32))
        have("wp", l)
        if turn:
            exchange(2 * (turn - 1), do_send, do_recv).wait_send()
            exchange(2 * (turn - 1) + 1, dq_send, dq_recv).wait_send()
        for buffer, c in ((do_send, not_ci), (do_own, ci)):
            at = pl.ds(pl.multiple_of(c * half, half), half)
            value = dot(dm_s[...], wp[at, :], 1, 1)
            buffer[...] = value.reshape(images, half_slots, half).astype(BF)
            if buffer is do_send:
                exchange(2 * turn, do_send, do_recv).start()
        hook(turn, "dmix")
        arrive(turn, 2)
        rounds(turn, 2, of_first(0), 0)
        go(turn, 2)
        if turn + 1 < layers:
            begin(feed, l - 1)
        have("heads", l)
        exchange(2 * turn, do_send, do_recv).wait_recv()
        lane = lax.broadcasted_iota(jnp.int32, (2 * half_slots, 128), 1)
        factor = HEAD**-0.5

        def one_image(i, carry):
            step = turn * images + i
            slot = lax.rem(step, 2)
            shape = shape_ref[xi * images + i]

            if turn:
                store_ds(l, i, slot).wait()
            else:

                @pl.when(i >= 2)
                def _():
                    store_ds(l, i, slot).wait()

            for pair in range(half // 128):
                at = pair * 128
                q, k, v = (
                    two_sides(
                        heads_s[0, i, :, w * half + at : w * half + at + 128],
                        heads_s[1, i, :, w * half + at : w * half + at + 128],
                    )
                    for w in range(3)
                )
                g = two_sides(do_own[i, :, at : at + 128], do_recv[i, :, at : at + 128])
                dqs, dks, dvs = [], [], []
                for e in range(2):
                    own = (lane // HEAD) == e
                    qm = jnp.where(own, q, jnp.zeros_like(q))
                    gm = jnp.where(own, g, jnp.zeros_like(g))
                    s = dot(qm, k, 1, 1) * factor + bias_s[shape, 2 * pair + e]
                    ex = jnp.exp(s - jnp.max(s, axis=1, keepdims=True))
                    p = ex / jnp.sum(ex, axis=1, keepdims=True)
                    dp = dot(gm, v, 1, 1)
                    ds = (p * (dp - jnp.sum(p * dp, axis=1, keepdims=True))).astype(BF)
                    ds_s[slot, 2 * pair + e, :, 0:slots] = ds
                    dvs.append(dot(p.astype(BF), g, 0, 0))
                    dqs.append(dot(ds, k))
                    dks.append(dot(ds, q, 0, 0))
                low = lane < HEAD
                for w, (zero, one, scale) in enumerate(
                    ((dqs[0], dqs[1], factor), (dks[0], dks[1], factor), (dvs[0], dvs[1], 1.0))
                ):
                    value = jnp.where(low, zero, one) * scale
                    dq_own[i, :, w * half + at : w * half + at + 128] = value[:half_slots].astype(BF)
                    dq_send[i, :, w * half + at : w * half + at + 128] = value[half_slots:].astype(BF)
            store_ds(l, i, slot).start()

            for number in range(3):
                if (turn, "im%d" % number) in SCHEDULE:

                    @pl.when(i == number)
                    def _(number=number):
                        hook(turn, "im%d" % number)

            return carry

        load_bias(l).wait()
        hook(turn, "exch")
        lax.fori_loop(0, images, one_image, 0)
        if turn + 1 < layers:
            load_bias(l - 1).start()
        exchange(2 * turn + 1, dq_send, dq_recv).start()
        d_branch = dm_s[...].astype(F32)
        for w in range(3):
            at = pl.ds(pl.multiple_of(w * width + ci * half, half), half)
            dq_s[:, at] = dq_own[:, :, w * half : (w + 1) * half].astype(F32).reshape(rows, half).astype(BF)
        exchange(2 * turn + 1, dq_send, dq_recv).wait_recv()
        for w in range(3):
            at = pl.ds(pl.multiple_of(w * width + not_ci * half, half), half)
            dq_s[:, at] = (
                dq_recv[:, :, w * half : (w + 1) * half].astype(F32).reshape(rows, half).astype(BF)
            )
        note(l, 2, dq_s[:, 0:width].astype(F32))
        note(l, 3, dq_s[:, 2 * width : 3 * width].astype(F32))
        three = 3 * block
        for x in range(2):
            sides = []
            for c in range(2):
                s = 2 * x + c
                low, top = s * three // 128 * 128, -(-(s + 1) * three // 128) * 128
                d_part = dq_s[:, low:top].astype(F32)[:, s * three - low : (s + 1) * three - low]
                sides.append(jnp.concatenate([d_part, d_branch[:, s * block : (s + 1) * block]], axis=1))
            dz_s[:, x * width : (x + 1) * width] = mine_first(sides[0], sides[1]).astype(BF)
            dz_s[:, (2 + x) * width : (3 + x) * width] = mine_first(sides[1], sides[0]).astype(BF)
        have("n", l)
        have("o", l)

        def of_attention(side):
            def product(x, h):
                at = pl.multiple_of((2 * side + x) * width + h * half, half)
                right = dz_s[:, pl.ds(at, half)]
                if h == 0:
                    return dot(n_s[...], right, 0, 0)
                column = lax.broadcasted_iota(jnp.int32, (width, half), 1)
                return jnp.where(column < block, dot(n_s[...], right, 0, 0), dot(o_s[...], right, 0, 0))

            return product

        hook(turn, "asm")
        if turn + 1 == layers:
            for step in (layers * images - 2, layers * images - 1):
                store_ds(last - step // images, step % images, step % 2).wait()
            for done in range(layers):
                for i in range(images):
                    for copy in reload(done, i):
                        copy.start()
        rounds(turn, 4, of_attention(1), 1)
        hook(turn, "attt")
        give(turn, 4)
        have("wq", l)
        have("h", l)
        d_normed = jnp.concatenate(
            [dot(dq_s[...], wq[i * half : (i + 1) * half, :], 1, 1) for i in range(2)], axis=1
        )
        entering = norm_step(l, h_s[...], d_normed, g1_ref, 0)
        if l:
            e_s[...] = entering.astype(BF).astype(F32)
        else:
            for i in range(images):
                for x in range(2):
                    at = i * half_slots + x * (half_slots // 2)
                    value = entering[at : at + half_slots // 2]
                    dx_send[x, i] = value.astype(BF)

                    @pl.when(xi == x)
                    def _(value=value, i=i):
                        dx_ref[xi * images + i] = value

            small_sum(0).start()
        hook(turn, "dn")
        arrive(turn, 4)
        rounds(turn, 4, of_attention(0), 0)
        if turn + 1 < layers:
            begin(attend, l - 1)
        else:
            for done in range(layers):
                for i in range(images):
                    for copy in reload(done, i):
                        copy.wait()
        go(turn, 4)
    exchange(15, dx_send.at[not_xi], dx_recv, across).wait()
    for i in range(images):
        dx_ref[not_xi * images + i] = dx_recv[i].astype(F32)
    out_keep.wait()
    out_send.wait()
    exchange(2 * layers - 2, do_send, do_recv).wait_send()
    exchange(2 * layers - 1, dq_send, dq_recv).wait_send()


def backward(shape_id, saved, vectors, images):
    e_first, last_blocks, bias_all, h_all, n_all = saved[:5]
    rows, width = e_first.shape
    layers, half, half_slots = n_all.shape[0], width // 2, rows // images
    ff = saved[10].shape[2]
    heads, slots, group, part = half // HEAD, 2 * half_slots, width // 8, half_slots // 2
    hbm, vm = pl.BlockSpec(memory_space=pl.ANY), pl.BlockSpec(memory_space=pltpu.VMEM)
    shape, v = jax.ShapeDtypeStruct, pltpu.VMEM
    shapes = len(GRIDS)
    unused, targets = bias_constants(slots, part)
    scratch = [
        v((rows, width), F32), v((rows, width), BF), v((rows, width), BF), v((2, images, half_slots, 3 * half), BF),
        v((rows, width), BF), v((rows, width), F32), v((rows, width), BF), v((rows, width), BF), v((rows, ff), BF),
        v((2, rows, half), F32), v((rows, width), F32), v((width, 3 * width), BF), v((width, width), BF),
        v((width, ff), BF), v((ff, width), BF), v((shapes, heads, slots, slots), F32),
        v((rows, width), BF), v((2, rows, half), BF), v((rows, ff), BF), v((rows, 3 * width), BF),
        v((images, half_slots, half), BF), v((images, half_slots, half), BF), v((images, half_slots, half), BF),
        v((images, half_slots, 3 * half), BF), v((images, half_slots, 3 * half), BF),
        v((images, half_slots, 3 * half), BF), v((2, heads, slots, 256), BF),
        v((2, 2, 2, 2, 2, group, half), BF), v((6, 2, 2, 2, 2, group, half), BF), v((6, 2, 2, 2, group, half), BF),
        v((6, 2, 2, group, half), BF), v((6, 2, group, half), BF), v((6, group, half), BF),
        v((2, images, part, width), BF), v((images, part, width), BF), v((5, layers, 16, width), F32),
        v((4, shapes, 16, LANES), F32),
        pltpu.SemaphoreType.DMA((layers * 30 + 16,)), pltpu.SemaphoreType.DMA((layers * 30 + 16,)),
        pltpu.SemaphoreType.DMA((14,)), pltpu.SemaphoreType.DMA((1,)), pltpu.SemaphoreType.DMA((2,)),
        pltpu.SemaphoreType.DMA((2,)), pltpu.SemaphoreType.DMA((layers * images * heads,)), pltpu.SemaphoreType.DMA((2,)),
        pltpu.SemaphoreType.REGULAR((6, 5)),
    ]
    return pl.pallas_call(
        backward_kernel,
        out_shape=[
            shape((2 * images, part, width), BF),
            shape((2 * images, part, width), F32),
            shape((layers, 16, width), F32),
            shape((layers, 6, group, half), F32),
            shape((shapes, 16, LANES), F32),
            shape((shapes, 16, LANES), F32),
            shape((layers, images, heads, slots, 256), BF),
        ],
        in_specs=[SM] + [hbm] * 17 + [vm] * 5,
        out_specs=[hbm] + [vm] * 5 + [hbm],
        scratch_shapes=scratch,
        compiler_params=pltpu.CompilerParams(
            collective_id=1, has_side_effects=True, vmem_limit_bytes=61 * 2**20
        ),
    )(shape_id, *saved, *vectors, targets)


def last_kernel(ci_ref, small_ref, matrix_ref, table_ref, other_ref, idx_ref, src_ref, *outs):
    layers, unused, group, half = matrix_ref.shape
    width, block = 2 * half, half // 2
    (g1, b1, wq, qb, vb, wp, pb, sa, table, g2, b2, w1, fb, w2, mb, sm) = outs
    for ref, row in ((g1, 0), (b1, 1), (qb, 2), (vb, 3), (pb, 4), (sa, 5), (g2, 6), (b2, 7), (mb, 8), (sm, 9)):
        ref[...] = jnp.concatenate([small_ref[l, row : row + 1, :] for l in range(layers)], axis=0)
    for l in range(layers):
        for t in range(fb.shape[1] // width):
            fb[l : l + 1, t * width : (t + 1) * width] = small_ref[l, 10 + t : 11 + t, :]
        w2[l] = jnp.concatenate([matrix_ref[l, 0], matrix_ref[l, 1]], axis=0).T
        w1[l, :, 0:half] = matrix_ref[l, 2]
        w1[l, :, half:width] = matrix_ref[l, 3]
        wq[l, :, 0:half] = matrix_ref[l, 4]
        wq[l, :, half : half + block] = matrix_ref[l, 5, :, 0:block]
        wp[l] = matrix_ref[l, 5, :, block:half]
    entries, heads = table.shape[1:]
    own = heads // 2
    both = [jnp.concatenate([table_ref[s], other_ref[s]], axis=0) for s in range(len(GRIDS))]
    rows = table_rows(both, idx_ref, src_ref, entries)
    for l in range(layers):
        mine, other = rows[l * own : (l + 1) * own], rows[16 + l * own : 16 + (l + 1) * own]
        first = ci_ref[0] == 0
        both = jnp.concatenate([jnp.where(first, mine, other), jnp.where(first, other, mine)], axis=0)
        pad = jnp.concatenate([both, jnp.zeros((16 - heads, entries), F32)], axis=0)
        table[l] = pad.T[:, :heads]


def last_form(ci, d_small, d_matrix, d_table, d_other, index, entries, heads, ff):
    layers, unused, group, half = d_matrix.shape
    width, block = 2 * half, half // 2
    shape = jax.ShapeDtypeStruct
    vector = shape((layers, width), F32)
    slots = index.shape[1] // 5
    sources, unused = bias_constants(slots, slots // 4)
    outs = [
        vector, vector, shape((layers, group, 3 * block), F32), vector, vector, shape((layers, group, block), F32),
        vector, vector, shape((layers, entries, heads), F32), vector, vector, shape((layers, group, width), F32),
        shape((layers, ff), F32), shape((layers, half, block), F32), vector, vector,
    ]
    return pl.pallas_call(
        last_kernel,
        out_shape=outs,
        in_specs=[SM] + [VM] * 6,
        out_specs=[VM] * 16,
        compiler_params=pltpu.CompilerParams(vmem_limit_bytes=40 * 2**20),
    )(ci, d_small, d_matrix, d_table, d_other, index, sources)


def attn_fwd_kernel(qkv_ref, bias_ref, o_ref):
    width = o_ref.shape[2]
    slots = o_ref.shape[1]
    lane = lax.broadcasted_iota(jnp.int32, (slots, 128), 1)
    for pair in range(width // 128):
        at = pair * 128
        q = qkv_ref[0, :, at : at + 128]
        k = qkv_ref[0, :, width + at : width + at + 128]
        v = qkv_ref[0, :, 2 * width + at : 2 * width + at + 128]
        outs = []
        for e in range(2):
            own = (lane // HEAD) == e
            qm = jnp.where(own, q, jnp.zeros_like(q))
            s = dot(qm, k, 1, 1) * HEAD**-0.5 + bias_ref[0, 2 * pair + e]
            ex = jnp.exp(s - jnp.max(s, axis=1, keepdims=True))
            p = ex / jnp.sum(ex, axis=1, keepdims=True)
            outs.append(dot(p.astype(BF), v))
        o_ref[0, :, at : at + 128] = jnp.where(lane < HEAD, outs[0], outs[1]).astype(BF)


def attn_fwd(qkv, bias):
    images, slots, wide = qkv.shape
    width = wide // 3
    heads = width // HEAD
    return pl.pallas_call(
        attn_fwd_kernel,
        grid=(images,),
        in_specs=[
            pl.BlockSpec((1, slots, wide), lambda i: (i, 0, 0)),
            pl.BlockSpec((1, heads, slots, slots), lambda i: (i, 0, 0, 0)),
        ],
        out_specs=pl.BlockSpec((1, slots, width), lambda i: (i, 0, 0)),
        out_shape=jax.ShapeDtypeStruct((images, slots, width), BF),
        compiler_params=pltpu.CompilerParams(vmem_limit_bytes=48 * 2**20),
    )(qkv, bias)


def bias_kernel(part, core_ref, table_ref, idx_ref, src_ref, tgt_ref, out_ref, nat_ref, wide_ref):
    make_bias(part, core_ref[0], table_ref, idx_ref, src_ref, tgt_ref, out_ref, nat_ref, wide_ref)


def bias_of(core, table, index, part):
    layers, unused, heads = table.shape
    own, slots = layers * (heads // 2), 4 * part
    sources, targets = bias_constants(slots, part)
    return pl.pallas_call(
        functools.partial(bias_kernel, part),
        out_shape=jax.ShapeDtypeStruct((len(GRIDS), own, slots, slots), F32),
        in_specs=[SM] + [VM] * 4,
        out_specs=VM,
        scratch_shapes=[pltpu.VMEM((own, slots, slots), F32), pltpu.VMEM((own * 24, LANES), F32)],
        compiler_params=pltpu.CompilerParams(vmem_limit_bytes=56 * 2**20),
    )(core, table, index, sources, targets)


def gather_rows(own, section, yi):
    depth = own.shape[0]
    cut = depth // 2
    beside = swap(own, "section", 1)
    first = swap(lax.dynamic_slice_in_dim(own, yi * cut, cut, 0), "section", 2)
    second = swap(first, "wide", 1)
    far = jnp.concatenate([pick(yi, first, second), pick(yi, second, first)], axis=0)
    far_beside = swap(far, "section", 1)
    whole = jnp.zeros((4 * depth, own.shape[1]), own.dtype)
    for r, piece in enumerate((own, beside, far, far_beside)):
        whole = lax.dynamic_update_slice_in_dim(whole, piece, (section ^ r) * depth, 0)
    return whole


def exchange_heads(value, ci, images):
    rows, width = value.shape
    half = width // 2
    keep = pick(ci, value[:, :half], value[:, half:])
    got = swap(pick(ci, value[:, half:], value[:, :half]), "section", 1)
    shape = (images, rows // images, half)
    return jnp.concatenate([keep.reshape(shape), got.reshape(shape)], axis=1)


def restore_heads(value, ci, blocks):
    images, slots, wide = value.shape
    rows, half = images * slots // 2, wide // blocks
    keep = value[:, : slots // 2].reshape(rows, wide)
    got = swap(value[:, slots // 2 :], "section", 1).reshape(rows, wide)
    pieces = []
    for b in range(blocks):
        a, o = keep[:, b * half : (b + 1) * half], got[:, b * half : (b + 1) * half]
        pieces += [pick(ci, a, o), pick(ci, o, a)]
    return jnp.concatenate(pieces, axis=1)


def norm(hidden, gain, offset):
    return (rows_norm(hidden.astype(F32)) * gain + offset).astype(BF)


def forward_general(hidden, owns, bias, vectors, images):
    section, wide = lax.axis_index("section"), lax.axis_index("wide")
    ci, yi = section % 2, wide % 2
    layers, width = owns[0].shape[0], hidden.shape[1]
    heads = width // 2 // HEAD
    kept = []
    for l in range(layers):
        gain1, offset1, q_b, v_b, proj_b, scale_a, gain2, offset2, fc1_b, fc2_b, scale_m = (
            v[l : l + 1].astype(F32) for v in vectors
        )
        wq, wp, w1, w2 = (gather_rows(own[l], section, yi) for own in owns)
        entering = hidden
        normed = norm(hidden, gain1, offset1)
        qkv = dot(normed, wq) + jnp.concatenate([q_b, jnp.zeros_like(q_b), v_b], axis=1)
        qkv = qkv.astype(BF)
        by_head = jnp.concatenate(
            [exchange_heads(qkv[:, b * width : (b + 1) * width], ci, images) for b in range(3)], axis=2
        )
        mixed = restore_heads(attn_fwd(by_head, bias[:, l * heads : (l + 1) * heads]), ci, 1)
        branch = dot(mixed, wp) + proj_b
        middle = (hidden.astype(F32) + scale_a * branch).astype(BF)
        normed2 = norm(middle, gain2, offset2)
        pre = dot(normed2, w1) + fc1_b
        cdf = 0.5 * (1.0 + lax.erf(pre * ROOT_HALF))
        act = (pre * cdf).astype(BF)
        slope = cdf + pre * jnp.exp(-0.5 * pre * pre) * INV_ROOT_2PI
        last = dot(act, w2) + fc2_b
        hidden = (middle.astype(F32) + scale_m * last).astype(BF)
        kept.append((entering, normed, by_head, mixed, branch, middle, normed2, act, slope, last, wq, wp, w1, w2))
    return hidden, list(zip(*kept))


def attn_bwd_kernel(qkv_ref, do_ref, bias_ref, dqkv_ref, ds_ref):
    width = do_ref.shape[2]
    slots = do_ref.shape[1]
    lane = lax.broadcasted_iota(jnp.int32, (slots, 128), 1)
    factor = HEAD**-0.5
    for pair in range(width // 128):
        at = pair * 128
        q, k, v = (qkv_ref[0, :, w * width + at : w * width + at + 128] for w in range(3))
        g = do_ref[0, :, at : at + 128]
        dqs, dks, dvs = [], [], []
        for e in range(2):
            own = (lane // HEAD) == e
            qm = jnp.where(own, q, jnp.zeros_like(q))
            gm = jnp.where(own, g, jnp.zeros_like(g))
            s = dot(qm, k, 1, 1) * factor + bias_ref[0, 2 * pair + e]
            ex = jnp.exp(s - jnp.max(s, axis=1, keepdims=True))
            p = ex / jnp.sum(ex, axis=1, keepdims=True)
            dp = dot(gm, v, 1, 1)
            ds = (p * (dp - jnp.sum(p * dp, axis=1, keepdims=True))).astype(BF)
            ds_ref[0, 2 * pair + e] = ds
            dvs.append(dot(p.astype(BF), g, 0, 0))
            dqs.append(dot(ds, k))
            dks.append(dot(ds, q, 0, 0))
        low = lane < HEAD
        for w, (zero, one, scale) in enumerate(
            ((dqs[0], dqs[1], factor), (dks[0], dks[1], factor), (dvs[0], dvs[1], 1.0))
        ):
            dqkv_ref[0, :, w * width + at : w * width + at + 128] = (
                jnp.where(low, zero, one) * scale
            ).astype(BF)


def attn_bwd(qkv, d_out, bias):
    images, slots, wide = qkv.shape
    width = wide // 3
    heads = width // HEAD
    one = lambda i: (i, 0, 0)
    return pl.pallas_call(
        attn_bwd_kernel,
        grid=(images,),
        in_specs=[
            pl.BlockSpec((1, slots, wide), one),
            pl.BlockSpec((1, slots, width), one),
            pl.BlockSpec((1, heads, slots, slots), lambda i: (i, 0, 0, 0)),
        ],
        out_specs=[
            pl.BlockSpec((1, slots, wide), one),
            pl.BlockSpec((1, heads, slots, slots), lambda i: (i, 0, 0, 0)),
        ],
        out_shape=[
            jax.ShapeDtypeStruct((images, slots, wide), BF),
            jax.ShapeDtypeStruct((images, heads, slots, slots), BF),
        ],
        compiler_params=pltpu.CompilerParams(vmem_limit_bytes=48 * 2**20),
    )(qkv, d_out, bias)


def norm_back(hidden, d_normed, gain):
    hidden = hidden.astype(F32)
    centered = hidden - jnp.mean(hidden, axis=1, keepdims=True)
    inv = lax.rsqrt(jnp.mean(centered * centered, axis=1, keepdims=True) + EPS)
    xhat = centered * inv
    dx = d_normed * gain
    mean_dx = jnp.mean(dx, axis=1, keepdims=True)
    mean_dxx = jnp.mean(dx * xhat, axis=1, keepdims=True)
    step = inv * (dx - mean_dx - xhat * mean_dxx)
    return step, jnp.sum(d_normed * xhat, axis=0), jnp.sum(d_normed, axis=0)


def backward_general(upstream, saved, bias, vectors, images):
    upstream = upstream.astype(BF)
    h_all, n_all, heads_all, o_all, r_all, h1_all, n2_all, u_all, slope_all, m_all = saved[:10]
    wq, wp, w1, w2 = saved[10:]
    gain1, scale_a, gain2, scale_m = (v.astype(F32) for v in vectors)
    section, wide = lax.axis_index("section"), lax.axis_index("wide")
    xi, ci = section // 2, section % 2
    wide_count = lax.axis_size("wide")
    layers = len(n_all)
    rows, width = upstream.shape
    half, half_slots = width // 2, rows // images
    heads = half // HEAD

    def columns(value, x, c):
        size = value.shape[1] // 4
        return value[:, (2 * x + c) * size : (2 * x + c + 1) * size]

    def add(a, b):
        return (a.astype(F32) + b.astype(F32)).astype(BF)

    def core_sum(left, right):
        own = [pick(ci, columns(right, x, 0), columns(right, x, 1)) for x in range(2)]
        other = [pick(ci, columns(right, x, 1), columns(right, x, 0)) for x in range(2)]
        got = swap(dot(left, jnp.concatenate(other, axis=1), 0, 0).astype(BF), "section", 1)
        return (dot(left, jnp.concatenate(own, axis=1), 0, 0) + got.astype(F32)).astype(BF)

    def x_step(value):
        size = value.shape[1] // 2
        low, top = value[:, :size], value[:, size:]
        return add(pick(xi, low, top), swap(pick(xi, top, low), "section", 2))

    def wide_steps(value):
        group = value.shape[0] // wide_count
        bit = 1
        while bit < wide_count:
            left = wide_count // bit
            cut = value.reshape(left // 2, 2, group, value.shape[-1])
            flag = (wide // bit) % 2
            keep = lax.dynamic_index_in_dim(cut, flag, 1, keepdims=False)
            send = lax.dynamic_index_in_dim(cut, 1 - flag, 1, keepdims=False)
            value = add(keep, swap(send, "wide", bit))
            bit *= 2
        return value.reshape(group, value.shape[-1])

    def x_first(left, right):
        return wide_steps(x_step(core_sum(left, right))).astype(F32)

    def wide_first(left, right):
        return x_step(wide_steps(core_sum(left, right))).astype(F32)

    small, matrices, d_scores = [None] * layers, [None] * layers, [None] * layers
    for l in reversed(range(layers)):
        up = upstream.astype(F32)
        d_mlp_scale = jnp.sum(up * m_all[l], axis=0)
        d_branch = (scale_m[l : l + 1] * up).astype(BF)
        d_fc2_b = jnp.sum(d_branch.astype(F32), axis=0)
        d_fc2 = wide_first(u_all[l], d_branch)
        d_pre = (dot(d_branch, w2[l], 1, 1) * slope_all[l]).astype(BF)
        d_fc1_b = jnp.sum(d_pre.astype(F32), axis=0).reshape(-1, width)
        d_fc1 = x_first(n2_all[l], d_pre)
        step, d_gain2, d_offset2 = norm_back(h1_all[l], dot(d_pre, w1[l], 1, 1), gain2[l : l + 1])
        up = (up + step).astype(BF).astype(F32)
        d_attn_scale = jnp.sum(up * r_all[l], axis=0)
        d_branch = (scale_a[l : l + 1] * up).astype(BF)
        d_proj_b = jnp.sum(d_branch.astype(F32), axis=0)
        d_proj = x_first(o_all[l], d_branch)
        d_mixed = exchange_heads(dot(d_branch, wp[l], 1, 1).astype(BF), ci, images)
        d_heads, d_scores[l] = attn_bwd(heads_all[l], d_mixed, bias[:, l * heads : (l + 1) * heads])
        d_qkv = restore_heads(d_heads, ci, 3)
        d_qkv_w = x_first(n_all[l], d_qkv)
        d_qkv_b = jnp.sum(d_qkv.astype(F32), axis=0)
        step, d_gain1, d_offset1 = norm_back(h_all[l], dot(d_qkv, wq[l], 1, 1), gain1[l : l + 1])
        entering = up + step
        upstream = entering.astype(BF)
        one = [d_gain1, d_offset1, d_qkv_b[:width], d_qkv_b[2 * width :], d_proj_b, d_attn_scale]
        one += [d_gain2, d_offset2, d_fc2_b, d_mlp_scale]
        one = jnp.concatenate([jnp.stack(one), d_fc1_b])
        small[l] = jnp.pad(one, ((0, 16 - one.shape[0]), (0, 0)))
        matrices[l] = (d_qkv_w, d_proj, d_fc1, d_fc2)
    matrices = [jnp.stack(group) for group in zip(*matrices)]
    return entering, jnp.stack(small), matrices, jnp.stack(d_scores)


def fold_kernel(part, core_ref, shape_ref, ds_ref, tgt_ref, out_ref, nat_ref, acc_ref, row_ref):
    layers, images, per_layer, slots = ds_ref.shape[:4]
    for s in range(len(GRIDS)):
        here = [jnp.where(shape_ref[i] == s, 1.0, 0.0).astype(F32) for i in range(images)]

        def read(h):
            return sum(ds_ref[h // per_layer, i, h % per_layer].astype(F32) * here[i] for i in range(images))

        out_ref[s] = fold_scores(
            s, part, core_ref[0], read, tgt_ref, layers * per_layer, nat_ref, acc_ref, row_ref
        )


def fold(core, shapes, d_scores, part):
    layers, images, per_layer, slots = d_scores.shape[:4]
    heads = layers * per_layer
    unused, targets = bias_constants(slots, part)
    return pl.pallas_call(
        functools.partial(fold_kernel, part),
        out_shape=jax.ShapeDtypeStruct((len(GRIDS), 16, LANES), F32),
        in_specs=[SM] * 2 + [VM] * 2,
        out_specs=VM,
        scratch_shapes=[
            pltpu.VMEM((heads, slots, slots), F32), pltpu.VMEM((heads * 24, LANES), F32),
            pltpu.VMEM((heads * 24, slots), F32),
        ],
        compiler_params=pltpu.CompilerParams(vmem_limit_bytes=56 * 2**20),
    )(core, shapes, d_scores, targets)


def table_kernel(table_ref, idx_ref, src_ref, out_ref):
    out_ref[...] = table_rows([table_ref[s] for s in range(len(GRIDS))], idx_ref, src_ref, out_ref.shape[1])


def table_form(d_table, index, entries):
    slots = index.shape[1] // 5
    sources, unused = bias_constants(slots, slots // 4)
    return pl.pallas_call(
        table_kernel,
        out_shape=jax.ShapeDtypeStruct((d_table.shape[1], entries), F32),
        in_specs=[VM] * 3,
        out_specs=VM,
        compiler_params=pltpu.CompilerParams(vmem_limit_bytes=40 * 2**20),
    )(d_table, index, sources)


def run_general(tokens, cotangent, shape_id, owns, table, index, vectors):
    section = lax.axis_index("section")
    xi, ci = section // 2, section % 2
    all_images, part, width = tokens.shape
    images = all_images // 2
    rows = images * 2 * part
    layers, entries, heads = table.shape
    own = heads // 2
    ff = owns[2].shape[2]

    def to_images(value):
        cut = value.reshape(2, images, part, width)
        keep = lax.dynamic_index_in_dim(cut, xi, 0, keepdims=False)
        got = swap(lax.dynamic_index_in_dim(cut, 1 - xi, 0, keepdims=False), "section", 2)
        both = jnp.concatenate([pick(xi, keep, got), pick(xi, got, keep)], axis=1)
        return both.reshape(rows, width)

    def to_slots(value):
        cut = value.reshape(images, 2, part, width)
        keep = lax.dynamic_index_in_dim(cut, xi, 1, keepdims=False)
        got = swap(lax.dynamic_index_in_dim(cut, 1 - xi, 1, keepdims=False), "section", 2)
        return jnp.concatenate([pick(xi, keep, got), pick(xi, got, keep)], axis=0)

    def all_sum(value, section_bits):
        for bit in section_bits:
            value = value + swap(value, "section", bit)
        bit = 1
        while bit < lax.axis_size("wide"):
            value = value + swap(value, "wide", bit)
            bit *= 2
        return value

    core = jnp.reshape(ci, (1,)).astype(jnp.int32)
    shapes = lax.dynamic_slice_in_dim(shape_id, xi * images, images, 0)
    bias_all = bias_of(core, table, index, part)
    bias = jnp.stack([lax.dynamic_index_in_dim(bias_all, shapes[i], 0, keepdims=False) for i in range(images)])
    hidden, saved = forward_general(to_images(tokens), owns, bias, vectors, images)
    place = jnp.arange(2 * part, dtype=jnp.int32)
    slot = place + ci * part + jnp.where(place >= part, part, 0)
    counts = sum(jnp.where(shapes == s, r * c + 1, 0) for s, (r, c) in enumerate(GRIDS))
    live = (slot[None, :] < counts[:, None]).reshape(rows, 1)
    upstream = jnp.where(live, to_images(cotangent), jnp.zeros((), BF))
    scales = (vectors[0], vectors[5], vectors[6], vectors[10])
    entering, d_small, matrices, d_scores = backward_general(upstream, saved, bias, scales, images)
    d_tokens = to_slots(entering.astype(BF)).astype(F32)
    d_small = all_sum(d_small.reshape(-1, width), (1, 2)).reshape(layers, 16, width)
    d_table = all_sum(fold(core, shapes, d_scores, part).reshape(-1, LANES), (2,)).reshape(-1, 16, LANES)
    other = swap(d_table, "section", 1)
    tables = [
        table_form(t, index, entries)[: layers * own].reshape(layers, own, entries)
        for t in (pick(ci, d_table, other), pick(ci, other, d_table))
    ]
    d_table = jnp.concatenate(tables, axis=1).transpose(0, 2, 1)
    wq, wp, w1, w2 = matrices
    fb = d_small[:, 10 : 10 + ff // width].reshape(layers, ff)
    g1, b1, qb, vb, pb, sa, g2, b2, mb, sm = (d_small[:, at] for at in range(10))
    return (to_slots(hidden), d_tokens, g1, b1, wq, qb, vb, wp, pb, sa, d_table, g2, b2, w1, fb, w2, mb, sm)


def shards(
    tokens,
    cotangent,
    shape_id,
    rel_index,
    norm1_gain,
    norm1_bias,
    qkv_weight,
    q_bias,
    v_bias,
    proj_weight,
    proj_bias,
    attn_scale,
    rel_table,
    norm2_gain,
    norm2_bias,
    fc1_weight,
    fc1_bias,
    fc2_weight,
    fc2_bias,
    mlp_scale,
):
    layers, entries, heads = rel_table.shape
    all_images, part, width = tokens.shape
    images = all_images // 2
    slots = 4 * part
    ff = fc1_weight.shape[2]
    index = jnp.stack(
        [
            jnp.concatenate(
                [rel_index[s, a * slots : (a + 1) * slots] for a in (0, 1, c, 1 + (r - 1) * c, r * c)]
            )
            for s, (r, c) in enumerate(GRIDS)
        ]
    )
    vectors = (
        norm1_gain, norm1_bias, q_bias, v_bias, proj_bias, attn_scale, norm2_gain, norm2_bias, fc1_bias, fc2_bias,
        mlp_scale,
    )
    owns = (qkv_weight, proj_weight, fc1_weight, fc2_weight)
    if layers != 2 or lax.axis_size("wide") != 8 or images * 2 * part > 320:
        return run_general(tokens, cotangent, shape_id, owns, rel_table, index, vectors)
    blocks, upstream, *saved = forward(shape_id, tokens, cotangent, owns, rel_table, index, vectors)
    scales = (norm1_gain, attn_scale, norm2_gain, mlp_scale)
    saved = [upstream, blocks] + saved
    out, d_tokens, d_small, d_matrix, d_table, d_other, unused = backward(shape_id, saved, scales, images)
    core = jnp.reshape(lax.axis_index("section") % 2, (1,)).astype(jnp.int32)
    return (out, d_tokens, *last_form(core, d_small, d_matrix, d_table, d_other, index, entries, heads, ff))


def solution(mesh):
    return jax.shard_map(
        shards,
        mesh=mesh,
        in_specs=(
            P("wide", "section", None),
            P("wide", "section", None),
            P("wide"),
            P(),
            P(),
            P(),
            P(None, "section", None),
            P(),
            P(),
            P(None, "section", None),
            P(),
            P(),
            P(),
            P(),
            P(),
            P(None, "section", None),
            P(),
            P(None, "section", None),
            P(),
            P(),
        ),
        out_specs=(
            P("wide", "section", None),
            P("wide", "section", None),
            P(),
            P(),
            P(None, "wide", "section"),
            P(),
            P(),
            P(None, "wide", "section"),
            P(),
            P(),
            P(),
            P(),
            P(),
            P(None, "wide", "section"),
            P(),
            P(None, "wide", "section"),
            P(),
            P(),
        ),
        check_vma=False,
    )
```
